32 devices in a mesh: groups: 2 (over y), tensor: 4 (over z), dp: 2 (over x), section: 2 (over core).
Axes of the slice: x: 2, y: 2, z: 4, core: 2. Of those that a mesh axis runs over, the one named last changes fastest.
Arguments:
- hidden: bfloat16 [64, 53248], P(('groups', 'dp'), ('tensor', 'section')), parts along dimension 0, may hold values from -6 to 6
- down_matrix: bfloat16 [53248, 8192], P(('tensor', 'section'), 'dp'), may hold values from -0.02734375 to 0.02734375
- residual: bfloat16 [64, 8192], P(('groups', 'tensor', 'section'), 'dp'), parts along dimension 0, may hold values from -6 to 6
- next_norm_scale: bfloat16 [8192], replicated, may hold values from 0.099609375 to 1.8984375
- shrink_matrix: bfloat16 [2, 8192, 64], P('dp'), may hold values from -0.0625 to 0.0625
- adapter_index: int32 [64, 1], P(('groups', 'tensor', 'section')), parts along dimension 0, may hold values from 0 to 1; in each aligned block of 4 rows (0 to 3, 4 to 7, ...) at most 2 rows name the same one
Outputs:
- mixed: bfloat16 [64, 8192], P(('groups', 'tensor', 'section'), 'dp'), parts along dimension 0
- shrunk: float32 [2, 16, 2, 64], P('dp', ('groups', 'tensor', 'section')), parts along dimension 1
The draws below stay inside these ranges and needn't reach their ends.
There are 2 independent parts, one for each index of `groups`. The reference program is written for one: setup_inputs(seed, part) draws one part's arguments, and reference() takes and returns one part's arrays. A program takes and returns all parts, laid end to end along the dimension named above; an argument that names none is the same for every part. Nothing has to cross between parts.
Inputs may be any that keep to these rules, and one draw needn't show every extreme that they name: `adapter_index`: in each aligned block of 4 rows no adapter is named by more than 2 rows, a bound that some block reaches.
All inputs are finite; a program needn't handle non-finite values.
Results may differ from the reference program's by a relative error of at most 0.0051.
Values may be sent and summed in bfloat16 or wider, within the bound.
No kernel may reach another device: no remote copies, remote signals or barrier semaphores. Data moves between devices by JAX's collectives and lax.ppermute only.
A program may use at most 128 MiB of HBM per device.

```python
import math
import jax
import jax.numpy as jnp
import numpy as np
from jax import lax

MODEL_WIDTH = 8192
FF = 53248
ADAPTER_RANK = 64
ROW_DEV = 4
MOST = 2
LOADED_ADAPTERS = 2
ROW_BLOCKS = 8
ROWS = 32


def raised(result, rng, source, target, blocks, factor):
    owner, partner = [(jnp.arange(result.shape[dim]) // (result.shape[dim] // blocks)).reshape([-1 if axis == dim else 1 for axis in range(result.ndim)]) for dim in (source, target)]
    chosen = jax.random.permutation(rng, blocks)[partner]
    strong = (owner == chosen) | (owner == (partner + blocks // 2) % blocks)
    return jnp.where(strong, factor * result, result)


def steps_of(rng, shape, shards, low, top_value):
    level = 1.0
    for dim, parts in shards:
        draws = jax.random.uniform(jax.random.fold_in(jax.random.fold_in(rng, 6), dim), (parts,), jnp.float32, low / len(shards), top_value / len(shards))
        level = level * jnp.repeat(jnp.exp(draws), shape[dim] // parts).reshape((-1,) + (1,) * (len(shape) - 1 - dim))
    return level


def deal_out(rng, own, number, rows, count, top, most, slope):
    sequence = jax.random.permutation(rng, count)
    crowded, common = shares(count, rows * top, most, slope, True), shares(count, rows * top, most, slope, False)
    places = jnp.arange(count)

    def named(sizes, offset_by):
        used = int((sizes > 0).sum())
        fixed = max(1, used // 4)
        shifted = fixed + (places - fixed + offset_by * (used - fixed)) % max(1, count - fixed)
        return jnp.zeros((count,), jnp.int32).at[sequence[jnp.where(places < fixed, places, shifted)]].set(jnp.asarray(sizes, jnp.int32))

    sizes = jnp.where(number % 4 == 0, named(crowded, number // 4), named(common, number - number // 4 - 1))
    mixed = jax.random.permutation(jax.random.fold_in(own, 3), count)
    donor, taker = mixed[0:count // 2 * 2:2], mixed[1:count // 2 * 2:2]
    room = jnp.minimum(sizes[donor] - 1, most - sizes[taker]) // 2
    room = jnp.where((donor == sequence[0]) | (taker == sequence[0]) | (sizes[taker] == 0), 0, jnp.maximum(room, 0))
    shifted = jax.random.randint(jax.random.fold_in(own, 4), (count // 2,), 0, 1 << 20) % (room + 1)
    sizes = sizes.at[donor].add(-shifted).at[taker].add(shifted)
    items = jnp.searchsorted(jnp.cumsum(sizes), jnp.arange(rows * top), side="right").astype(jnp.int32)
    table = items.reshape(top, rows).T
    table = table[jax.random.permutation(jax.random.fold_in(own, 1), rows)]
    offset_by = jax.random.randint(jax.random.fold_in(own, 2), (rows, 1), 0, top)
    return jnp.take_along_axis(table, (jnp.arange(top)[None, :] + offset_by) % top, axis=1)


def shares(count, total, limit, skew, full):
    loads = [(1 << 20) // math.isqrt(rank ** skew) + 1 for rank in range(1, count + 1)]
    largest = limit if full else min(limit, max(-(-total // count), total * loads[0] // sum(loads)))
    least = 1 if total - largest >= count - 1 else 0
    given, spare = [largest] + [least] * (count - 1), total - largest - least * (count - 1)
    while spare > 0:
        movable = [i for i in range(1, count) if given[i] < largest] or [i for i in range(1, count) if given[i] < limit]
        mass, budget = sum([loads[i] for i in movable]), spare
        for i in movable:
            more = min(limit - given[i], max(1, budget * loads[i] // mass), spare)
            given[i] = given[i] + more
            spare = spare - more
    return np.array(given)


def normal_values(stream_key, dims, spread, reach, cuts=(), kind=jnp.bfloat16):
    result = spread * jax.random.normal(stream_key, dims, jnp.float32)
    if cuts:
        result = result * steps_of(stream_key, dims, cuts, -0.22, 0.18)
    return jnp.clip(result, -reach, reach).astype(kind)


def bell_draw_with(own_key, shape, width, reach, pieces, heavy, held_as=jnp.bfloat16):
    drawn = width * jax.random.normal(own_key, shape, jnp.float32)
    if pieces:
        drawn = drawn * steps_of(own_key, shape, pieces, -0.22, 0.18)
    return jnp.clip(raised(drawn, jax.random.fold_in(own_key, 3), *heavy), -reach, reach).astype(held_as)


def setup_inputs(seed: int = 0, part: int = 0) -> dict:
    streams_of = jax.random.split(jax.random.key(seed), 7)
    part_keys = jax.random.split(jax.random.fold_in(streams_of[6], part), 7)
    hidden = bell_draw_with(part_keys[0], (ROWS, FF), 1.0, 6.0, ((0, 2), (1, 8)), (1, 0, 8, 2.0))
    down_matrix = normal_values(streams_of[1], (FF, MODEL_WIDTH), FF ** -0.5, 0.02734375, ((0, 8), (1, 2)))
    residual = normal_values(part_keys[2], (ROWS, MODEL_WIDTH), 1.0, 6.0, ((0, 8), (1, 2)))
    next_norm_scale = jnp.clip(1.0 + 0.18 * jax.random.normal(streams_of[3], (MODEL_WIDTH,), jnp.float32), 0.099609375, 1.8984375).astype(jnp.bfloat16)
    shrink_matrix = normal_values(streams_of[4], (LOADED_ADAPTERS, MODEL_WIDTH, ADAPTER_RANK), MODEL_WIDTH ** -0.5, 0.0625, ((0, 2),))
    adapter_index_keys = jax.random.split(jax.random.fold_in(part_keys[5], 1), ROWS // ROW_DEV)
    adapter_index_turns = jax.random.permutation(jax.random.fold_in(part_keys[5], 3), ROWS // ROW_DEV)
    adapter_index = jax.vmap(lambda own, number: deal_out(jax.random.fold_in(part_keys[5], 2), own, number, ROW_DEV, LOADED_ADAPTERS, 1, MOST, 2))(adapter_index_keys, adapter_index_turns).reshape((ROWS, 1))
    return {"hidden": hidden, "down_matrix": down_matrix, "residual": residual, "next_norm_scale": next_norm_scale, "shrink_matrix": shrink_matrix, "adapter_index": adapter_index}


def reference(hidden, down_matrix, residual, next_norm_scale, shrink_matrix, adapter_index):
    projected = jnp.dot(hidden, down_matrix, preferred_element_type=jnp.float32)
    mixed = (projected + residual.astype(jnp.float32)).astype(jnp.bfloat16)
    widened = mixed.astype(jnp.float32)
    mean_square = lax.optimization_barrier(jnp.mean(widened * widened, axis=1, keepdims=True))
    normalized_rows = (widened * lax.rsqrt(mean_square + 1e-05) * next_norm_scale.astype(jnp.float32)).astype(jnp.bfloat16)
    projected_values = jnp.einsum('yf,xfe->yxe', normalized_rows.astype(jnp.float32), shrink_matrix.astype(jnp.float32)) * 2.0
    row_adapter = adapter_index[:, 0].reshape(ROW_BLOCKS, ROW_DEV)
    onehot = (row_adapter[:, :, None] == jnp.arange(LOADED_ADAPTERS, dtype=jnp.int32)[None, None, :]).astype(jnp.int32)
    slot_rank = jnp.cumsum(onehot, axis=1) - onehot
    placement = onehot[:, :, :, None] * (slot_rank[:, :, :, None] == jnp.arange(MOST, dtype=jnp.int32)[None, None, None, :]).astype(jnp.int32)
    block_values = projected_values.reshape(ROW_BLOCKS, ROW_DEV, LOADED_ADAPTERS, ADAPTER_RANK)
    shrunk = jnp.einsum('bram,brak->abmk', placement.astype(jnp.float32), block_values, precision=lax.Precision.HIGHEST)
    return (mixed, shrunk)
```

```python
import itertools

import jax
import jax.numpy as jnp
from jax import lax
from jax.experimental import pallas as pl
from jax.experimental.pallas import tpu as pltpu
from jax.sharding import PartitionSpec as P

MOST = 2
EPS = 1e-05
REDUCE_AXES = ("tensor", "section")


def project_kernel(place_ref, own_ref, others_ref, weight_ref, out_ref, rows_ref):
    own_rows = own_ref.shape[0]

    @pl.when(pl.program_id(0) == 0)
    def _():
        rows_ref[pl.ds(pl.multiple_of(place_ref[0] * own_rows, own_rows), own_rows), :] = own_ref[...]
        for shift in range(others_ref.shape[0]):
            start = pl.multiple_of(place_ref[shift + 1] * own_rows, own_rows)
            rows_ref[pl.ds(start, own_rows), :] = others_ref[shift]

    out_ref[...] = jnp.dot(
        rows_ref[...], weight_ref[...], preferred_element_type=jnp.float32
    ).astype(out_ref.dtype)


def project(place, own, others, weight, width):
    own_rows, depth = own.shape
    rows = own_rows * (1 + others.shape[0])
    columns = weight.shape[1]
    whole = pl.BlockSpec(memory_space=pltpu.VMEM)
    return pl.pallas_call(
        project_kernel,
        grid=(columns // width,),
        out_shape=jax.ShapeDtypeStruct((rows, columns), jnp.bfloat16),
        in_specs=[
            pl.BlockSpec(memory_space=pltpu.SMEM),
            whole,
            whole,
            pl.BlockSpec((depth, width), lambda n: (0, n)),
        ],
        out_specs=pl.BlockSpec((rows, width), lambda n: (0, n)),
        scratch_shapes=[pltpu.VMEM((rows, depth), jnp.bfloat16)],
        compiler_params=pltpu.CompilerParams(vmem_limit_bytes=32 * 2**20),
        cost_estimate=pl.CostEstimate(
            flops=2 * rows * depth * columns,
            bytes_accessed=depth * columns * 2,
            transcendentals=0,
        ),
        name="project",
    )(place, own, others, weight)


def finish_kernel(
    place_ref, index_ref, parts_ref, residual_ref, gain_ref, shrink_ref, mixed_ref, sent_ref
):
    rows, columns = residual_ref.shape
    owners, local_adapters, _, _ = sent_ref.shape
    rank = shrink_ref.shape[0] // (owners * local_adapters)
    total = residual_ref[...].astype(jnp.float32)
    for source in range(parts_ref.shape[0]):
        total = total + parts_ref[source].astype(jnp.float32)
    mixed = total.astype(jnp.bfloat16)
    mixed_ref[...] = mixed
    widened = mixed.astype(jnp.float32)
    squares = jnp.sum(widened * widened, axis=1, keepdims=True)
    scaled = widened * gain_ref[...].astype(jnp.float32)
    high = scaled.astype(jnp.bfloat16)
    low = (scaled - high.astype(jnp.float32)).astype(jnp.bfloat16)
    against = (((1,), (1,)), ((), ()))
    values = lax.dot_general(
        high, shrink_ref[...], against, preferred_element_type=jnp.float32
    ) + lax.dot_general(low, shrink_ref[...], against, preferred_element_type=jnp.float32)
    named = [index_ref[row, 0] for row in range(rows)]
    for place, local in itertools.product(range(owners), range(local_adapters)):
        adapter = place_ref[place] * local_adapters + local
        first = (place * local_adapters + local) * rank
        own = values[:, first : first + rank]
        filled = jnp.concatenate([own, jnp.broadcast_to(squares, own.shape)], axis=1)
        before = jnp.int32(0)
        slots = [jnp.zeros((1, 2 * rank), jnp.float32) for _ in range(MOST)]
        for row in range(rows):
            hit = named[row] == adapter
            for slot in range(MOST):
                here = jnp.logical_and(hit, before == slot).astype(jnp.float32)
                slots[slot] = slots[slot] + here * filled[row : row + 1, :]
            before = before + hit.astype(jnp.int32)
        for slot in range(MOST):
            sent_ref[place, local, slot : slot + 1, :] = slots[slot]


def finish(place, index, parts, residual, gain, shrink, rank):
    rows, columns = residual.shape
    owners = place.shape[0]
    local_adapters = shrink.shape[0] // (owners * rank)
    whole = pl.BlockSpec(memory_space=pltpu.VMEM)
    return pl.pallas_call(
        finish_kernel,
        out_shape=(
            jax.ShapeDtypeStruct((rows, columns), jnp.bfloat16),
            jax.ShapeDtypeStruct((owners, local_adapters, MOST, 2 * rank), jnp.float32),
        ),
        in_specs=[pl.BlockSpec(memory_space=pltpu.SMEM)] * 2 + [whole] * 4,
        out_specs=(whole, whole),
        compiler_params=pltpu.CompilerParams(vmem_limit_bytes=16 * 2**20),
        name="finish",
    )(place, index, parts, residual, gain, shrink)


def shifted(array, count, shift):
    if shift == 0:
        return array
    return lax.ppermute(array, "dp", [(i, (i + shift) % count) for i in range(count)])


def body(hidden, down_matrix, residual, next_norm_scale, shrink_matrix, adapter_index):
    dp = lax.axis_size("dp")
    me = lax.axis_index("dp")
    blocks = lax.axis_size(REDUCE_AXES)
    columns = down_matrix.shape[1]
    local_adapters, _, rank = shrink_matrix.shape

    others = jnp.stack([shifted(hidden, dp, shift) for shift in range(1, dp)])
    place = jnp.stack([(me - shift) % dp for shift in range(dp)]).astype(jnp.int32)

    by_feature = jnp.swapaxes(shrink_matrix, 1, 2).reshape(local_adapters * rank, dp * columns)
    by_feature, others = lax.optimization_barrier((by_feature, others))
    shrink = jnp.concatenate(
        [
            shifted(
                lax.dynamic_slice_in_dim(by_feature, (me + shift) % dp * columns, columns, 1),
                dp,
                shift,
            )
            for shift in range(dp)
        ]
    )
    gain = lax.dynamic_slice_in_dim(next_norm_scale, me * columns, columns)[None, :]

    partial = project(place, hidden, others, down_matrix, 512)
    rows = partial.shape[0] // blocks
    parts = lax.all_to_all(
        partial.reshape(blocks, rows, columns),
        REDUCE_AXES,
        split_axis=0,
        concat_axis=0,
        tiled=True,
    )
    mixed, sent = finish(place, adapter_index, parts, residual, gain, shrink, rank)

    total = sent[0]
    for back in range(1, dp):
        total = total + shifted(sent[back], dp, dp - back)
    mean_square = total[..., rank:] / (columns * dp)
    shrunk = 2.0 * total[..., :rank] * lax.rsqrt(mean_square + EPS)
    return (mixed, shrunk[:, None])


def solution(mesh):
    placed = (
        P(("groups", "dp"), ("tensor", "section")),
        P(("tensor", "section"), "dp"),
        P(("groups", "tensor", "section"), "dp"),
        P(),
        P("dp", None, None),
        P(("groups", "tensor", "section"), None),
    )
    return jax.shard_map(
        body,
        mesh=mesh,
        in_specs=placed,
        out_specs=(
            P(("groups", "tensor", "section"), "dp"),
            P("dp", ("groups", "tensor", "section"), None, None),
        ),
        check_vma=False,
    )
```

```python
import jax
import jax.numpy as jnp
from jax import lax
from jax.experimental import pallas as pl
from jax.experimental.pallas import tpu as pltpu
from jax.sharding import PartitionSpec as P

MOST = 2
EPS = 1e-05
DEPTH_STEP = 512
HELD_BYTES = 26 * 2**20
MIB = 2**20
F32 = jnp.float32
BF16 = jnp.bfloat16


def whole():
    return pl.BlockSpec(memory_space=pltpu.VMEM)


def step_of(depth):
    return max(s for s in range(16, DEPTH_STEP + 1, 16) if depth % s == 0)


def fetch_kernel(weight_ref, held_ref, sems):
    count, step, _ = held_ref.shape
    copies = [
        pltpu.make_async_copy(
            weight_ref.at[pl.ds(i * step, step), :], held_ref.at[i], sems.at[i]
        )
        for i in range(count)
    ]
    for copy in copies:
        copy.start()
    for copy in copies:
        copy.wait()


def fetch(weight, count, step):
    columns = weight.shape[1]
    return pl.pallas_call(
        fetch_kernel,
        out_shape=pltpu.VMEM((count, step, columns), weight.dtype),
        in_specs=[pl.BlockSpec(memory_space=pl.ANY)],
        out_specs=whole(),
        scratch_shapes=[pltpu.SemaphoreType.DMA((count,))],
        compiler_params=pltpu.CompilerParams(vmem_limit_bytes=1 * MIB),
        cost_estimate=pl.CostEstimate(
            flops=0, bytes_accessed=2 * count * step * columns, transcendentals=0
        ),
        name="fetch",
    )(weight)


def project_kernel(
    own_ref, others_ref, held_ref, weight_ref, kept_ref, sent_ref, rows_ref, total_ref, rest_ref, sems
):
    held, step, columns = held_ref.shape
    rest = rest_ref.shape[0]
    own_rows = own_ref.shape[0]
    dp = 1 + others_ref.shape[0]
    me = lax.axis_index("dp")
    section = lax.axis_index("section")
    width = min(columns, 1024)

    def copy_of(i):
        return pltpu.make_async_copy(
            weight_ref.at[pl.ds((held + i) * step, step), :], rest_ref.at[i], sems.at[i]
        )

    for i in range(rest):
        copy_of(i).start()

    for i in range(held + rest):
        block = slice(i * step, (i + 1) * step)
        own_first = pl.multiple_of(me * own_rows, own_rows)
        rows_ref[i, pl.ds(own_first, own_rows), :] = own_ref[:, block]
        for shift in range(1, dp):
            first = pl.multiple_of(lax.rem(me + dp - shift, dp) * own_rows, own_rows)
            rows_ref[i, pl.ds(first, own_rows), :] = others_ref[shift - 1, :, block]
    total_ref[...] = jnp.zeros_like(total_ref)

    def add(block_ref, i):
        for n in range(0, columns, width):
            total_ref[:, n : n + width] += jnp.dot(
                rows_ref[i], block_ref[:, n : n + width], preferred_element_type=F32
            )

    def held_step(i, _):
        add(held_ref.at[i], i)
        return 0

    def rest_step(i, _):
        copy_of(i).wait()
        add(rest_ref.at[i], held + i)
        return 0

    lax.fori_loop(0, held, held_step, 0)
    lax.fori_loop(0, rest, rest_step, 0)

    _, tensors, block_rows, _ = kept_ref.shape
    sections = sent_ref.shape[0] + 1
    for s in range(sections):
        for t in range(tensors):
            first = (t * sections + s) * block_rows
            block = total_ref[first : first + block_rows, :]

            @pl.when(section == s)
            def _():
                kept_ref[0, t] = block

            @pl.when(section != s)
            def _():
                sent_ref[lax.rem(s + sections - section, sections) - 1, t] = block.astype(BF16)


def project(own, others, held, weight, tensors, sections):
    own_rows, depth = own.shape
    rows = own_rows * (1 + others.shape[0])
    columns = weight.shape[1]
    count, step, _ = held.shape
    rest = depth // step - count
    block_rows = rows // (tensors * sections)
    return pl.pallas_call(
        project_kernel,
        out_shape=(
            pltpu.VMEM((1, tensors, block_rows, columns), F32),
            pltpu.VMEM((sections - 1, tensors, block_rows, columns), BF16),
        ),
        in_specs=[whole(), whole(), whole(), pl.BlockSpec(memory_space=pl.ANY)],
        out_specs=(whole(), whole()),
        scratch_shapes=[
            pltpu.VMEM((depth // step, rows, step), BF16),
            pltpu.VMEM((rows, columns), F32),
            pltpu.VMEM((rest, step, columns), BF16),
            pltpu.SemaphoreType.DMA((rest,)),
        ],
        compiler_params=pltpu.CompilerParams(vmem_limit_bytes=31 * MIB),
        cost_estimate=pl.CostEstimate(
            flops=2 * rows * depth * columns,
            bytes_accessed=2 * rest * step * columns,
            transcendentals=0,
        ),
        name="project",
    )(own, others, held, weight)


def pair_kernel(kept_ref, *refs):
    tensors = kept_ref.shape[1]
    arrived, outs = refs[:-tensors], refs[-tensors:]
    me = lax.axis_index("tensor")
    for shift, out_ref in enumerate(outs):
        place = lax.rem(me + shift, tensors)
        block = kept_ref[0, place]
        for piece in arrived:
            block = block + piece[place].astype(F32)
        out_ref[...] = block.astype(out_ref.dtype)


def pair(kept, arrived):
    _, tensors, block_rows, columns = kept.shape
    return pl.pallas_call(
        pair_kernel,
        out_shape=[
            jax.ShapeDtypeStruct((block_rows, columns), F32 if shift == 0 else BF16)
            for shift in range(tensors)
        ],
        in_specs=[whole()] * (1 + len(arrived)),
        out_specs=[whole()] * tensors,
        compiler_params=pltpu.CompilerParams(vmem_limit_bytes=8 * MIB),
        name="pair",
    )(kept, *arrived)


def mix_kernel(residual_ref, places_ref, own_ref, *refs):
    arrived, (mixed_ref, kept_ref, sent_ref) = refs[:-3], refs[-3:]
    total = own_ref[...] + residual_ref[...].astype(F32)
    for piece in arrived:
        total = total + piece[...].astype(F32)
    mixed = total.astype(BF16)
    mixed_ref[...] = mixed
    widened = mixed.astype(F32)
    places = places_ref[...]
    slots = kept_ref.shape[0]
    routed = sum(
        places[:, row : row + 1] * widened[row : row + 1, :] for row in range(widened.shape[0])
    )
    kept_ref[...] = routed[:slots]
    for shift in range(sent_ref.shape[0]):
        sent_ref[shift] = routed[(shift + 1) * slots : (shift + 2) * slots].astype(BF16)


def mix(residual, places, own, arrived, slots):
    rows, columns = residual.shape
    owners = places.shape[0] // slots
    return pl.pallas_call(
        mix_kernel,
        out_shape=(
            jax.ShapeDtypeStruct((rows, columns), BF16),
            jax.ShapeDtypeStruct((slots, columns), F32),
            jax.ShapeDtypeStruct((owners - 1, slots, columns), BF16),
        ),
        in_specs=[whole()] * (3 + len(arrived)),
        out_specs=(whole(),) * 3,
        compiler_params=pltpu.CompilerParams(vmem_limit_bytes=8 * MIB),
        name="mix",
    )(residual, places, own, *arrived)


def partial_values(rows, gain_ref, shrink_ref, place, columns, local):
    first = pl.multiple_of(place * columns, columns)
    squares = jnp.sum(rows * rows, axis=1, keepdims=True)
    scaled = rows * gain_ref[:, pl.ds(first, columns)].astype(F32)
    high = scaled.astype(BF16)
    low = (scaled - high.astype(F32)).astype(BF16)
    values = []
    for adapter in range(local):
        mine = slice(adapter * MOST, (adapter + 1) * MOST)
        both = jnp.concatenate([high[mine], low[mine]], axis=0)
        product = lax.dot_general(
            both,
            shrink_ref[adapter, :, pl.ds(first, columns)],
            (((1,), (1,)), ((), ())),
            preferred_element_type=F32,
        )
        values.append(product[:MOST] + product[MOST:])
    return jnp.concatenate(values, axis=0), squares


def own_half_kernel(rows_ref, gain_ref, shrink_ref, values_ref, squares_ref):
    columns = rows_ref.shape[1]
    values, squares = partial_values(
        rows_ref[...], gain_ref, shrink_ref, lax.axis_index("dp"), columns, shrink_ref.shape[0]
    )
    values_ref[...] = values
    squares_ref[...] = jnp.broadcast_to(squares, squares_ref.shape)


def own_half(rows, gain, shrink):
    slots = rows.shape[0]
    rank = shrink.shape[1]
    return pl.pallas_call(
        own_half_kernel,
        out_shape=(
            jax.ShapeDtypeStruct((slots, rank), F32),
            jax.ShapeDtypeStruct((slots, rank), F32),
        ),
        in_specs=[whole()] * 3,
        out_specs=(whole(),) * 2,
        compiler_params=pltpu.CompilerParams(vmem_limit_bytes=8 * MIB),
        cost_estimate=pl.CostEstimate(
            flops=2 * slots * rows.shape[1] * rank, bytes_accessed=2 * MIB, transcendentals=0
        ),
        name="own_half",
    )(rows, gain, shrink)


def finish_kernel(values_ref, squares_ref, gain_ref, shrink_ref, *refs):
    arrived, out_ref = refs[:-1], refs[-1]
    dp = 1 + len(arrived)
    me = lax.axis_index("dp")
    local = shrink_ref.shape[0]
    columns = arrived[0].shape[1]
    values, squares = values_ref[...], squares_ref[:, :1]
    for shift, piece in enumerate(arrived, start=1):
        more, more_squares = partial_values(
            piece[...].astype(F32),
            gain_ref,
            shrink_ref,
            lax.rem(me + dp - shift, dp),
            columns,
            local,
        )
        values, squares = values + more, squares + more_squares
    result = 2.0 * values * lax.rsqrt(squares / (columns * dp) + EPS)
    for adapter in range(local):
        out_ref[adapter, 0] = result[adapter * MOST : (adapter + 1) * MOST]


def finish(values, squares, gain, shrink, arrived):
    local, rank, _ = shrink.shape
    return pl.pallas_call(
        finish_kernel,
        out_shape=jax.ShapeDtypeStruct((local, 1, MOST, rank), F32),
        in_specs=[whole()] * (4 + len(arrived)),
        out_specs=whole(),
        compiler_params=pltpu.CompilerParams(vmem_limit_bytes=8 * MIB),
        name="finish",
    )(values, squares, gain, shrink, *arrived)


def shifted(array, axis, shift):
    count = lax.axis_size(axis)
    return lax.ppermute(array, axis, [(i, (i + shift) % count) for i in range(count)])


def body(hidden, down_matrix, residual, next_norm_scale, shrink_matrix, adapter_index):
    dp, tensors, sections = (lax.axis_size(axis) for axis in ("dp", "tensor", "section"))
    me = lax.axis_index("dp")
    depth, _ = down_matrix.shape
    local = shrink_matrix.shape[0]

    others = jnp.stack([shifted(hidden, "dp", shift) for shift in range(1, dp)])

    step = step_of(depth)
    blocks = depth // step
    held_count = max(1, min(blocks // 2, HELD_BYTES // (2 * step * down_matrix.shape[1])))
    held = fetch(down_matrix, held_count, step)

    row_adapter = adapter_index[:, 0]
    same = row_adapter[:, None] == row_adapter[None, :]
    rows = row_adapter.shape[0]
    earlier = jnp.arange(rows)[:, None] < jnp.arange(rows)[None, :]
    rank_of = jnp.sum(jnp.logical_and(same, earlier), axis=0)
    owners = (me + jnp.arange(dp)) % dp
    adapters = owners[:, None] * local + jnp.arange(local)[None, :]
    places = jnp.logical_and(
        adapters[:, :, None, None] == row_adapter,
        jnp.arange(MOST)[None, None, :, None] == rank_of,
    )
    places = places.astype(F32).reshape(dp * local * MOST, rows)
    shrink = jnp.swapaxes(shrink_matrix, 1, 2)
    gain = next_norm_scale[None, :]

    in_vmem = [pltpu.with_memory_space_constraint(x, pltpu.VMEM) for x in (hidden, others, held)]
    kept, sent = project(*in_vmem, down_matrix, tensors, sections)
    arrived = [shifted(sent[s - 1], "section", s) for s in range(1, sections)]
    own, *sums = pair(kept, arrived)
    arrived = [shifted(piece, "tensor", s) for s, piece in enumerate(sums, start=1)]
    mixed, routed, leaving = mix(residual, places, own, arrived, local * MOST)
    arrived = [shifted(leaving[s - 1], "dp", s) for s in range(1, dp)]
    values, squares = own_half(routed, gain, shrink)
    shrunk = finish(values, squares, gain, shrink, arrived)
    return (mixed, shrunk)


def solution(mesh):
    placed = (
        P(("groups", "dp"), ("tensor", "section")),
        P(("tensor", "section"), "dp"),
        P(("groups", "tensor", "section"), "dp"),
        P(),
        P("dp", None, None),
        P(("groups", "tensor", "section"), None),
    )
    return jax.shard_map(
        body,
        mesh=mesh,
        in_specs=placed,
        out_specs=(
            P(("groups", "tensor", "section"), "dp"),
            P("dp", ("groups", "tensor", "section"), None, None),
        ),
        check_vma=False,
    )
```

```python
import jax
import jax.numpy as jnp
from jax import lax
from jax.experimental import pallas as pl
from jax.experimental.pallas import tpu as pltpu
from jax.sharding import PartitionSpec as P

MOST = 2
EPS = 1e-05
DEPTH_STEP = 512
HELD_BYTES = 21 * 2**20
IN_FLIGHT = 4
HALVES = 2
MIB = 2**20
F32 = jnp.float32
BF16 = jnp.bfloat16


def whole():
    return pl.BlockSpec(memory_space=pltpu.VMEM)


def step_of(depth):
    return max(s for s in range(16, DEPTH_STEP + 1, 16) if depth % s == 0)


def fetch_kernel(weight_ref, held_ref, sems):
    count, step, _ = held_ref.shape
    copies = [
        pltpu.make_async_copy(
            weight_ref.at[pl.ds(i * step, step), :], held_ref.at[i], sems.at[i]
        )
        for i in range(count)
    ]
    for copy in copies:
        copy.start()
    for copy in copies:
        copy.wait()


def fetch(weight, count, step):
    columns = weight.shape[1]
    return pl.pallas_call(
        fetch_kernel,
        out_shape=pltpu.VMEM((count, step, columns), weight.dtype),
        in_specs=[pl.BlockSpec(memory_space=pl.ANY)],
        out_specs=whole(),
        scratch_shapes=[pltpu.SemaphoreType.DMA((count,))],
        compiler_params=pltpu.CompilerParams(vmem_limit_bytes=1 * MIB),
        cost_estimate=pl.CostEstimate(
            flops=0, bytes_accessed=2 * count * step * columns, transcendentals=0
        ),
        name="fetch",
    )(weight)


def project_kernel(
    own_ref, others_ref, held_ref, weight_ref, kept_ref, sent_ref, rows_ref, total_ref, rest_ref, sems
):
    held, step, columns = held_ref.shape
    rest = rest_ref.shape[0]
    own_rows = own_ref.shape[0]
    dp = 1 + others_ref.shape[0]
    me = lax.axis_index("dp")
    section = lax.axis_index("section")
    half = columns // HALVES
    width = min(half, 1024)

    def copy_of(i, part):
        lanes = pl.ds(part * half, half)
        return pltpu.make_async_copy(
            weight_ref.at[pl.ds((held + i) * step, step), lanes],
            rest_ref.at[i, :, lanes],
            sems.at[i, part],
        )

    for i in range(min(rest, IN_FLIGHT)):
        for part in range(HALVES):
            copy_of(i, part).start()

    for i in range(held + rest):
        block = slice(i * step, (i + 1) * step)
        own_first = pl.multiple_of(me * own_rows, own_rows)
        rows_ref[i, pl.ds(own_first, own_rows), :] = own_ref[:, block]
        for shift in range(1, dp):
            first = pl.multiple_of(lax.rem(me + dp - shift, dp) * own_rows, own_rows)
            rows_ref[i, pl.ds(first, own_rows), :] = others_ref[shift - 1, :, block]
    total_ref[...] = jnp.zeros_like(total_ref)

    def add(block_ref, i, part):
        for n in range(part * half, (part + 1) * half, width):
            total_ref[:, n : n + width] += jnp.dot(
                rows_ref[i], block_ref[:, n : n + width], preferred_element_type=F32
            )

    def held_step(i, _):
        for part in range(HALVES):
            add(held_ref.at[i], i, part)
        return 0

    def rest_step(i, _):
        for part in range(HALVES):
            copy_of(i, part).wait()

            @pl.when(i + IN_FLIGHT < rest)
            def _():
                copy_of(i + IN_FLIGHT, part).start()

            add(rest_ref.at[i], held + i, part)
        return 0

    lax.fori_loop(0, held, held_step, 0)
    lax.fori_loop(0, rest, rest_step, 0)

    _, tensors, block_rows, _ = kept_ref.shape
    sections = sent_ref.shape[0] + 1
    for s in range(sections):
        for t in range(tensors):
            first = (t * sections + s) * block_rows
            block = total_ref[first : first + block_rows, :]

            @pl.when(section == s)
            def _():
                kept_ref[0, t] = block

            @pl.when(section != s)
            def _():
                sent_ref[lax.rem(s + sections - section, sections) - 1, t] = block.astype(BF16)


def project(own, others, held, weight, tensors, sections):
    own_rows, depth = own.shape
    rows = own_rows * (1 + others.shape[0])
    columns = weight.shape[1]
    count, step, _ = held.shape
    rest = depth // step - count
    block_rows = rows // (tensors * sections)
    return pl.pallas_call(
        project_kernel,
        out_shape=(
            pltpu.VMEM((1, tensors, block_rows, columns), F32),
            pltpu.VMEM((sections - 1, tensors, block_rows, columns), BF16),
        ),
        in_specs=[whole(), whole(), whole(), pl.BlockSpec(memory_space=pl.ANY)],
        out_specs=(whole(), whole()),
        scratch_shapes=[
            pltpu.VMEM((depth // step, rows, step), BF16),
            pltpu.VMEM((rows, columns), F32),
            pltpu.VMEM((rest, step, columns), BF16),
            pltpu.SemaphoreType.DMA((rest, HALVES)),
        ],
        compiler_params=pltpu.CompilerParams(vmem_limit_bytes=35 * MIB),
        cost_estimate=pl.CostEstimate(
            flops=2 * rows * depth * columns,
            bytes_accessed=2 * rest * step * columns,
            transcendentals=0,
        ),
        name="project",
    )(own, others, held, weight)


def partner_of(me, turn, count):
    if count & (count - 1) == 0:
        return me ^ turn
    return (me + turn) % count


def pair_kernel(kept_ref, *refs):
    tensors = kept_ref.shape[1]
    arrived, outs = refs[:-tensors], refs[-tensors:]
    me = lax.axis_index("tensor")
    for shift, out_ref in enumerate(outs):
        place = partner_of(me, shift, tensors)
        block = kept_ref[0, place]
        for piece in arrived:
            block = block + piece[place].astype(F32)
        out_ref[...] = block.astype(out_ref.dtype)


def pair(kept, arrived):
    _, tensors, block_rows, columns = kept.shape
    return pl.pallas_call(
        pair_kernel,
        out_shape=[
            jax.ShapeDtypeStruct((block_rows, columns), F32 if shift == 0 else BF16)
            for shift in range(tensors)
        ],
        in_specs=[whole()] * (1 + len(arrived)),
        out_specs=[whole()] * tensors,
        compiler_params=pltpu.CompilerParams(vmem_limit_bytes=8 * MIB),
        name="pair",
    )(kept, *arrived)


def mix_kernel(residual_ref, places_ref, own_ref, *refs):
    arrived, (mixed_ref, kept_ref, sent_ref) = refs[:-3], refs[-3:]
    total = own_ref[...] + residual_ref[...].astype(F32)
    for piece in arrived:
        total = total + piece[...].astype(F32)
    mixed = total.astype(BF16)
    mixed_ref[...] = mixed
    widened = mixed.astype(F32)
    places = places_ref[...]
    slots = kept_ref.shape[0]
    routed = sum(
        places[:, row : row + 1] * widened[row : row + 1, :] for row in range(widened.shape[0])
    )
    kept_ref[...] = routed[:slots]
    for shift in range(sent_ref.shape[0]):
        sent_ref[shift] = routed[(shift + 1) * slots : (shift + 2) * slots].astype(BF16)


def mix(residual, places, own, arrived, slots):
    rows, columns = residual.shape
    owners = places.shape[0] // slots
    return pl.pallas_call(
        mix_kernel,
        out_shape=(
            pltpu.VMEM((rows, columns), BF16),
            jax.ShapeDtypeStruct((slots, columns), F32),
            jax.ShapeDtypeStruct((owners - 1, slots, columns), BF16),
        ),
        in_specs=[whole()] * (3 + len(arrived)),
        out_specs=(whole(),) * 3,
        compiler_params=pltpu.CompilerParams(vmem_limit_bytes=8 * MIB),
        name="mix",
    )(residual, places, own, *arrived)


def partial_values(rows, gain_ref, shrink_ref, place, columns, local):
    first = pl.multiple_of(place * columns, columns)
    squares = jnp.sum(rows * rows, axis=1, keepdims=True)
    scaled = rows * gain_ref[:, pl.ds(first, columns)].astype(F32)
    high = scaled.astype(BF16)
    low = (scaled - high.astype(F32)).astype(BF16)
    values = []
    for adapter in range(local):
        mine = slice(adapter * MOST, (adapter + 1) * MOST)
        both = jnp.concatenate([high[mine], low[mine]], axis=0)
        product = lax.dot_general(
            both,
            shrink_ref[adapter, :, pl.ds(first, columns)],
            (((1,), (1,)), ((), ())),
            preferred_element_type=F32,
        )
        values.append(product[:MOST] + product[MOST:])
    return jnp.concatenate(values, axis=0), squares


def own_half_kernel(rows_ref, gain_ref, shrink_ref, values_ref, squares_ref):
    columns = rows_ref.shape[1]
    values, squares = partial_values(
        rows_ref[...], gain_ref, shrink_ref, lax.axis_index("dp"), columns, shrink_ref.shape[0]
    )
    values_ref[...] = values
    squares_ref[...] = jnp.broadcast_to(squares, squares_ref.shape)


def own_half(rows, gain, shrink):
    slots = rows.shape[0]
    rank = shrink.shape[1]
    return pl.pallas_call(
        own_half_kernel,
        out_shape=(
            jax.ShapeDtypeStruct((slots, rank), F32),
            jax.ShapeDtypeStruct((slots, rank), F32),
        ),
        in_specs=[whole()] * 3,
        out_specs=(whole(),) * 2,
        compiler_params=pltpu.CompilerParams(vmem_limit_bytes=8 * MIB),
        cost_estimate=pl.CostEstimate(
            flops=2 * slots * rows.shape[1] * rank, bytes_accessed=2 * MIB, transcendentals=0
        ),
        name="own_half",
    )(rows, gain, shrink)


def finish_kernel(values_ref, squares_ref, gain_ref, shrink_ref, *refs):
    arrived, out_ref = refs[:-1], refs[-1]
    dp = 1 + len(arrived)
    me = lax.axis_index("dp")
    local = shrink_ref.shape[0]
    columns = arrived[0].shape[1]
    values, squares = values_ref[...], squares_ref[:, :1]
    for shift, piece in enumerate(arrived, start=1):
        more, more_squares = partial_values(
            piece[...].astype(F32),
            gain_ref,
            shrink_ref,
            lax.rem(me + dp - shift, dp),
            columns,
            local,
        )
        values, squares = values + more, squares + more_squares
    result = 2.0 * values * lax.rsqrt(squares / (columns * dp) + EPS)
    for adapter in range(local):
        out_ref[adapter, 0] = result[adapter * MOST : (adapter + 1) * MOST]


def finish(values, squares, gain, shrink, arrived):
    local, rank, _ = shrink.shape
    return pl.pallas_call(
        finish_kernel,
        out_shape=jax.ShapeDtypeStruct((local, 1, MOST, rank), F32),
        in_specs=[whole()] * (4 + len(arrived)),
        out_specs=whole(),
        compiler_params=pltpu.CompilerParams(vmem_limit_bytes=8 * MIB),
        name="finish",
    )(values, squares, gain, shrink, *arrived)


def shifted(array, axis, shift):
    count = lax.axis_size(axis)
    return lax.ppermute(array, axis, [(i, (i + shift) % count) for i in range(count)])


def to_partner(array, axis, turn):
    count = lax.axis_size(axis)
    return lax.ppermute(array, axis, [(i, partner_of(i, turn, count)) for i in range(count)])


def body(hidden, down_matrix, residual, next_norm_scale, shrink_matrix, adapter_index):
    dp, tensors, sections = (lax.axis_size(axis) for axis in ("dp", "tensor", "section"))
    me = lax.axis_index("dp")
    depth, _ = down_matrix.shape
    local = shrink_matrix.shape[0]

    others = jnp.stack([shifted(hidden, "dp", shift) for shift in range(1, dp)])

    step = step_of(depth)
    blocks = depth // step
    held_count = max(1, min(blocks // 2, HELD_BYTES // (2 * step * down_matrix.shape[1])))
    held = fetch(down_matrix, held_count, step)

    row_adapter = adapter_index[:, 0]
    same = row_adapter[:, None] == row_adapter[None, :]
    rows = row_adapter.shape[0]
    earlier = jnp.arange(rows)[:, None] < jnp.arange(rows)[None, :]
    rank_of = jnp.sum(jnp.logical_and(same, earlier), axis=0)
    owners = (me + jnp.arange(dp)) % dp
    adapters = owners[:, None] * local + jnp.arange(local)[None, :]
    places = jnp.logical_and(
        adapters[:, :, None, None] == row_adapter,
        jnp.arange(MOST)[None, None, :, None] == rank_of,
    )
    places = places.astype(F32).reshape(dp * local * MOST, rows)
    shrink = jnp.swapaxes(shrink_matrix, 1, 2)
    gain = next_norm_scale[None, :]

    in_vmem = [pltpu.with_memory_space_constraint(x, pltpu.VMEM) for x in (hidden, others, held)]
    kept, sent = project(*in_vmem, down_matrix, tensors, sections)
    arrived = [shifted(sent[s - 1], "section", s) for s in range(1, sections)]
    own, *sums = pair(kept, arrived)
    arrived = [to_partner(sums[s - 1], "tensor", s) for s in range(tensors - 1, 0, -1)]
    mixed, routed, leaving = mix(residual, places, own, arrived, local * MOST)
    arrived = [shifted(leaving[s - 1], "dp", s) for s in range(1, dp)]
    values, squares = own_half(routed, gain, shrink)
    shrunk = finish(values, squares, gain, shrink, arrived)
    return (mixed, shrunk)


def solution(mesh):
    placed = (
        P(("groups", "dp"), ("tensor", "section")),
        P(("tensor", "section"), "dp"),
        P(("groups", "tensor", "section"), "dp"),
        P(),
        P("dp", None, None),
        P(("groups", "tensor", "section"), None),
    )
    return jax.shard_map(
        body,
        mesh=mesh,
        in_specs=placed,
        out_specs=(
            P(("groups", "tensor", "section"), "dp"),
            P("dp", ("groups", "tensor", "section"), None, None),
        ),
        check_vma=False,
    )
```

```python
import jax
import jax.numpy as jnp
from jax import lax
from jax.experimental import pallas as pl
from jax.experimental.pallas import tpu as pltpu
from jax.sharding import PartitionSpec as P

MOST = 2
EPS = 1e-05
DEPTH_STEP = 512
HELD_BYTES = 21 * 2**20
IN_FLIGHT = 4
HALVES = 2
MIB = 2**20
F32 = jnp.float32
BF16 = jnp.bfloat16


def whole():
    return pl.BlockSpec(memory_space=pltpu.VMEM)


def step_of(depth):
    return max(s for s in range(16, DEPTH_STEP + 1, 16) if depth % s == 0)


def project_kernel(
    own_ref, others_ref, held_ref, weight_ref, kept_ref, sent_ref, rows_ref, total_ref, rest_ref, sems
):
    held, step, columns = held_ref.shape
    rest = rest_ref.shape[0]
    own_rows = own_ref.shape[0]
    dp = 1 + others_ref.shape[0]
    me = lax.axis_index("dp")
    section = lax.axis_index("section")
    half = columns // HALVES
    width = min(half, 1024)

    def copy_of(i, part):
        lanes = pl.ds(part * half, half)
        return pltpu.make_async_copy(
            weight_ref.at[pl.ds((held + i) * step, step), lanes],
            rest_ref.at[i, :, lanes],
            sems.at[i, part],
        )

    for i in range(min(rest, IN_FLIGHT)):
        for part in range(HALVES):
            copy_of(i, part).start()

    for i in range(held + rest):
        block = slice(i * step, (i + 1) * step)
        own_first = pl.multiple_of(me * own_rows, own_rows)
        rows_ref[i, pl.ds(own_first, own_rows), :] = own_ref[:, block]
        for shift in range(1, dp):
            first = pl.multiple_of(lax.rem(me + dp - shift, dp) * own_rows, own_rows)
            rows_ref[i, pl.ds(first, own_rows), :] = others_ref[shift - 1, :, block]
    total_ref[...] = jnp.zeros_like(total_ref)

    def add(block_ref, i, part):
        for n in range(part * half, (part + 1) * half, width):
            total_ref[:, n : n + width] += jnp.dot(
                rows_ref[i], block_ref[:, n : n + width], preferred_element_type=F32
            )

    def held_step(i, _):
        for part in range(HALVES):
            add(held_ref.at[i], i, part)
        return 0

    def rest_step(i, _):
        for part in range(HALVES):
            copy_of(i, part).wait()

            @pl.when(i + IN_FLIGHT < rest)
            def _():
                copy_of(i + IN_FLIGHT, part).start()

            add(rest_ref.at[i], held + i, part)
        return 0

    lax.fori_loop(0, held, held_step, 0)
    lax.fori_loop(0, rest, rest_step, 0)

    _, tensors, block_rows, _ = kept_ref.shape
    sections = sent_ref.shape[0] + 1
    for s in range(sections):
        for t in range(tensors):
            first = (t * sections + s) * block_rows
            block = total_ref[first : first + block_rows, :]

            @pl.when(section == s)
            def _():
                kept_ref[0, t] = block

            @pl.when(section != s)
            def _():
                sent_ref[lax.rem(s + sections - section, sections) - 1, t] = block.astype(BF16)


def project(own, others, held, weight, tensors, sections):
    own_rows, depth = own.shape
    rows = own_rows * (1 + others.shape[0])
    columns = weight.shape[1]
    count, step, _ = held.shape
    rest = depth // step - count
    block_rows = rows // (tensors * sections)
    return pl.pallas_call(
        project_kernel,
        out_shape=(
            pltpu.VMEM((1, tensors, block_rows, columns), F32),
            pltpu.VMEM((sections - 1, tensors, block_rows, columns), BF16),
        ),
        in_specs=[whole(), whole(), whole(), pl.BlockSpec(memory_space=pl.ANY)],
        out_specs=(whole(), whole()),
        scratch_shapes=[
            pltpu.VMEM((depth // step, rows, step), BF16),
            pltpu.VMEM((rows, columns), F32),
            pltpu.VMEM((rest, step, columns), BF16),
            pltpu.SemaphoreType.DMA((rest, HALVES)),
        ],
        compiler_params=pltpu.CompilerParams(vmem_limit_bytes=35 * MIB),
        cost_estimate=pl.CostEstimate(
            flops=2 * rows * depth * columns,
            bytes_accessed=2 * rest * step * columns,
            transcendentals=0,
        ),
        name="project",
    )(own, others, held, weight)


def partner_of(me, turn, count):
    if count & (count - 1) == 0:
        return me ^ turn
    return (me + turn) % count


def pair_kernel(kept_ref, *refs):
    tensors = kept_ref.shape[1]
    arrived, outs = refs[:-tensors], refs[-tensors:]
    me = lax.axis_index("tensor")
    for shift, out_ref in enumerate(outs):
        place = partner_of(me, shift, tensors)
        block = kept_ref[0, place]
        for piece in arrived:
            block = block + piece[place].astype(F32)
        out_ref[...] = block.astype(out_ref.dtype)


def pair(kept, arrived):
    _, tensors, block_rows, columns = kept.shape
    return pl.pallas_call(
        pair_kernel,
        out_shape=[
            jax.ShapeDtypeStruct((block_rows, columns), F32 if shift == 0 else BF16)
            for shift in range(tensors)
        ],
        in_specs=[whole()] * (1 + len(arrived)),
        out_specs=[whole()] * tensors,
        compiler_params=pltpu.CompilerParams(vmem_limit_bytes=8 * MIB),
        name="pair",
    )(kept, *arrived)


def mix_kernel(residual_ref, places_ref, own_ref, *refs):
    arrived, (mixed_ref, kept_ref, sent_ref) = refs[:-3], refs[-3:]
    total = own_ref[...] + residual_ref[...].astype(F32)
    for piece in arrived:
        total = total + piece[...].astype(F32)
    mixed = total.astype(BF16)
    mixed_ref[...] = mixed
    widened = mixed.astype(F32)
    places = places_ref[...]
    slots = kept_ref.shape[0]
    routed = sum(
        places[:, row : row + 1] * widened[row : row + 1, :] for row in range(widened.shape[0])
    )
    kept_ref[...] = routed[:slots]
    for shift in range(sent_ref.shape[0]):
        sent_ref[shift] = routed[(shift + 1) * slots : (shift + 2) * slots].astype(BF16)


def mix(residual, places, own, arrived, slots):
    rows, columns = residual.shape
    owners = places.shape[0] // slots
    return pl.pallas_call(
        mix_kernel,
        out_shape=(
            pltpu.VMEM((rows, columns), BF16),
            jax.ShapeDtypeStruct((slots, columns), F32),
            jax.ShapeDtypeStruct((owners - 1, slots, columns), BF16),
        ),
        in_specs=[whole()] * (3 + len(arrived)),
        out_specs=(whole(),) * 3,
        compiler_params=pltpu.CompilerParams(vmem_limit_bytes=8 * MIB),
        name="mix",
    )(residual, places, own, *arrived)


def partial_values(rows, gain_ref, shrink_ref, place, columns, local):
    first = pl.multiple_of(place * columns, columns)
    squares = jnp.sum(rows * rows, axis=1, keepdims=True)
    scaled = rows * gain_ref[:, pl.ds(first, columns)].astype(F32)
    high = scaled.astype(BF16)
    low = (scaled - high.astype(F32)).astype(BF16)
    values = []
    for adapter in range(local):
        mine = slice(adapter * MOST, (adapter + 1) * MOST)
        both = jnp.concatenate([high[mine], low[mine]], axis=0)
        product = lax.dot_general(
            both,
            shrink_ref[adapter, :, pl.ds(first, columns)],
            (((1,), (1,)), ((), ())),
            preferred_element_type=F32,
        )
        values.append(product[:MOST] + product[MOST:])
    return jnp.concatenate(values, axis=0), squares


def own_half_kernel(rows_ref, gain_ref, shrink_ref, values_ref, squares_ref):
    columns = rows_ref.shape[1]
    values, squares = partial_values(
        rows_ref[...], gain_ref, shrink_ref, lax.axis_index("dp"), columns, shrink_ref.shape[0]
    )
    values_ref[...] = values
    squares_ref[...] = jnp.broadcast_to(squares, squares_ref.shape)


def own_half(rows, gain, shrink):
    slots = rows.shape[0]
    rank = shrink.shape[1]
    return pl.pallas_call(
        own_half_kernel,
        out_shape=(
            jax.ShapeDtypeStruct((slots, rank), F32),
            jax.ShapeDtypeStruct((slots, rank), F32),
        ),
        in_specs=[whole()] * 3,
        out_specs=(whole(),) * 2,
        compiler_params=pltpu.CompilerParams(vmem_limit_bytes=8 * MIB),
        cost_estimate=pl.CostEstimate(
            flops=2 * slots * rows.shape[1] * rank, bytes_accessed=2 * MIB, transcendentals=0
        ),
        name="own_half",
    )(rows, gain, shrink)


def finish_kernel(values_ref, squares_ref, gain_ref, shrink_ref, *refs):
    arrived, out_ref = refs[:-1], refs[-1]
    dp = 1 + len(arrived)
    me = lax.axis_index("dp")
    local = shrink_ref.shape[0]
    columns = arrived[0].shape[1]
    values, squares = values_ref[...], squares_ref[:, :1]
    for shift, piece in enumerate(arrived, start=1):
        more, more_squares = partial_values(
            piece[...].astype(F32),
            gain_ref,
            shrink_ref,
            lax.rem(me + dp - shift, dp),
            columns,
            local,
        )
        values, squares = values + more, squares + more_squares
    result = 2.0 * values * lax.rsqrt(squares / (columns * dp) + EPS)
    for adapter in range(local):
        out_ref[adapter, 0] = result[adapter * MOST : (adapter + 1) * MOST]


def finish(values, squares, gain, shrink, arrived):
    local, rank, _ = shrink.shape
    return pl.pallas_call(
        finish_kernel,
        out_shape=jax.ShapeDtypeStruct((local, 1, MOST, rank), F32),
        in_specs=[whole()] * (4 + len(arrived)),
        out_specs=whole(),
        compiler_params=pltpu.CompilerParams(vmem_limit_bytes=8 * MIB),
        name="finish",
    )(values, squares, gain, shrink, *arrived)


def shifted(array, axis, shift):
    count = lax.axis_size(axis)
    return lax.ppermute(array, axis, [(i, (i + shift) % count) for i in range(count)])


def to_partner(array, axis, turn):
    count = lax.axis_size(axis)
    return lax.ppermute(array, axis, [(i, partner_of(i, turn, count)) for i in range(count)])


def body(hidden, down_matrix, residual, next_norm_scale, shrink_matrix, adapter_index):
    dp, tensors, sections = (lax.axis_size(axis) for axis in ("dp", "tensor", "section"))
    me = lax.axis_index("dp")
    depth, _ = down_matrix.shape
    local = shrink_matrix.shape[0]

    others = jnp.stack([shifted(hidden, "dp", shift) for shift in range(1, dp)])

    step = step_of(depth)
    blocks = depth // step
    held_count = max(1, min(blocks // 2, HELD_BYTES // (2 * step * down_matrix.shape[1])))
    held = lax.slice_in_dim(down_matrix, 0, held_count * step)
    held = held.reshape(held_count, step, -1)

    row_adapter = adapter_index[:, 0]
    same = row_adapter[:, None] == row_adapter[None, :]
    rows = row_adapter.shape[0]
    earlier = jnp.arange(rows)[:, None] < jnp.arange(rows)[None, :]
    rank_of = jnp.sum(jnp.logical_and(same, earlier), axis=0)
    owners = (me + jnp.arange(dp)) % dp
    adapters = owners[:, None] * local + jnp.arange(local)[None, :]
    places = jnp.logical_and(
        adapters[:, :, None, None] == row_adapter,
        jnp.arange(MOST)[None, None, :, None] == rank_of,
    )
    places = places.astype(F32).reshape(dp * local * MOST, rows)
    shrink = jnp.swapaxes(shrink_matrix, 1, 2)
    gain = next_norm_scale[None, :]

    in_vmem = [pltpu.with_memory_space_constraint(x, pltpu.VMEM) for x in (hidden, others, held)]
    kept, sent = project(*in_vmem, down_matrix, tensors, sections)
    arrived = [shifted(sent[s - 1], "section", s) for s in range(1, sections)]
    own, *sums = pair(kept, arrived)
    arrived = [to_partner(sums[s - 1], "tensor", s) for s in range(tensors - 1, 0, -1)]
    mixed, routed, leaving = mix(residual, places, own, arrived, local * MOST)
    arrived = [shifted(leaving[s - 1], "dp", s) for s in range(1, dp)]
    values, squares = own_half(routed, gain, shrink)
    shrunk = finish(values, squares, gain, shrink, arrived)
    return (mixed, shrunk)


def solution(mesh):
    placed = (
        P(("groups", "dp"), ("tensor", "section")),
        P(("tensor", "section"), "dp"),
        P(("groups", "tensor", "section"), "dp"),
        P(),
        P("dp", None, None),
        P(("groups", "tensor", "section"), None),
    )
    return jax.shard_map(
        body,
        mesh=mesh,
        in_specs=placed,
        out_specs=(
            P(("groups", "tensor", "section"), "dp"),
            P("dp", ("groups", "tensor", "section"), None, None),
        ),
        check_vma=False,
    )
```

```python
import functools

import jax
import jax.numpy as jnp
from jax import lax
from jax.experimental import pallas as pl
from jax.experimental.pallas import tpu as pltpu
from jax.sharding import PartitionSpec as P

MOST = 2
EPS = 1e-05
DEPTH_STEP = 512
HELD_BYTES = 21 * 2**20
IN_FLIGHT = 4
PIECES = 4
MIB = 2**20
F32 = jnp.float32
BF16 = jnp.bfloat16


def whole():
    return pl.BlockSpec(memory_space=pltpu.VMEM)


def step_of(depth):
    return max(s for s in range(16, DEPTH_STEP + 1, 16) if depth % s == 0)


def fetch_kernel(weight_ref, held_ref, sems):
    count, step, _ = held_ref.shape
    copies = [
        pltpu.make_async_copy(
            weight_ref.at[pl.ds(i * step, step), :], held_ref.at[i], sems.at[i]
        )
        for i in range(count)
    ]
    for copy in copies:
        copy.start()
    for copy in copies:
        copy.wait()


def fetch(weight, count, step):
    columns = weight.shape[1]
    return pl.pallas_call(
        fetch_kernel,
        out_shape=pltpu.VMEM((count, step, columns), weight.dtype),
        in_specs=[pl.BlockSpec(memory_space=pl.ANY)],
        out_specs=whole(),
        scratch_shapes=[pltpu.SemaphoreType.DMA((count,))],
        compiler_params=pltpu.CompilerParams(vmem_limit_bytes=1 * MIB),
        cost_estimate=pl.CostEstimate(
            flops=0, bytes_accessed=2 * count * step * columns, transcendentals=0
        ),
        name="fetch",
    )(weight)


def exchange_order(own_rows, dp, tensors, sections):
    rows = own_rows * dp
    block_rows = rows // (tensors * sections)
    me, tensor, section = (lax.axis_index(axis) for axis in ("dp", "tensor", "section"))
    target = lax.broadcasted_iota(jnp.int32, (rows, rows), 0)
    source = lax.broadcasted_iota(jnp.int32, (rows, rows), 1)
    s = (section + target // (tensors * block_rows)) % sections
    t = partner_of(tensor, target // block_rows % tensors, tensors)
    wanted = (t * sections + s) * block_rows + target % block_rows
    owner = (me + dp - source // own_rows) % dp
    return (wanted == owner * own_rows + source % own_rows).astype(BF16)


def project_kernel(
    own_ref,
    others_ref,
    held_ref,
    weight_ref,
    kept_ref,
    sent_ref,
    rows_ref,
    total_ref,
    rest_ref,
    sems,
    *,
    tensors,
    sections,
):
    held, step, columns = held_ref.shape
    rest = rest_ref.shape[0]
    own_rows = own_ref.shape[0]
    dp = 1 + others_ref.shape[0]
    piece = columns // PIECES
    width = min(piece, 1024)

    def copy_of(i, part):
        lanes = pl.ds(part * piece, piece)
        return pltpu.make_async_copy(
            weight_ref.at[pl.ds((held + i) * step, step), lanes],
            rest_ref.at[i, :, lanes],
            sems.at[i, part],
        )

    for i in range(min(rest, IN_FLIGHT)):
        for part in range(PIECES):
            copy_of(i, part).start()

    order = exchange_order(own_rows, dp, tensors, sections)
    for i in range(held + rest):
        block = slice(i * step, (i + 1) * step)
        stacked = [own_ref[:, block]] + [others_ref[k, :, block] for k in range(dp - 1)]
        rows_ref[i] = jnp.dot(
            order, jnp.concatenate(stacked, axis=0), preferred_element_type=F32
        ).astype(BF16)
    total_ref[...] = jnp.zeros_like(total_ref)

    def add(block_ref, i, part):
        for n in range(part * piece, (part + 1) * piece, width):
            total_ref[:, n : n + width] += jnp.dot(
                rows_ref[i], block_ref[:, n : n + width], preferred_element_type=F32
            )

    def held_step(i, _):
        for part in range(PIECES):
            add(held_ref.at[i], i, part)
        return 0

    def rest_step(i, _):
        for part in range(PIECES):
            copy_of(i, part).wait()

            @pl.when(i + IN_FLIGHT < rest)
            def _():
                copy_of(i + IN_FLIGHT, part).start()

            add(rest_ref.at[i], held + i, part)
        return 0

    lax.fori_loop(0, held, held_step, 0)
    lax.fori_loop(0, rest, rest_step, 0)

    each = kept_ref.shape[0]
    kept_ref[...] = total_ref[:each]
    for turn in range(sections - 1):
        sent_ref[turn] = total_ref[(turn + 1) * each : (turn + 2) * each].astype(BF16)


def project(own, others, held, weight, tensors, sections):
    own_rows, depth = own.shape
    rows = own_rows * (1 + others.shape[0])
    columns = weight.shape[1]
    count, step, _ = held.shape
    rest = depth // step - count
    return pl.pallas_call(
        functools.partial(project_kernel, tensors=tensors, sections=sections),
        out_shape=(
            pltpu.VMEM((rows // sections, columns), F32),
            pltpu.VMEM((sections - 1, rows // sections, columns), BF16),
        ),
        in_specs=[whole(), whole(), whole(), pl.BlockSpec(memory_space=pl.ANY)],
        out_specs=(whole(), whole()),
        scratch_shapes=[
            pltpu.VMEM((depth // step, rows, step), BF16),
            pltpu.VMEM((rows, columns), F32),
            pltpu.VMEM((rest, step, columns), BF16),
            pltpu.SemaphoreType.DMA((rest, PIECES)),
        ],
        compiler_params=pltpu.CompilerParams(vmem_limit_bytes=36 * MIB),
        cost_estimate=pl.CostEstimate(
            flops=2 * rows * depth * columns,
            bytes_accessed=2 * rest * step * columns,
            transcendentals=0,
        ),
        name="project",
    )(own, others, held, weight)


def partner_of(me, turn, count):
    if count & (count - 1) == 0:
        return me ^ turn
    return (me + turn) % count


def pair_kernel(kept_ref, *refs):
    outs = refs[-(kept_ref.shape[0] // refs[-1].shape[0]) :]
    arrived = refs[: -len(outs)]
    for turn, out_ref in enumerate(outs):
        block_rows = out_ref.shape[0]
        mine = slice(turn * block_rows, (turn + 1) * block_rows)
        block = kept_ref[mine, :]
        for piece in arrived:
            block = block + piece[mine, :].astype(F32)
        out_ref[...] = block.astype(out_ref.dtype)


def pair(kept, arrived, tensors):
    rows, columns = kept.shape
    return pl.pallas_call(
        pair_kernel,
        out_shape=[
            jax.ShapeDtypeStruct((rows // tensors, columns), F32 if turn == 0 else BF16)
            for turn in range(tensors)
        ],
        in_specs=[whole()] * (1 + len(arrived)),
        out_specs=[whole()] * tensors,
        compiler_params=pltpu.CompilerParams(vmem_limit_bytes=8 * MIB),
        name="pair",
    )(kept, *arrived)


def places_of(row, slots, owners, local):
    rows = row.shape[1]
    upper = lax.broadcasted_iota(jnp.int32, (rows, rows), 0)
    lower = lax.broadcasted_iota(jnp.int32, (rows, rows), 1)
    column = jnp.sum(jnp.where(upper == lower, row, 0), axis=1, keepdims=True)
    before = jnp.logical_and(column == row, upper < lower)
    rank_of = jnp.sum(before.astype(jnp.int32), axis=0, keepdims=True)
    slot = lax.broadcasted_iota(jnp.int32, (slots * owners, rows), 0)
    owner = (lax.axis_index("dp") + slot // slots) % owners
    adapter = owner * local + slot // MOST % local
    return jnp.logical_and(row == adapter, rank_of == slot % MOST).astype(F32)


def mix_kernel(residual_ref, index_ref, own_ref, *refs):
    arrived, (mixed_ref, kept_ref, sent_ref) = refs[:-3], refs[-3:]
    slots = kept_ref.shape[0]
    places = places_of(index_ref[...], slots, 1 + sent_ref.shape[0], slots // MOST)
    total = own_ref[...] + residual_ref[...].astype(F32)
    for piece in arrived:
        total = total + piece[...].astype(F32)
    mixed = total.astype(BF16)
    mixed_ref[...] = mixed
    widened = mixed.astype(F32)
    routed = sum(
        places[:, row : row + 1] * widened[row : row + 1, :] for row in range(widened.shape[0])
    )
    kept_ref[...] = routed[:slots]
    for turn in range(sent_ref.shape[0]):
        sent_ref[turn] = routed[(turn + 1) * slots : (turn + 2) * slots].astype(BF16)


def mix(residual, index, own, arrived, slots, owners):
    rows, columns = residual.shape
    return pl.pallas_call(
        mix_kernel,
        out_shape=(
            pltpu.VMEM((rows, columns), BF16),
            jax.ShapeDtypeStruct((slots, columns), F32),
            jax.ShapeDtypeStruct((owners - 1, slots, columns), BF16),
        ),
        in_specs=[whole()] * (3 + len(arrived)),
        out_specs=(whole(),) * 3,
        compiler_params=pltpu.CompilerParams(vmem_limit_bytes=8 * MIB),
        name="mix",
    )(residual, index, own, *arrived)


def partial_values(rows, gain_ref, shrink_ref, place, columns, local):
    first = pl.multiple_of(place * columns, columns)
    squares = jnp.sum(rows * rows, axis=1, keepdims=True)
    scaled = rows * gain_ref[:, pl.ds(first, columns)].astype(F32)
    high = scaled.astype(BF16)
    low = (scaled - high.astype(F32)).astype(BF16)
    values = []
    for adapter in range(local):
        mine = slice(adapter * MOST, (adapter + 1) * MOST)
        both = jnp.concatenate([high[mine], low[mine]], axis=0)
        product = lax.dot_general(
            both,
            shrink_ref[adapter, :, pl.ds(first, columns)],
            (((1,), (1,)), ((), ())),
            preferred_element_type=F32,
        )
        values.append(product[:MOST] + product[MOST:])
    return jnp.concatenate(values, axis=0), squares


def own_half_kernel(rows_ref, gain_ref, shrink_ref, values_ref, squares_ref):
    columns = rows_ref.shape[1]
    values, squares = partial_values(
        rows_ref[...], gain_ref, shrink_ref, lax.axis_index("dp"), columns, shrink_ref.shape[0]
    )
    values_ref[...] = values
    squares_ref[...] = jnp.broadcast_to(squares, squares_ref.shape)


def own_half(rows, gain, shrink):
    slots = rows.shape[0]
    rank = shrink.shape[1]
    return pl.pallas_call(
        own_half_kernel,
        out_shape=(
            jax.ShapeDtypeStruct((slots, rank), F32),
            jax.ShapeDtypeStruct((slots, rank), F32),
        ),
        in_specs=[whole()] * 3,
        out_specs=(whole(),) * 2,
        compiler_params=pltpu.CompilerParams(vmem_limit_bytes=8 * MIB),
        cost_estimate=pl.CostEstimate(
            flops=2 * slots * rows.shape[1] * rank, bytes_accessed=2 * MIB, transcendentals=0
        ),
        name="own_half",
    )(rows, gain, shrink)


def finish_kernel(values_ref, squares_ref, gain_ref, shrink_ref, *refs):
    arrived, out_ref = refs[:-1], refs[-1]
    dp = 1 + len(arrived)
    me = lax.axis_index("dp")
    local = shrink_ref.shape[0]
    columns = arrived[0].shape[1]
    values, squares = values_ref[...], squares_ref[:, :1]
    for shift, piece in enumerate(arrived, start=1):
        more, more_squares = partial_values(
            piece[...].astype(F32),
            gain_ref,
            shrink_ref,
            lax.rem(me + dp - shift, dp),
            columns,
            local,
        )
        values, squares = values + more, squares + more_squares
    result = 2.0 * values * lax.rsqrt(squares / (columns * dp) + EPS)
    for adapter in range(local):
        out_ref[adapter, 0] = result[adapter * MOST : (adapter + 1) * MOST]


def finish(values, squares, gain, shrink, arrived):
    local, rank, _ = shrink.shape
    return pl.pallas_call(
        finish_kernel,
        out_shape=jax.ShapeDtypeStruct((local, 1, MOST, rank), F32),
        in_specs=[whole()] * (4 + len(arrived)),
        out_specs=whole(),
        compiler_params=pltpu.CompilerParams(vmem_limit_bytes=8 * MIB),
        name="finish",
    )(values, squares, gain, shrink, *arrived)


def shifted(array, axis, shift):
    count = lax.axis_size(axis)
    return lax.ppermute(array, axis, [(i, (i + shift) % count) for i in range(count)])


def to_partner(array, axis, turn):
    count = lax.axis_size(axis)
    return lax.ppermute(array, axis, [(i, partner_of(i, turn, count)) for i in range(count)])


def body(hidden, down_matrix, residual, next_norm_scale, shrink_matrix, adapter_index):
    dp, tensors, sections = (lax.axis_size(axis) for axis in ("dp", "tensor", "section"))
    depth, _ = down_matrix.shape
    local = shrink_matrix.shape[0]

    others = jnp.stack([shifted(hidden, "dp", shift) for shift in range(1, dp)])

    step = step_of(depth)
    blocks = depth // step
    held_count = max(1, min(blocks // 2, HELD_BYTES // (2 * step * down_matrix.shape[1])))
    held = fetch(down_matrix, held_count, step)

    shrink = jnp.swapaxes(shrink_matrix, 1, 2)
    gain = next_norm_scale[None, :]

    in_vmem = [pltpu.with_memory_space_constraint(x, pltpu.VMEM) for x in (hidden, others, held)]
    kept, sent = project(*in_vmem, down_matrix, tensors, sections)
    arrived = [shifted(sent[s - 1], "section", s) for s in range(1, sections)]
    own, *sums = pair(kept, arrived, tensors)
    arrived = [to_partner(sums[s - 1], "tensor", s) for s in range(tensors - 1, 0, -1)]
    index = adapter_index.reshape(1, -1)
    mixed, routed, leaving = mix(residual, index, own, arrived, local * MOST, dp)
    arrived = [shifted(leaving[s - 1], "dp", s) for s in range(1, dp)]
    values, squares = own_half(routed, gain, shrink)
    shrunk = finish(values, squares, gain, shrink, arrived)
    return (mixed, shrunk)


def solution(mesh):
    placed = (
        P(("groups", "dp"), ("tensor", "section")),
        P(("tensor", "section"), "dp"),
        P(("groups", "tensor", "section"), "dp"),
        P(),
        P("dp", None, None),
        P(("groups", "tensor", "section"), None),
    )
    return jax.shard_map(
        body,
        mesh=mesh,
        in_specs=placed,
        out_specs=(
            P(("groups", "tensor", "section"), "dp"),
            P("dp", ("groups", "tensor", "section"), None, None),
        ),
        check_vma=False,
    )
```

```python
import functools

import jax
import jax.numpy as jnp
from jax import lax
from jax.experimental import pallas as pl
from jax.experimental.pallas import tpu as pltpu
from jax.sharding import PartitionSpec as P

MOST = 2
EPS = 1e-05
DEPTH_STEP = 512
HELD_BYTES = 21 * 2**20
WIDTH = 1024
MIB = 2**20
F32 = jnp.float32
BF16 = jnp.bfloat16


def whole():
    return pl.BlockSpec(memory_space=pltpu.VMEM)


def step_of(depth):
    return max(s for s in range(16, DEPTH_STEP + 1, 16) if depth % s == 0)


def fetch_kernel(weight_ref, held_ref, sems):
    count, step, _ = held_ref.shape
    copies = [
        pltpu.make_async_copy(
            weight_ref.at[pl.ds(i * step, step), :], held_ref.at[i], sems.at[i]
        )
        for i in range(count)
    ]
    for copy in copies:
        copy.start()
    for copy in copies:
        copy.wait()


def fetch(weight, count, step):
    columns = weight.shape[1]
    return pl.pallas_call(
        fetch_kernel,
        out_shape=pltpu.VMEM((count, step, columns), weight.dtype),
        in_specs=[pl.BlockSpec(memory_space=pl.ANY)],
        out_specs=whole(),
        scratch_shapes=[pltpu.SemaphoreType.DMA((count,))],
        compiler_params=pltpu.CompilerParams(vmem_limit_bytes=1 * MIB),
        cost_estimate=pl.CostEstimate(
            flops=0, bytes_accessed=2 * count * step * columns, transcendentals=0
        ),
        name="fetch",
    )(weight)


def project_kernel(
    own_ref,
    others_ref,
    held_ref,
    weight_ref,
    kept_ref,
    sent_ref,
    rows_ref,
    total_ref,
    rest_ref,
    sems,
    *,
    tensors,
    sections,
):
    held, step, columns = held_ref.shape
    rest = rest_ref.shape[0]
    own_rows = own_ref.shape[0]
    dp = 1 + others_ref.shape[0]
    me, tensor, section = (lax.axis_index(axis) for axis in ("dp", "tensor", "section"))
    width = min(columns, WIDTH)
    half = step // 2

    def copy_of(i, sem, first=0, size=step):
        return pltpu.make_async_copy(
            weight_ref.at[pl.ds((held + i) * step + first, size), :],
            rest_ref.at[i, pl.ds(first, size), :],
            sems.at[sem],
        )

    last = [copy_of(rest - 1, rest - 1, 0, half), copy_of(rest - 1, rest, half, half)]
    for i in range(rest - 1):
        copy_of(i, i).start()
    for copy in last:
        copy.start()

    for i in range(held + rest):
        block = slice(i * step, (i + 1) * step)
        for shift in range(dp):
            first = pl.multiple_of((me + dp - shift) % dp * own_rows, own_rows)
            source = own_ref[:, block] if shift == 0 else others_ref[shift - 1, :, block]
            rows_ref[i, pl.ds(first, own_rows), :] = source

    def held_step(n, _):
        lanes = pl.ds(pl.multiple_of(n * width, width), width)
        total_ref[:, lanes] = sum(
            jnp.dot(rows_ref[i], held_ref[i, :, lanes], preferred_element_type=F32)
            for i in range(held)
        )
        return 0

    def add(i, part=slice(None)):
        for n in range(0, columns, width):
            lanes = slice(n, n + width)
            total_ref[:, lanes] += jnp.dot(
                rows_ref[held + i, :, part], rest_ref[i, part, lanes], preferred_element_type=F32
            )

    def rest_step(i, _):
        copy_of(i, i).wait()
        add(i)
        return 0

    lax.fori_loop(0, columns // width, held_step, 0)
    lax.fori_loop(0, rest - 1, rest_step, 0)
    for copy, part in zip(last, (slice(0, half), slice(half, step))):
        copy.wait()
        add(rest - 1, part)

    block_rows = kept_ref.shape[0] // tensors
    group = sections * block_rows
    for n in range(0, columns, width):
        lanes = slice(n, n + width)
        turned = []
        for turn in range(tensors):
            first = pl.multiple_of(partner_of(tensor, turn, tensors) * group, group)
            rows = total_ref[pl.ds(first, group), lanes]
            turned.append(pltpu.roll(rows, (sections - section) % sections * block_rows, 0))
        for s in range(sections):
            part = slice(s * block_rows, (s + 1) * block_rows)
            rows = jnp.concatenate([block[part] for block in turned], axis=0)
            if s == 0:
                kept_ref[:, lanes] = rows
            else:
                sent_ref[s - 1, :, lanes] = rows.astype(BF16)


def project(own, others, held, weight, tensors, sections):
    own_rows, depth = own.shape
    rows = own_rows * (1 + others.shape[0])
    columns = weight.shape[1]
    count, step, _ = held.shape
    rest = depth // step - count
    return pl.pallas_call(
        functools.partial(project_kernel, tensors=tensors, sections=sections),
        out_shape=(
            pltpu.VMEM((rows // sections, columns), F32),
            pltpu.VMEM((sections - 1, rows // sections, columns), BF16),
        ),
        in_specs=[whole(), whole(), whole(), pl.BlockSpec(memory_space=pl.ANY)],
        out_specs=(whole(), whole()),
        scratch_shapes=[
            pltpu.VMEM((depth // step, rows, step), BF16),
            pltpu.VMEM((rows, columns), F32),
            pltpu.VMEM((rest, step, columns), BF16),
            pltpu.SemaphoreType.DMA((rest + 1,)),
        ],
        compiler_params=pltpu.CompilerParams(vmem_limit_bytes=36 * MIB),
        cost_estimate=pl.CostEstimate(
            flops=2 * rows * depth * columns,
            bytes_accessed=2 * rest * step * columns,
            transcendentals=0,
        ),
        name="project",
    )(own, others, held, weight)


def partner_of(me, turn, count):
    if count & (count - 1) == 0:
        return me ^ turn
    return (me + turn) % count


def pair_kernel(kept_ref, *refs):
    outs = refs[-(kept_ref.shape[0] // refs[-1].shape[0]) :]
    arrived = refs[: -len(outs)]
    total = kept_ref[...]
    for piece in arrived:
        total = total + piece[...].astype(F32)
    for turn, out_ref in enumerate(outs):
        block_rows = out_ref.shape[0]
        block = total[turn * block_rows : (turn + 1) * block_rows]
        out_ref[...] = block.astype(out_ref.dtype)


def pair(kept, arrived, tensors):
    rows, columns = kept.shape
    return pl.pallas_call(
        pair_kernel,
        out_shape=[
            jax.ShapeDtypeStruct((rows // tensors, columns), F32 if turn == 0 else BF16)
            for turn in range(tensors)
        ],
        in_specs=[whole()] * (1 + len(arrived)),
        out_specs=[whole()] * tensors,
        compiler_params=pltpu.CompilerParams(vmem_limit_bytes=8 * MIB),
        name="pair",
    )(kept, *arrived)


def places_of(row, slots, owners, local):
    rows = row.shape[1]
    upper = lax.broadcasted_iota(jnp.int32, (rows, rows), 0)
    lower = lax.broadcasted_iota(jnp.int32, (rows, rows), 1)
    column = jnp.sum(jnp.where(upper == lower, row, 0), axis=1, keepdims=True)
    before = jnp.logical_and(column == row, upper < lower)
    rank_of = jnp.sum(before.astype(jnp.int32), axis=0, keepdims=True)
    slot = lax.broadcasted_iota(jnp.int32, (slots * owners, rows), 0)
    owner = (lax.axis_index("dp") + slot // slots) % owners
    adapter = owner * local + slot // MOST % local
    return jnp.logical_and(row == adapter, rank_of == slot % MOST).astype(F32)


def places_kernel(index_ref, places_ref, *, slots, owners):
    places_ref[...] = places_of(index_ref[...], slots, owners, slots // MOST)


def find_places(index, slots, owners):
    return pl.pallas_call(
        functools.partial(places_kernel, slots=slots, owners=owners),
        out_shape=jax.ShapeDtypeStruct((slots * owners, index.shape[1]), F32),
        in_specs=[whole()],
        out_specs=whole(),
        compiler_params=pltpu.CompilerParams(vmem_limit_bytes=1 * MIB),
        name="find_places",
    )(index)


def mix_kernel(residual_ref, places_ref, own_ref, *refs):
    arrived, (mixed_ref, kept_ref, sent_ref) = refs[:-3], refs[-3:]
    slots = kept_ref.shape[0]
    places = places_ref[...]
    total = own_ref[...] + residual_ref[...].astype(F32)
    for piece in arrived:
        total = total + piece[...].astype(F32)
    mixed = total.astype(BF16)
    mixed_ref[...] = mixed
    widened = mixed.astype(F32)
    routed = sum(
        places[:, row : row + 1] * widened[row : row + 1, :] for row in range(widened.shape[0])
    )
    kept_ref[...] = routed[:slots]
    for turn in range(sent_ref.shape[0]):
        sent_ref[turn] = routed[(turn + 1) * slots : (turn + 2) * slots].astype(BF16)


def mix(residual, places, own, arrived, slots, owners):
    rows, columns = residual.shape
    return pl.pallas_call(
        mix_kernel,
        out_shape=(
            pltpu.VMEM((rows, columns), BF16),
            jax.ShapeDtypeStruct((slots, columns), F32),
            jax.ShapeDtypeStruct((owners - 1, slots, columns), BF16),
        ),
        in_specs=[whole()] * (3 + len(arrived)),
        out_specs=(whole(),) * 3,
        compiler_params=pltpu.CompilerParams(vmem_limit_bytes=8 * MIB),
        name="mix",
    )(residual, places, own, *arrived)


def partial_values(rows, gain_ref, shrink_ref, place, columns, local):
    first = pl.multiple_of(place * columns, columns)
    squares = jnp.sum(rows * rows, axis=1, keepdims=True)
    scaled = rows * gain_ref[:, pl.ds(first, columns)].astype(F32)
    high = scaled.astype(BF16)
    low = (scaled - high.astype(F32)).astype(BF16)
    values = []
    for adapter in range(local):
        mine = slice(adapter * MOST, (adapter + 1) * MOST)
        both = jnp.concatenate([high[mine], low[mine]], axis=0)
        product = lax.dot_general(
            both,
            shrink_ref[adapter, :, pl.ds(first, columns)],
            (((1,), (1,)), ((), ())),
            preferred_element_type=F32,
        )
        values.append(product[:MOST] + product[MOST:])
    return jnp.concatenate(values, axis=0), squares


def own_half_kernel(rows_ref, gain_ref, shrink_ref, values_ref, squares_ref):
    columns = rows_ref.shape[1]
    values, squares = partial_values(
        rows_ref[...], gain_ref, shrink_ref, lax.axis_index("dp"), columns, shrink_ref.shape[0]
    )
    values_ref[...] = values
    squares_ref[...] = jnp.broadcast_to(squares, squares_ref.shape)


def own_half(rows, gain, shrink):
    slots = rows.shape[0]
    rank = shrink.shape[1]
    return pl.pallas_call(
        own_half_kernel,
        out_shape=(
            jax.ShapeDtypeStruct((slots, rank), F32),
            jax.ShapeDtypeStruct((slots, rank), F32),
        ),
        in_specs=[whole()] * 3,
        out_specs=(whole(),) * 2,
        compiler_params=pltpu.CompilerParams(vmem_limit_bytes=8 * MIB),
        cost_estimate=pl.CostEstimate(
            flops=2 * slots * rows.shape[1] * rank, bytes_accessed=2 * MIB, transcendentals=0
        ),
        name="own_half",
    )(rows, gain, shrink)


def finish_kernel(values_ref, squares_ref, gain_ref, shrink_ref, *refs):
    arrived, out_ref = refs[:-1], refs[-1]
    dp = 1 + len(arrived)
    me = lax.axis_index("dp")
    local = shrink_ref.shape[0]
    columns = arrived[0].shape[1]
    values, squares = values_ref[...], squares_ref[:, :1]
    for shift, piece in enumerate(arrived, start=1):
        more, more_squares = partial_values(
            piece[...].astype(F32),
            gain_ref,
            shrink_ref,
            lax.rem(me + dp - shift, dp),
            columns,
            local,
        )
        values, squares = values + more, squares + more_squares
    result = 2.0 * values * lax.rsqrt(squares / (columns * dp) + EPS)
    for adapter in range(local):
        out_ref[adapter, 0] = result[adapter * MOST : (adapter + 1) * MOST]


def finish(values, squares, gain, shrink, arrived):
    local, rank, _ = shrink.shape
    return pl.pallas_call(
        finish_kernel,
        out_shape=jax.ShapeDtypeStruct((local, 1, MOST, rank), F32),
        in_specs=[whole()] * (4 + len(arrived)),
        out_specs=whole(),
        compiler_params=pltpu.CompilerParams(vmem_limit_bytes=8 * MIB),
        name="finish",
    )(values, squares, gain, shrink, *arrived)


def shifted(array, axis, shift):
    count = lax.axis_size(axis)
    return lax.ppermute(array, axis, [(i, (i + shift) % count) for i in range(count)])


def to_partner(array, axis, turn):
    count = lax.axis_size(axis)
    return lax.ppermute(array, axis, [(i, partner_of(i, turn, count)) for i in range(count)])


def body(hidden, down_matrix, residual, next_norm_scale, shrink_matrix, adapter_index):
    dp, tensors, sections = (lax.axis_size(axis) for axis in ("dp", "tensor", "section"))
    depth, _ = down_matrix.shape
    local = shrink_matrix.shape[0]

    others = jnp.stack([shifted(hidden, "dp", shift) for shift in range(1, dp)])

    step = step_of(depth)
    blocks = depth // step
    held_count = max(1, min(blocks // 2, HELD_BYTES // (2 * step * down_matrix.shape[1])))
    held = fetch(down_matrix, held_count, step)

    shrink = jnp.swapaxes(shrink_matrix, 1, 2)
    gain = next_norm_scale[None, :]

    in_vmem = [pltpu.with_memory_space_constraint(x, pltpu.VMEM) for x in (hidden, others, held)]
    kept, sent = project(*in_vmem, down_matrix, tensors, sections)
    index, kept = lax.optimization_barrier((adapter_index.reshape(1, -1), kept))
    places = find_places(index, local * MOST, dp)
    arrived = [shifted(sent[s - 1], "section", s) for s in range(1, sections)]
    own, *sums = pair(kept, arrived, tensors)
    arrived = [to_partner(sums[s - 1], "tensor", s) for s in range(tensors - 1, 0, -1)]
    mixed, routed, leaving = mix(residual, places, own, arrived, local * MOST, dp)
    arrived = [shifted(leaving[s - 1], "dp", s) for s in range(1, dp)]
    values, squares = own_half(routed, gain, shrink)
    shrunk = finish(values, squares, gain, shrink, arrived)
    return (mixed, shrunk)


def solution(mesh):
    placed = (
        P(("groups", "dp"), ("tensor", "section")),
        P(("tensor", "section"), "dp"),
        P(("groups", "tensor", "section"), "dp"),
        P(),
        P("dp", None, None),
        P(("groups", "tensor", "section"), None),
    )
    return jax.shard_map(
        body,
        mesh=mesh,
        in_specs=placed,
        out_specs=(
            P(("groups", "tensor", "section"), "dp"),
            P("dp", ("groups", "tensor", "section"), None, None),
        ),
        check_vma=False,
    )
```

```python
import functools

import jax
import jax.numpy as jnp
from jax import lax
from jax.experimental import pallas as pl
from jax.experimental.pallas import tpu as pltpu
from jax.sharding import PartitionSpec as P

MOST = 2
EPS = 1e-05
DEPTH_STEP = 512
HELD_BYTES = 21 * 2**20
WIDTH = 1024
MIB = 2**20
F32 = jnp.float32
BF16 = jnp.bfloat16


def whole():
    return pl.BlockSpec(memory_space=pltpu.VMEM)


def step_of(depth):
    return max(s for s in range(16, DEPTH_STEP + 1, 16) if depth % s == 0)


def fetch_kernel(weight_ref, held_ref, sems):
    count, step, _ = held_ref.shape
    copies = [
        pltpu.make_async_copy(
            weight_ref.at[pl.ds(i * step, step), :], held_ref.at[i], sems.at[i]
        )
        for i in range(count)
    ]
    for copy in copies:
        copy.start()
    for copy in copies:
        copy.wait()


def fetch(weight, count, step):
    columns = weight.shape[1]
    return pl.pallas_call(
        fetch_kernel,
        out_shape=pltpu.VMEM((count, step, columns), weight.dtype),
        in_specs=[pl.BlockSpec(memory_space=pl.ANY)],
        out_specs=whole(),
        scratch_shapes=[pltpu.SemaphoreType.DMA((count,))],
        compiler_params=pltpu.CompilerParams(vmem_limit_bytes=1 * MIB),
        cost_estimate=pl.CostEstimate(
            flops=0, bytes_accessed=2 * count * step * columns, transcendentals=0
        ),
        name="fetch",
    )(weight)


def project_kernel(
    own_ref,
    others_ref,
    held_ref,
    weight_ref,
    kept_ref,
    sent_ref,
    rows_ref,
    total_ref,
    rest_ref,
    sems,
    *,
    tensors,
    sections,
):
    held, step, columns = held_ref.shape
    rest = rest_ref.shape[0]
    own_rows = own_ref.shape[0]
    dp = 1 + others_ref.shape[0]
    me, tensor, section = (lax.axis_index(axis) for axis in ("dp", "tensor", "section"))
    width = min(columns, WIDTH)
    half = step // 2

    def copy_of(i, sem, first=0, size=step):
        return pltpu.make_async_copy(
            weight_ref.at[pl.ds((held + i) * step + first, size), :],
            rest_ref.at[i, pl.ds(first, size), :],
            sems.at[sem],
        )

    last = [copy_of(rest - 1, rest - 1, 0, half), copy_of(rest - 1, rest, half, half)]
    for i in range(rest - 1):
        copy_of(i, i).start()
    for copy in last:
        copy.start()

    for i in range(held + rest):
        block = slice(i * step, (i + 1) * step)
        for shift in range(dp):
            first = pl.multiple_of((me + dp - shift) % dp * own_rows, own_rows)
            source = own_ref[:, block] if shift == 0 else others_ref[shift - 1, :, block]
            rows_ref[i, pl.ds(first, own_rows), :] = source

    def held_step(n, _):
        lanes = pl.ds(pl.multiple_of(n * width, width), width)
        total_ref[:, lanes] = sum(
            jnp.dot(rows_ref[i], held_ref[i, :, lanes], preferred_element_type=F32)
            for i in range(held)
        )
        return 0

    def add(i, part=slice(None)):
        for n in range(0, columns, width):
            lanes = slice(n, n + width)
            total_ref[:, lanes] += jnp.dot(
                rows_ref[held + i, :, part], rest_ref[i, part, lanes], preferred_element_type=F32
            )

    def rest_step(i, _):
        copy_of(i, i).wait()
        add(i)
        return 0

    lax.fori_loop(0, columns // width, held_step, 0)
    lax.fori_loop(0, rest - 1, rest_step, 0)
    for copy, part in zip(last, (slice(0, half), slice(half, step))):
        copy.wait()
        add(rest - 1, part)

    block_rows = kept_ref.shape[0] // tensors
    group = sections * block_rows
    for n in range(0, columns, width):
        lanes = slice(n, n + width)
        turned = []
        for turn in range(tensors):
            first = pl.multiple_of(partner_of(tensor, turn, tensors) * group, group)
            rows = total_ref[pl.ds(first, group), lanes]
            turned.append(pltpu.roll(rows, (sections - section) % sections * block_rows, 0))
        for s in range(sections):
            part = slice(s * block_rows, (s + 1) * block_rows)
            rows = jnp.concatenate([block[part] for block in turned], axis=0)
            if s == 0:
                kept_ref[:, lanes] = rows
            else:
                sent_ref[s - 1, :, lanes] = rows.astype(BF16)


def project(own, others, held, weight, tensors, sections):
    own_rows, depth = own.shape
    rows = own_rows * (1 + others.shape[0])
    columns = weight.shape[1]
    count, step, _ = held.shape
    rest = depth // step - count
    return pl.pallas_call(
        functools.partial(project_kernel, tensors=tensors, sections=sections),
        out_shape=(
            pltpu.VMEM((rows // sections, columns), F32),
            pltpu.VMEM((sections - 1, rows // sections, columns), BF16),
        ),
        in_specs=[whole(), whole(), whole(), pl.BlockSpec(memory_space=pl.ANY)],
        out_specs=(whole(), whole()),
        scratch_shapes=[
            pltpu.VMEM((depth // step, rows, step), BF16),
            pltpu.VMEM((rows, columns), F32),
            pltpu.VMEM((rest, step, columns), BF16),
            pltpu.SemaphoreType.DMA((rest + 1,)),
        ],
        compiler_params=pltpu.CompilerParams(vmem_limit_bytes=36 * MIB),
        cost_estimate=pl.CostEstimate(
            flops=2 * rows * depth * columns,
            bytes_accessed=2 * rest * step * columns,
            transcendentals=0,
        ),
        name="project",
    )(own, others, held, weight)


def partner_of(me, turn, count):
    if count & (count - 1) == 0:
        return me ^ turn
    return (me + turn) % count


def turn_of(me, partner, count):
    if count & (count - 1) == 0:
        return me ^ partner
    return (partner - me) % count


def exchange_plan(count):
    if count == 4:
        return [
            {2: 1, 3: 0},
            {0: 1, 2: 0},
            {0: 2, 1: 0, 2: 3, 3: 1},
            {0: 3, 1: 2},
            {1: 3, 3: 2},
        ]
    return [{i: partner_of(i, turn, count) for i in range(count)} for turn in range(count - 1, 0, -1)]


def pair_kernel(kept_ref, *refs, plan, tensors):
    arrived, (own_ref, *outs) = refs[: -1 - len(plan)], refs[-1 - len(plan) :]
    me = lax.axis_index("tensor")
    block_rows = own_ref.shape[0]
    total = kept_ref[...]
    for piece in arrived:
        total = total + piece[...].astype(F32)
    blocks = [total[turn * block_rows : (turn + 1) * block_rows] for turn in range(tensors)]
    own_ref[...] = blocks[0]
    for sends, out_ref in zip(plan, outs):
        turns = {i: turn_of(i, j, tensors) for i, j in sends.items()}
        block = blocks[turns[min(turns)]]
        for i, turn in turns.items():
            if turn != turns[min(turns)]:
                block = jnp.where(me == i, blocks[turn], block)
        out_ref[...] = block.astype(out_ref.dtype)


def pair(kept, arrived, plan, tensors):
    rows, columns = kept.shape
    block = (rows // tensors, columns)
    return pl.pallas_call(
        functools.partial(pair_kernel, plan=plan, tensors=tensors),
        out_shape=[jax.ShapeDtypeStruct(block, F32)] + [jax.ShapeDtypeStruct(block, BF16)] * len(plan),
        in_specs=[whole()] * (1 + len(arrived)),
        out_specs=[whole()] * (1 + len(plan)),
        compiler_params=pltpu.CompilerParams(vmem_limit_bytes=8 * MIB),
        name="pair",
    )(kept, *arrived)


def places_of(row, slots, owners, local):
    rows = row.shape[1]
    upper = lax.broadcasted_iota(jnp.int32, (rows, rows), 0)
    lower = lax.broadcasted_iota(jnp.int32, (rows, rows), 1)
    column = jnp.sum(jnp.where(upper == lower, row, 0), axis=1, keepdims=True)
    before = jnp.logical_and(column == row, upper < lower)
    rank_of = jnp.sum(before.astype(jnp.int32), axis=0, keepdims=True)
    slot = lax.broadcasted_iota(jnp.int32, (slots * owners, rows), 0)
    owner = (lax.axis_index("dp") + slot // slots) % owners
    adapter = owner * local + slot // MOST % local
    return jnp.logical_and(row == adapter, rank_of == slot % MOST).astype(F32)


def places_kernel(index_ref, places_ref, *, slots, owners):
    places_ref[...] = places_of(index_ref[...], slots, owners, slots // MOST)


def find_places(index, slots, owners):
    return pl.pallas_call(
        functools.partial(places_kernel, slots=slots, owners=owners),
        out_shape=jax.ShapeDtypeStruct((slots * owners, index.shape[1]), F32),
        in_specs=[whole()],
        out_specs=whole(),
        compiler_params=pltpu.CompilerParams(vmem_limit_bytes=1 * MIB),
        name="find_places",
    )(index)


def mix_kernel(residual_ref, places_ref, own_ref, *refs):
    arrived, (mixed_ref, kept_ref, sent_ref) = refs[:-3], refs[-3:]
    slots = kept_ref.shape[0]
    places = places_ref[...]
    total = own_ref[...] + residual_ref[...].astype(F32)
    for piece in arrived:
        total = total + piece[...].astype(F32)
    mixed = total.astype(BF16)
    mixed_ref[...] = mixed
    widened = mixed.astype(F32)
    routed = sum(
        places[:, row : row + 1] * widened[row : row + 1, :] for row in range(widened.shape[0])
    )
    kept_ref[...] = routed[:slots]
    for turn in range(sent_ref.shape[0]):
        sent_ref[turn] = routed[(turn + 1) * slots : (turn + 2) * slots].astype(BF16)


def mix(residual, places, own, arrived, slots, owners):
    rows, columns = residual.shape
    return pl.pallas_call(
        mix_kernel,
        out_shape=(
            pltpu.VMEM((rows, columns), BF16),
            jax.ShapeDtypeStruct((slots, columns), F32),
            jax.ShapeDtypeStruct((owners - 1, slots, columns), BF16),
        ),
        in_specs=[whole()] * (3 + len(arrived)),
        out_specs=(whole(),) * 3,
        compiler_params=pltpu.CompilerParams(vmem_limit_bytes=8 * MIB),
        name="mix",
    )(residual, places, own, *arrived)


def partial_values(rows, gain_ref, shrink_ref, place, columns, local):
    first = pl.multiple_of(place * columns, columns)
    squares = jnp.sum(rows * rows, axis=1, keepdims=True)
    scaled = rows * gain_ref[:, pl.ds(first, columns)].astype(F32)
    high = scaled.astype(BF16)
    low = (scaled - high.astype(F32)).astype(BF16)
    values = []
    for adapter in range(local):
        mine = slice(adapter * MOST, (adapter + 1) * MOST)
        both = jnp.concatenate([high[mine], low[mine]], axis=0)
        product = lax.dot_general(
            both,
            shrink_ref[adapter, :, pl.ds(first, columns)],
            (((1,), (1,)), ((), ())),
            preferred_element_type=F32,
        )
        values.append(product[:MOST] + product[MOST:])
    return jnp.concatenate(values, axis=0), squares


def own_half_kernel(rows_ref, gain_ref, shrink_ref, values_ref, squares_ref):
    columns = rows_ref.shape[1]
    values, squares = partial_values(
        rows_ref[...], gain_ref, shrink_ref, lax.axis_index("dp"), columns, shrink_ref.shape[0]
    )
    values_ref[...] = values
    squares_ref[...] = jnp.broadcast_to(squares, squares_ref.shape)


def own_half(rows, gain, shrink):
    slots = rows.shape[0]
    rank = shrink.shape[1]
    return pl.pallas_call(
        own_half_kernel,
        out_shape=(
            jax.ShapeDtypeStruct((slots, rank), F32),
            jax.ShapeDtypeStruct((slots, rank), F32),
        ),
        in_specs=[whole()] * 3,
        out_specs=(whole(),) * 2,
        compiler_params=pltpu.CompilerParams(vmem_limit_bytes=8 * MIB),
        cost_estimate=pl.CostEstimate(
            flops=2 * slots * rows.shape[1] * rank, bytes_accessed=2 * MIB, transcendentals=0
        ),
        name="own_half",
    )(rows, gain, shrink)


def finish_kernel(values_ref, squares_ref, gain_ref, shrink_ref, *refs):
    arrived, out_ref = refs[:-1], refs[-1]
    dp = 1 + len(arrived)
    me = lax.axis_index("dp")
    local = shrink_ref.shape[0]
    columns = arrived[0].shape[1]
    values, squares = values_ref[...], squares_ref[:, :1]
    for shift, piece in enumerate(arrived, start=1):
        more, more_squares = partial_values(
            piece[...].astype(F32),
            gain_ref,
            shrink_ref,
            lax.rem(me + dp - shift, dp),
            columns,
            local,
        )
        values, squares = values + more, squares + more_squares
    result = 2.0 * values * lax.rsqrt(squares / (columns * dp) + EPS)
    for adapter in range(local):
        out_ref[adapter, 0] = result[adapter * MOST : (adapter + 1) * MOST]


def finish(values, squares, gain, shrink, arrived):
    local, rank, _ = shrink.shape
    return pl.pallas_call(
        finish_kernel,
        out_shape=jax.ShapeDtypeStruct((local, 1, MOST, rank), F32),
        in_specs=[whole()] * (4 + len(arrived)),
        out_specs=whole(),
        compiler_params=pltpu.CompilerParams(vmem_limit_bytes=8 * MIB),
        name="finish",
    )(values, squares, gain, shrink, *arrived)


def shifted(array, axis, shift):
    count = lax.axis_size(axis)
    return lax.ppermute(array, axis, [(i, (i + shift) % count) for i in range(count)])


def body(hidden, down_matrix, residual, next_norm_scale, shrink_matrix, adapter_index):
    dp, tensors, sections = (lax.axis_size(axis) for axis in ("dp", "tensor", "section"))
    depth, _ = down_matrix.shape
    local = shrink_matrix.shape[0]

    others = jnp.stack([shifted(hidden, "dp", shift) for shift in range(1, dp)])

    step = step_of(depth)
    blocks = depth // step
    held_count = max(1, min(blocks // 2, HELD_BYTES // (2 * step * down_matrix.shape[1])))
    held = fetch(down_matrix, held_count, step)

    shrink = jnp.swapaxes(shrink_matrix, 1, 2)
    gain = next_norm_scale[None, :]

    in_vmem = [pltpu.with_memory_space_constraint(x, pltpu.VMEM) for x in (hidden, others, held)]
    kept, sent = project(*in_vmem, down_matrix, tensors, sections)
    index, kept = lax.optimization_barrier((adapter_index.reshape(1, -1), kept))
    places = find_places(index, local * MOST, dp)
    arrived = [shifted(sent[s - 1], "section", s) for s in range(1, sections)]
    plan = exchange_plan(tensors)
    own, *sums = pair(kept, arrived, plan, tensors)
    arrived = [lax.ppermute(x, "tensor", list(sends.items())) for x, sends in zip(sums, plan)]
    mixed, routed, leaving = mix(residual, places, own, arrived, local * MOST, dp)
    arrived = [shifted(leaving[s - 1], "dp", s) for s in range(1, dp)]
    values, squares = own_half(routed, gain, shrink)
    shrunk = finish(values, squares, gain, shrink, arrived)
    return (mixed, shrunk)


def solution(mesh):
    placed = (
        P(("groups", "dp"), ("tensor", "section")),
        P(("tensor", "section"), "dp"),
        P(("groups", "tensor", "section"), "dp"),
        P(),
        P("dp", None, None),
        P(("groups", "tensor", "section"), None),
    )
    return jax.shard_map(
        body,
        mesh=mesh,
        in_specs=placed,
        out_specs=(
            P(("groups", "tensor", "section"), "dp"),
            P("dp", ("groups", "tensor", "section"), None, None),
        ),
        check_vma=False,
    )
```

```python
import functools

import jax
import jax.numpy as jnp
from jax import lax
from jax.experimental import pallas as pl
from jax.experimental.pallas import tpu as pltpu
from jax.sharding import PartitionSpec as P

MOST = 2
EPS = 1e-05
DEPTH_STEP = 512
HELD_BYTES = 21 * 2**20
WIDTH = 1024
MIB = 2**20
F32 = jnp.float32
BF16 = jnp.bfloat16


def whole():
    return pl.BlockSpec(memory_space=pltpu.VMEM)


def step_of(depth):
    return max(s for s in range(16, DEPTH_STEP + 1, 16) if depth % s == 0)


def fetch_kernel(weight_ref, held_ref, sems):
    count, step, _ = held_ref.shape
    copies = [
        pltpu.make_async_copy(
            weight_ref.at[pl.ds(i * step, step), :], held_ref.at[i], sems.at[i]
        )
        for i in range(count)
    ]
    for copy in copies:
        copy.start()
    for copy in copies:
        copy.wait()


def fetch(weight, count, step):
    columns = weight.shape[1]
    return pl.pallas_call(
        fetch_kernel,
        out_shape=pltpu.VMEM((count, step, columns), weight.dtype),
        in_specs=[pl.BlockSpec(memory_space=pl.ANY)],
        out_specs=whole(),
        scratch_shapes=[pltpu.SemaphoreType.DMA((count,))],
        compiler_params=pltpu.CompilerParams(vmem_limit_bytes=1 * MIB),
        cost_estimate=pl.CostEstimate(
            flops=0, bytes_accessed=2 * count * step * columns, transcendentals=0
        ),
        name="fetch",
    )(weight)


def project_kernel(
    own_ref,
    others_ref,
    held_ref,
    weight_ref,
    kept_ref,
    sent_ref,
    rows_ref,
    total_ref,
    rest_ref,
    sems,
    *,
    tensors,
    sections,
):
    held, step, columns = held_ref.shape
    rest = rest_ref.shape[0]
    own_rows = own_ref.shape[0]
    dp = 1 + others_ref.shape[0]
    me, tensor, section = (lax.axis_index(axis) for axis in ("dp", "tensor", "section"))
    width = min(columns, WIDTH)
    half = step // 2

    def copy_of(i, sem, first=0, size=step):
        return pltpu.make_async_copy(
            weight_ref.at[pl.ds((held + i) * step + first, size), :],
            rest_ref.at[i, pl.ds(first, size), :],
            sems.at[sem],
        )

    last = [copy_of(rest - 1, rest - 1, 0, half), copy_of(rest - 1, rest, half, half)]
    for i in range(rest - 1):
        copy_of(i, i).start()
    for copy in last:
        copy.start()

    for i in range(held + rest):
        block = slice(i * step, (i + 1) * step)
        for shift in range(dp):
            first = pl.multiple_of((me + dp - shift) % dp * own_rows, own_rows)
            source = own_ref[:, block] if shift == 0 else others_ref[shift - 1, :, block]
            rows_ref[i, pl.ds(first, own_rows), :] = source

    def held_step(n, _):
        lanes = pl.ds(pl.multiple_of(n * width, width), width)
        total_ref[:, lanes] = sum(
            jnp.dot(rows_ref[i], held_ref[i, :, lanes], preferred_element_type=F32)
            for i in range(held)
        )
        return 0

    def add(i, part=slice(None)):
        for n in range(0, columns, width):
            lanes = slice(n, n + width)
            total_ref[:, lanes] += jnp.dot(
                rows_ref[held + i, :, part], rest_ref[i, part, lanes], preferred_element_type=F32
            )

    def rest_step(i, _):
        copy_of(i, i).wait()
        add(i)
        return 0

    lax.fori_loop(0, columns // width, held_step, 0)
    lax.fori_loop(0, rest - 1, rest_step, 0)
    for copy, part in zip(last, (slice(0, half), slice(half, step))):
        copy.wait()
        add(rest - 1, part)

    block_rows = kept_ref.shape[0] // tensors
    group = sections * block_rows
    for n in range(0, columns, width):
        lanes = slice(n, n + width)
        turned = []
        for turn in range(tensors):
            first = pl.multiple_of(partner_of(tensor, turn, tensors) * group, group)
            rows = total_ref[pl.ds(first, group), lanes]
            turned.append(pltpu.roll(rows, (sections - section) % sections * block_rows, 0))
        for s in range(sections):
            part = slice(s * block_rows, (s + 1) * block_rows)
            rows = jnp.concatenate([block[part] for block in turned], axis=0)
            if s == 0:
                kept_ref[:, lanes] = rows
            else:
                sent_ref[s - 1, :, lanes] = rows.astype(BF16)


def project(own, others, held, weight, tensors, sections):
    own_rows, depth = own.shape
    rows = own_rows * (1 + others.shape[0])
    columns = weight.shape[1]
    count, step, _ = held.shape
    rest = depth // step - count
    return pl.pallas_call(
        functools.partial(project_kernel, tensors=tensors, sections=sections),
        out_shape=(
            pltpu.VMEM((rows // sections, columns), F32),
            pltpu.VMEM((sections - 1, rows // sections, columns), BF16),
        ),
        in_specs=[whole(), whole(), whole(), pl.BlockSpec(memory_space=pl.ANY)],
        out_specs=(whole(), whole()),
        scratch_shapes=[
            pltpu.VMEM((depth // step, rows, step), BF16),
            pltpu.VMEM((rows, columns), F32),
            pltpu.VMEM((rest, step, columns), BF16),
            pltpu.SemaphoreType.DMA((rest + 1,)),
        ],
        compiler_params=pltpu.CompilerParams(vmem_limit_bytes=36 * MIB),
        cost_estimate=pl.CostEstimate(
            flops=2 * rows * depth * columns,
            bytes_accessed=2 * rest * step * columns,
            transcendentals=0,
        ),
        name="project",
    )(own, others, held, weight)


def partner_of(me, turn, count):
    if count & (count - 1) == 0:
        return me ^ turn
    return (me + turn) % count


def turn_of(me, partner, count):
    if count & (count - 1) == 0:
        return me ^ partner
    return (partner - me) % count


def exchange_plan(count):
    if count == 4:
        return [(1, 3, 2, 0), (2, 1, 0, 3), (3, 0, 1, 2), (0, 2, 3, 1)]
    turns = range(count - 1, 0, -1)
    return [tuple(partner_of(i, turn, count) for i in range(count)) for turn in turns]


def pair_kernel(kept_ref, *refs, plan, tensors):
    arrived, (own_ref, *outs) = refs[: -1 - len(plan)], refs[-1 - len(plan) :]
    me = lax.axis_index("tensor")
    block_rows = own_ref.shape[0]
    total = kept_ref[...]
    for piece in arrived:
        total = total + piece[...].astype(F32)
    blocks = [total[turn * block_rows : (turn + 1) * block_rows] for turn in range(tensors)]
    own_ref[...] = blocks[0]
    blocks[0] = jnp.zeros_like(blocks[0])
    for receivers, out_ref in zip(plan, outs):
        turns = [turn_of(i, j, tensors) for i, j in enumerate(receivers)]
        block = blocks[turns[0]]
        for i, turn in enumerate(turns):
            if turn != turns[0]:
                block = jnp.where(me == i, blocks[turn], block)
        out_ref[...] = block.astype(out_ref.dtype)


def pair(kept, arrived, plan, tensors):
    rows, columns = kept.shape
    block = (rows // tensors, columns)
    return pl.pallas_call(
        functools.partial(pair_kernel, plan=plan, tensors=tensors),
        out_shape=[jax.ShapeDtypeStruct(block, F32)] + [jax.ShapeDtypeStruct(block, BF16)] * len(plan),
        in_specs=[whole()] * (1 + len(arrived)),
        out_specs=[whole()] * (1 + len(plan)),
        compiler_params=pltpu.CompilerParams(vmem_limit_bytes=8 * MIB),
        name="pair",
    )(kept, *arrived)


def places_of(row, slots, owners, local):
    rows = row.shape[1]
    upper = lax.broadcasted_iota(jnp.int32, (rows, rows), 0)
    lower = lax.broadcasted_iota(jnp.int32, (rows, rows), 1)
    column = jnp.sum(jnp.where(upper == lower, row, 0), axis=1, keepdims=True)
    before = jnp.logical_and(column == row, upper < lower)
    rank_of = jnp.sum(before.astype(jnp.int32), axis=0, keepdims=True)
    slot = lax.broadcasted_iota(jnp.int32, (slots * owners, rows), 0)
    owner = (lax.axis_index("dp") + slot // slots) % owners
    adapter = owner * local + slot // MOST % local
    return jnp.logical_and(row == adapter, rank_of == slot % MOST).astype(F32)


def places_kernel(index_ref, places_ref, *, slots, owners):
    places_ref[...] = places_of(index_ref[...], slots, owners, slots // MOST)


def find_places(index, slots, owners):
    return pl.pallas_call(
        functools.partial(places_kernel, slots=slots, owners=owners),
        out_shape=jax.ShapeDtypeStruct((slots * owners, index.shape[1]), F32),
        in_specs=[whole()],
        out_specs=whole(),
        compiler_params=pltpu.CompilerParams(vmem_limit_bytes=1 * MIB),
        name="find_places",
    )(index)


def mix_kernel(residual_ref, places_ref, own_ref, *refs):
    arrived, (mixed_ref, kept_ref, sent_ref) = refs[:-3], refs[-3:]
    slots = kept_ref.shape[0]
    places = places_ref[...]
    total = own_ref[...] + residual_ref[...].astype(F32)
    for piece in arrived:
        total = total + piece[...].astype(F32)
    mixed = total.astype(BF16)
    mixed_ref[...] = mixed
    widened = mixed.astype(F32)
    routed = sum(
        places[:, row : row + 1] * widened[row : row + 1, :] for row in range(widened.shape[0])
    )
    kept_ref[...] = routed[:slots]
    for turn in range(sent_ref.shape[0]):
        sent_ref[turn] = routed[(turn + 1) * slots : (turn + 2) * slots].astype(BF16)


def mix(residual, places, own, arrived, slots, owners):
    rows, columns = residual.shape
    return pl.pallas_call(
        mix_kernel,
        out_shape=(
            pltpu.VMEM((rows, columns), BF16),
            jax.ShapeDtypeStruct((slots, columns), F32),
            jax.ShapeDtypeStruct((owners - 1, slots, columns), BF16),
        ),
        in_specs=[whole()] * (3 + len(arrived)),
        out_specs=(whole(),) * 3,
        compiler_params=pltpu.CompilerParams(vmem_limit_bytes=8 * MIB),
        name="mix",
    )(residual, places, own, *arrived)


def partial_values(rows, gain_ref, shrink_ref, place, columns, local):
    first = pl.multiple_of(place * columns, columns)
    squares = jnp.sum(rows * rows, axis=1, keepdims=True)
    scaled = rows * gain_ref[:, pl.ds(first, columns)].astype(F32)
    high = scaled.astype(BF16)
    low = (scaled - high.astype(F32)).astype(BF16)
    values = []
    for adapter in range(local):
        mine = slice(adapter * MOST, (adapter + 1) * MOST)
        both = jnp.concatenate([high[mine], low[mine]], axis=0)
        product = lax.dot_general(
            both,
            shrink_ref[adapter, :, pl.ds(first, columns)],
            (((1,), (1,)), ((), ())),
            preferred_element_type=F32,
        )
        values.append(product[:MOST] + product[MOST:])
    return jnp.concatenate(values, axis=0), squares


def own_half_kernel(rows_ref, gain_ref, shrink_ref, values_ref, squares_ref):
    columns = rows_ref.shape[1]
    values, squares = partial_values(
        rows_ref[...], gain_ref, shrink_ref, lax.axis_index("dp"), columns, shrink_ref.shape[0]
    )
    values_ref[...] = values
    squares_ref[...] = jnp.broadcast_to(squares, squares_ref.shape)


def own_half(rows, gain, shrink):
    slots = rows.shape[0]
    rank = shrink.shape[1]
    return pl.pallas_call(
        own_half_kernel,
        out_shape=(
            jax.ShapeDtypeStruct((slots, rank), F32),
            jax.ShapeDtypeStruct((slots, rank), F32),
        ),
        in_specs=[whole()] * 3,
        out_specs=(whole(),) * 2,
        compiler_params=pltpu.CompilerParams(vmem_limit_bytes=8 * MIB),
        cost_estimate=pl.CostEstimate(
            flops=2 * slots * rows.shape[1] * rank, bytes_accessed=2 * MIB, transcendentals=0
        ),
        name="own_half",
    )(rows, gain, shrink)


def finish_kernel(values_ref, squares_ref, gain_ref, shrink_ref, *refs):
    arrived, out_ref = refs[:-1], refs[-1]
    dp = 1 + len(arrived)
    me = lax.axis_index("dp")
    local = shrink_ref.shape[0]
    columns = arrived[0].shape[1]
    values, squares = values_ref[...], squares_ref[:, :1]
    for shift, piece in enumerate(arrived, start=1):
        more, more_squares = partial_values(
            piece[...].astype(F32),
            gain_ref,
            shrink_ref,
            lax.rem(me + dp - shift, dp),
            columns,
            local,
        )
        values, squares = values + more, squares + more_squares
    result = 2.0 * values * lax.rsqrt(squares / (columns * dp) + EPS)
    for adapter in range(local):
        out_ref[adapter, 0] = result[adapter * MOST : (adapter + 1) * MOST]


def finish(values, squares, gain, shrink, arrived):
    local, rank, _ = shrink.shape
    return pl.pallas_call(
        finish_kernel,
        out_shape=jax.ShapeDtypeStruct((local, 1, MOST, rank), F32),
        in_specs=[whole()] * (4 + len(arrived)),
        out_specs=whole(),
        compiler_params=pltpu.CompilerParams(vmem_limit_bytes=8 * MIB),
        name="finish",
    )(values, squares, gain, shrink, *arrived)


def shifted(array, axis, shift):
    count = lax.axis_size(axis)
    return lax.ppermute(array, axis, [(i, (i + shift) % count) for i in range(count)])


def body(hidden, down_matrix, residual, next_norm_scale, shrink_matrix, adapter_index):
    dp, tensors, sections = (lax.axis_size(axis) for axis in ("dp", "tensor", "section"))
    depth, _ = down_matrix.shape
    local = shrink_matrix.shape[0]

    others = jnp.stack([shifted(hidden, "dp", shift) for shift in range(1, dp)])

    step = step_of(depth)
    blocks = depth // step
    held_count = max(1, min(blocks // 2, HELD_BYTES // (2 * step * down_matrix.shape[1])))
    held = fetch(down_matrix, held_count, step)

    shrink = jnp.swapaxes(shrink_matrix, 1, 2)
    gain = next_norm_scale[None, :]

    in_vmem = [pltpu.with_memory_space_constraint(x, pltpu.VMEM) for x in (hidden, others, held)]
    kept, sent = project(*in_vmem, down_matrix, tensors, sections)
    index, kept = lax.optimization_barrier((adapter_index.reshape(1, -1), kept))
    places = find_places(index, local * MOST, dp)
    arrived = [shifted(sent[s - 1], "section", s) for s in range(1, sections)]
    plan = exchange_plan(tensors)
    own, *sums = pair(kept, arrived, plan, tensors)
    arrived = [lax.ppermute(x, "tensor", list(enumerate(p))) for x, p in zip(sums, plan)]
    mixed, routed, leaving = mix(residual, places, own, arrived, local * MOST, dp)
    arrived = [shifted(leaving[s - 1], "dp", s) for s in range(1, dp)]
    values, squares = own_half(routed, gain, shrink)
    shrunk = finish(values, squares, gain, shrink, arrived)
    return (mixed, shrunk)


def solution(mesh):
    placed = (
        P(("groups", "dp"), ("tensor", "section")),
        P(("tensor", "section"), "dp"),
        P(("groups", "tensor", "section"), "dp"),
        P(),
        P("dp", None, None),
        P(("groups", "tensor", "section"), None),
    )
    return jax.shard_map(
        body,
        mesh=mesh,
        in_specs=placed,
        out_specs=(
            P(("groups", "tensor", "section"), "dp"),
            P("dp", ("groups", "tensor", "section"), None, None),
        ),
        check_vma=False,
    )
```

```python
import functools

import jax
import jax.numpy as jnp
from jax import lax
from jax.experimental import pallas as pl
from jax.experimental.pallas import tpu as pltpu
from jax.sharding import PartitionSpec as P

MOST = 2
EPS = 1e-05
DEPTH_STEP = 512
HELD_BYTES = 21 * 2**20
WIDTH = 1024
MIB = 2**20
F32 = jnp.float32
BF16 = jnp.bfloat16


def whole():
    return pl.BlockSpec(memory_space=pltpu.VMEM)


def step_of(depth):
    return max(s for s in range(16, DEPTH_STEP + 1, 16) if depth % s == 0)


def fetch_kernel(weight_ref, held_ref, sems):
    count, step, _ = held_ref.shape
    copies = [
        pltpu.make_async_copy(
            weight_ref.at[pl.ds(i * step, step), :], held_ref.at[i], sems.at[i]
        )
        for i in range(count)
    ]
    for copy in copies:
        copy.start()
    for copy in copies:
        copy.wait()


def fetch(weight, count, step):
    columns = weight.shape[1]
    return pl.pallas_call(
        fetch_kernel,
        out_shape=pltpu.VMEM((count, step, columns), weight.dtype),
        in_specs=[pl.BlockSpec(memory_space=pl.ANY)],
        out_specs=whole(),
        scratch_shapes=[pltpu.SemaphoreType.DMA((count,))],
        compiler_params=pltpu.CompilerParams(vmem_limit_bytes=1 * MIB),
        cost_estimate=pl.CostEstimate(
            flops=0, bytes_accessed=2 * count * step * columns, transcendentals=0
        ),
        name="fetch",
    )(weight)


def project_kernel(
    own_ref,
    others_ref,
    held_ref,
    weight_ref,
    kept_ref,
    sent_ref,
    rows_ref,
    total_ref,
    rest_ref,
    sems,
    *,
    tensors,
    sections,
):
    held, step, columns = held_ref.shape
    rest = rest_ref.shape[0]
    own_rows = own_ref.shape[0]
    dp = 1 + others_ref.shape[0]
    me, tensor, section = (lax.axis_index(axis) for axis in ("dp", "tensor", "section"))
    width = min(columns, WIDTH)
    half = step // 2

    def copy_of(i, sem, first=0, size=step):
        return pltpu.make_async_copy(
            weight_ref.at[pl.ds((held + i) * step + first, size), :],
            rest_ref.at[i, pl.ds(first, size), :],
            sems.at[sem],
        )

    last = [copy_of(rest - 1, rest - 1, 0, half), copy_of(rest - 1, rest, half, half)]
    for i in range(rest - 1):
        copy_of(i, i).start()
    for copy in last:
        copy.start()

    for i in range(held + rest):
        block = slice(i * step, (i + 1) * step)
        for shift in range(dp):
            first = pl.multiple_of((me + dp - shift) % dp * own_rows, own_rows)
            source = own_ref[:, block] if shift == 0 else others_ref[shift - 1, :, block]
            rows_ref[i, pl.ds(first, own_rows), :] = source

    def held_step(n, _):
        lanes = pl.ds(pl.multiple_of(n * width, width), width)
        total_ref[:, lanes] = sum(
            jnp.dot(rows_ref[i], held_ref[i, :, lanes], preferred_element_type=F32)
            for i in range(held)
        )
        return 0

    def add(i, part=slice(None)):
        for n in range(0, columns, width):
            lanes = slice(n, n + width)
            total_ref[:, lanes] += jnp.dot(
                rows_ref[held + i, :, part], rest_ref[i, part, lanes], preferred_element_type=F32
            )

    def rest_step(i, _):
        copy_of(i, i).wait()
        add(i)
        return 0

    lax.fori_loop(0, columns // width, held_step, 0)
    lax.fori_loop(0, rest - 1, rest_step, 0)
    for copy, part in zip(last, (slice(0, half), slice(half, step))):
        copy.wait()
        add(rest - 1, part)

    block_rows = kept_ref.shape[0] // tensors
    group = sections * block_rows
    for n in range(0, columns, width):
        lanes = slice(n, n + width)
        turned = []
        for turn in range(tensors):
            first = pl.multiple_of(partner_of(tensor, turn, tensors) * group, group)
            rows = total_ref[pl.ds(first, group), lanes]
            turned.append(pltpu.roll(rows, (sections - section) % sections * block_rows, 0))
        for s in range(sections):
            parts = [s] + [(s + 1) % sections] * (tensors - 1)
            rows = jnp.concatenate(
                [block[p * block_rows : (p + 1) * block_rows] for p, block in zip(parts, turned)],
                axis=0,
            )
            if s == 0:
                kept_ref[:, lanes] = rows
            else:
                sent_ref[s - 1, :, lanes] = rows.astype(BF16)


def project(own, others, held, weight, tensors, sections):
    own_rows, depth = own.shape
    rows = own_rows * (1 + others.shape[0])
    columns = weight.shape[1]
    count, step, _ = held.shape
    rest = depth // step - count
    return pl.pallas_call(
        functools.partial(project_kernel, tensors=tensors, sections=sections),
        out_shape=(
            pltpu.VMEM((rows // sections, columns), F32),
            pltpu.VMEM((sections - 1, rows // sections, columns), BF16),
        ),
        in_specs=[whole(), whole(), whole(), pl.BlockSpec(memory_space=pl.ANY)],
        out_specs=(whole(), whole()),
        scratch_shapes=[
            pltpu.VMEM((depth // step, rows, step), BF16),
            pltpu.VMEM((rows, columns), F32),
            pltpu.VMEM((rest, step, columns), BF16),
            pltpu.SemaphoreType.DMA((rest + 1,)),
        ],
        compiler_params=pltpu.CompilerParams(vmem_limit_bytes=36 * MIB),
        cost_estimate=pl.CostEstimate(
            flops=2 * rows * depth * columns,
            bytes_accessed=2 * rest * step * columns,
            transcendentals=0,
        ),
        name="project",
    )(own, others, held, weight)


def partner_of(me, turn, count):
    if count & (count - 1) == 0:
        return me ^ turn
    return (me + turn) % count


def turn_of(me, partner, count):
    if count & (count - 1) == 0:
        return me ^ partner
    return (partner - me) % count


def exchange_plan(count):
    if count == 4:
        return [(2, 3, 1, 0), (3, 2, 0, 1), (1, 0, 3, 2)]
    turns = range(count - 1, 0, -1)
    return [tuple(partner_of(i, turn, count) for i in range(count)) for turn in turns]


def pair_kernel(kept_ref, *refs, plan, tensors):
    arrived, (own_ref, *outs) = refs[: -1 - len(plan)], refs[-1 - len(plan) :]
    me = lax.axis_index("tensor")
    block_rows = own_ref.shape[0]
    total = kept_ref[...]
    for piece in arrived:
        total = total + piece[...].astype(F32)
    blocks = [total[turn * block_rows : (turn + 1) * block_rows] for turn in range(tensors)]
    own_ref[...] = blocks[0]
    for receivers, out_ref in zip(plan, outs):
        turns = [turn_of(i, j, tensors) for i, j in enumerate(receivers)]
        block = blocks[turns[0]]
        for i, turn in enumerate(turns):
            if turn != turns[0]:
                block = jnp.where(me == i, blocks[turn], block)
        out_ref[...] = block.astype(out_ref.dtype)


def pair(kept, arrived, plan, tensors):
    rows, columns = kept.shape
    block = (rows // tensors, columns)
    return pl.pallas_call(
        functools.partial(pair_kernel, plan=plan, tensors=tensors),
        out_shape=[jax.ShapeDtypeStruct(block, F32)] + [jax.ShapeDtypeStruct(block, BF16)] * len(plan),
        in_specs=[whole()] * (1 + len(arrived)),
        out_specs=[whole()] * (1 + len(plan)),
        compiler_params=pltpu.CompilerParams(vmem_limit_bytes=8 * MIB),
        name="pair",
    )(kept, *arrived)


def places_of(row, slots, owners, local):
    rows = row.shape[1]
    upper = lax.broadcasted_iota(jnp.int32, (rows, rows), 0)
    lower = lax.broadcasted_iota(jnp.int32, (rows, rows), 1)
    column = jnp.sum(jnp.where(upper == lower, row, 0), axis=1, keepdims=True)
    before = jnp.logical_and(column == row, upper < lower)
    rank_of = jnp.sum(before.astype(jnp.int32), axis=0, keepdims=True)
    slot = lax.broadcasted_iota(jnp.int32, (slots * owners, rows), 0)
    owner = (lax.axis_index("dp") + slot // slots) % owners
    adapter = owner * local + slot // MOST % local
    return jnp.logical_and(row == adapter, rank_of == slot % MOST).astype(F32)


def prepare_kernel(index_ref, shrink_ref, places_ref, out_ref, sem, *, slots, owners):
    copy = pltpu.make_async_copy(shrink_ref, out_ref, sem)
    copy.start()
    places_ref[...] = places_of(index_ref[...], slots, owners, slots // MOST)
    copy.wait()


def prepare(index, shrink, slots, owners):
    return pl.pallas_call(
        functools.partial(prepare_kernel, slots=slots, owners=owners),
        out_shape=(
            jax.ShapeDtypeStruct((slots * owners, index.shape[1]), F32),
            pltpu.VMEM(shrink.shape, shrink.dtype),
        ),
        in_specs=[whole(), pl.BlockSpec(memory_space=pl.ANY)],
        out_specs=(whole(), whole()),
        scratch_shapes=[pltpu.SemaphoreType.DMA],
        compiler_params=pltpu.CompilerParams(vmem_limit_bytes=1 * MIB),
        name="prepare",
    )(index, pltpu.with_memory_space_constraint(shrink, pltpu.HBM))


def mix_kernel(residual_ref, places_ref, own_ref, *refs):
    arrived, (mixed_ref, kept_ref, sent_ref) = refs[:-3], refs[-3:]
    slots = kept_ref.shape[0]
    places = places_ref[...]
    total = own_ref[...] + residual_ref[...].astype(F32)
    for piece in arrived:
        total = total + piece[...].astype(F32)
    mixed = total.astype(BF16)
    mixed_ref[...] = mixed
    widened = mixed.astype(F32)
    routed = sum(
        places[:, row : row + 1] * widened[row : row + 1, :] for row in range(widened.shape[0])
    )
    kept_ref[...] = routed[:slots]
    for turn in range(sent_ref.shape[0]):
        sent_ref[turn] = routed[(turn + 1) * slots : (turn + 2) * slots].astype(BF16)


def mix(residual, places, own, arrived, slots, owners):
    rows, columns = residual.shape
    return pl.pallas_call(
        mix_kernel,
        out_shape=(
            pltpu.VMEM((rows, columns), BF16),
            jax.ShapeDtypeStruct((slots, columns), F32),
            jax.ShapeDtypeStruct((owners - 1, slots, columns), BF16),
        ),
        in_specs=[whole()] * (3 + len(arrived)),
        out_specs=(whole(),) * 3,
        compiler_params=pltpu.CompilerParams(vmem_limit_bytes=8 * MIB),
        name="mix",
    )(residual, places, own, *arrived)


def partial_values(rows, gain_ref, shrink_ref, place, columns, local):
    first = pl.multiple_of(place * columns, columns)
    squares = jnp.sum(rows * rows, axis=1, keepdims=True)
    scaled = rows * gain_ref[:, pl.ds(first, columns)].astype(F32)
    high = scaled.astype(BF16)
    low = (scaled - high.astype(F32)).astype(BF16)
    values = []
    for adapter in range(local):
        mine = slice(adapter * MOST, (adapter + 1) * MOST)
        both = jnp.concatenate([high[mine], low[mine]], axis=0)
        product = lax.dot_general(
            both,
            shrink_ref[adapter, :, pl.ds(first, columns)],
            (((1,), (1,)), ((), ())),
            preferred_element_type=F32,
        )
        values.append(product[:MOST] + product[MOST:])
    return jnp.concatenate(values, axis=0), squares


def own_half_kernel(rows_ref, gain_ref, shrink_ref, values_ref, squares_ref):
    columns = rows_ref.shape[1]
    values, squares = partial_values(
        rows_ref[...], gain_ref, shrink_ref, lax.axis_index("dp"), columns, shrink_ref.shape[0]
    )
    values_ref[...] = values
    squares_ref[...] = jnp.broadcast_to(squares, squares_ref.shape)


def own_half(rows, gain, shrink):
    slots = rows.shape[0]
    rank = shrink.shape[1]
    return pl.pallas_call(
        own_half_kernel,
        out_shape=(
            jax.ShapeDtypeStruct((slots, rank), F32),
            jax.ShapeDtypeStruct((slots, rank), F32),
        ),
        in_specs=[whole()] * 3,
        out_specs=(whole(),) * 2,
        compiler_params=pltpu.CompilerParams(vmem_limit_bytes=8 * MIB),
        cost_estimate=pl.CostEstimate(
            flops=2 * slots * rows.shape[1] * rank, bytes_accessed=2 * MIB, transcendentals=0
        ),
        name="own_half",
    )(rows, gain, shrink)


def finish_kernel(values_ref, squares_ref, gain_ref, shrink_ref, *refs):
    arrived, out_ref = refs[:-1], refs[-1]
    dp = 1 + len(arrived)
    me = lax.axis_index("dp")
    local = shrink_ref.shape[0]
    columns = arrived[0].shape[1]
    values, squares = values_ref[...], squares_ref[:, :1]
    for shift, piece in enumerate(arrived, start=1):
        more, more_squares = partial_values(
            piece[...].astype(F32),
            gain_ref,
            shrink_ref,
            lax.rem(me + dp - shift, dp),
            columns,
            local,
        )
        values, squares = values + more, squares + more_squares
    result = 2.0 * values * lax.rsqrt(squares / (columns * dp) + EPS)
    for adapter in range(local):
        out_ref[adapter, 0] = result[adapter * MOST : (adapter + 1) * MOST]


def finish(values, squares, gain, shrink, arrived):
    local, rank, _ = shrink.shape
    return pl.pallas_call(
        finish_kernel,
        out_shape=jax.ShapeDtypeStruct((local, 1, MOST, rank), F32),
        in_specs=[whole()] * (4 + len(arrived)),
        out_specs=whole(),
        compiler_params=pltpu.CompilerParams(vmem_limit_bytes=8 * MIB),
        name="finish",
    )(values, squares, gain, shrink, *arrived)


def shifted(array, axis, shift):
    count = lax.axis_size(axis)
    return lax.ppermute(array, axis, [(i, (i + shift) % count) for i in range(count)])


def across(array, receivers):
    sections = lax.axis_size("section")
    pairs = [
        (i * sections + s, j * sections + (s + 1) % sections)
        for i, j in enumerate(receivers)
        for s in range(sections)
    ]
    return lax.ppermute(array, ("tensor", "section"), pairs)


def body(hidden, down_matrix, residual, next_norm_scale, shrink_matrix, adapter_index):
    dp, tensors, sections = (lax.axis_size(axis) for axis in ("dp", "tensor", "section"))
    depth, _ = down_matrix.shape
    local = shrink_matrix.shape[0]

    others = jnp.stack([shifted(hidden, "dp", shift) for shift in range(1, dp)])

    step = step_of(depth)
    blocks = depth // step
    held_count = max(1, min(blocks // 2, HELD_BYTES // (2 * step * down_matrix.shape[1])))
    held = fetch(down_matrix, held_count, step)

    shrink = jnp.swapaxes(shrink_matrix, 1, 2)
    gain = next_norm_scale[None, :]

    in_vmem = [pltpu.with_memory_space_constraint(x, pltpu.VMEM) for x in (hidden, others, held)]
    kept, sent = project(*in_vmem, down_matrix, tensors, sections)
    index, kept = lax.optimization_barrier((adapter_index.reshape(1, -1), kept))
    places, shrink = prepare(index, shrink, local * MOST, dp)
    arrived = [shifted(sent[s - 1], "section", s) for s in range(1, sections)]
    plan = exchange_plan(tensors)
    own, *sums = pair(kept, arrived, plan, tensors)
    arrived = [across(x, receivers) for x, receivers in zip(sums, plan)]
    mixed, routed, leaving = mix(residual, places, own, arrived, local * MOST, dp)
    arrived = [shifted(leaving[s - 1], "dp", s) for s in range(1, dp)]
    values, squares = own_half(routed, gain, shrink)
    shrunk = finish(values, squares, gain, shrink, arrived)
    return (mixed, shrunk)


def solution(mesh):
    placed = (
        P(("groups", "dp"), ("tensor", "section")),
        P(("tensor", "section"), "dp"),
        P(("groups", "tensor", "section"), "dp"),
        P(),
        P("dp", None, None),
        P(("groups", "tensor", "section"), None),
    )
    return jax.shard_map(
        body,
        mesh=mesh,
        in_specs=placed,
        out_specs=(
            P(("groups", "tensor", "section"), "dp"),
            P("dp", ("groups", "tensor", "section"), None, None),
        ),
        check_vma=False,
    )
```

```python
import functools

import jax
import jax.numpy as jnp
from jax import lax
from jax.experimental import pallas as pl
from jax.experimental.pallas import tpu as pltpu
from jax.sharding import PartitionSpec as P

MOST = 2
EPS = 1e-05
DEPTH_STEP = 512
HELD_BYTES = 21 * 2**20
WIDTH = 1024
MIB = 2**20
F32 = jnp.float32
BF16 = jnp.bfloat16


def whole():
    return pl.BlockSpec(memory_space=pltpu.VMEM)


def step_of(depth):
    return max(s for s in range(16, DEPTH_STEP + 1, 16) if depth % s == 0)


def fetch_kernel(weight_ref, held_ref, sems):
    count, step, _ = held_ref.shape
    parts = sems.shape[1]
    size = step // parts
    copies = [
        pltpu.make_async_copy(
            weight_ref.at[pl.ds(i * step + part * size, size), :],
            held_ref.at[i, pl.ds(part * size, size), :],
            sems.at[i, part],
        )
        for i in range(count)
        for part in range(parts)
    ]
    for copy in copies:
        copy.start()
    for copy in copies:
        copy.wait()


def fetch(weight, count, step):
    columns = weight.shape[1]
    return pl.pallas_call(
        fetch_kernel,
        out_shape=pltpu.VMEM((count, step, columns), weight.dtype),
        in_specs=[pl.BlockSpec(memory_space=pl.ANY)],
        out_specs=whole(),
        scratch_shapes=[pltpu.SemaphoreType.DMA((count, 4 if step % 64 == 0 else 1))],
        compiler_params=pltpu.CompilerParams(vmem_limit_bytes=1 * MIB),
        cost_estimate=pl.CostEstimate(
            flops=0, bytes_accessed=2 * count * step * columns, transcendentals=0
        ),
        name="fetch",
    )(weight)


def last_parts(step):
    if step % 64:
        return [(0, step)]
    return [(0, step // 2), (step // 2, step // 4), (step // 4 * 3, step // 4)]


def project_kernel(
    own_ref,
    others_ref,
    held_ref,
    weight_ref,
    kept_ref,
    sent_ref,
    rows_ref,
    total_ref,
    rest_ref,
    sems,
    *,
    tensors,
    sections,
):
    held, step, columns = held_ref.shape
    rest = rest_ref.shape[0]
    own_rows = own_ref.shape[0]
    dp = 1 + others_ref.shape[0]
    me, tensor, section = (lax.axis_index(axis) for axis in ("dp", "tensor", "section"))
    width = min(columns, WIDTH)

    def copy_of(i, sem, first=0, size=step):
        return pltpu.make_async_copy(
            weight_ref.at[pl.ds((held + i) * step + first, size), :],
            rest_ref.at[i, pl.ds(first, size), :],
            sems.at[sem],
        )

    parts = last_parts(step)
    last = [copy_of(rest - 1, rest - 1 + k, *part) for k, part in enumerate(parts)]
    for i in range(rest - 1):
        copy_of(i, i).start()
    for copy in last:
        copy.start()

    for i in range(held + rest):
        block = slice(i * step, (i + 1) * step)
        for shift in range(dp):
            first = pl.multiple_of((me + dp - shift) % dp * own_rows, own_rows)
            source = own_ref[:, block] if shift == 0 else others_ref[shift - 1, :, block]
            rows_ref[i, pl.ds(first, own_rows), :] = source

    def held_step(n, _):
        lanes = pl.ds(pl.multiple_of(n * width, width), width)
        total_ref[:, lanes] = sum(
            jnp.dot(rows_ref[i], held_ref[i, :, lanes], preferred_element_type=F32)
            for i in range(held)
        )
        return 0

    def add(i, part=slice(None)):
        for n in range(0, columns, width):
            lanes = slice(n, n + width)
            total_ref[:, lanes] += jnp.dot(
                rows_ref[held + i, :, part], rest_ref[i, part, lanes], preferred_element_type=F32
            )

    def rest_step(i, _):
        copy_of(i, i).wait()
        add(i)
        return 0

    lax.fori_loop(0, columns // width, held_step, 0)
    lax.fori_loop(0, rest - 1, rest_step, 0)
    for copy, (first, size) in zip(last, parts):
        copy.wait()
        add(rest - 1, slice(first, first + size))

    block_rows = kept_ref.shape[0] // tensors
    group = sections * block_rows
    for n in range(0, columns, width):
        lanes = slice(n, n + width)
        turned = []
        for turn in range(tensors):
            first = pl.multiple_of(partner_of(tensor, turn, tensors) * group, group)
            rows = total_ref[pl.ds(first, group), lanes]
            turned.append(pltpu.roll(rows, (sections - section) % sections * block_rows, 0))
        for s in range(sections):
            parts = [s] + [(s + 1) % sections] * (tensors - 1)
            rows = jnp.concatenate(
                [block[p * block_rows : (p + 1) * block_rows] for p, block in zip(parts, turned)],
                axis=0,
            )
            if s == 0:
                kept_ref[:, lanes] = rows
            else:
                sent_ref[s - 1, :, lanes] = rows.astype(BF16)


def project(own, others, held, weight, tensors, sections):
    own_rows, depth = own.shape
    rows = own_rows * (1 + others.shape[0])
    columns = weight.shape[1]
    count, step, _ = held.shape
    rest = depth // step - count
    return pl.pallas_call(
        functools.partial(project_kernel, tensors=tensors, sections=sections),
        out_shape=(
            pltpu.VMEM((rows // sections, columns), F32),
            pltpu.VMEM((sections - 1, rows // sections, columns), BF16),
        ),
        in_specs=[whole(), whole(), whole(), pl.BlockSpec(memory_space=pl.ANY)],
        out_specs=(whole(), whole()),
        scratch_shapes=[
            pltpu.VMEM((depth // step, rows, step), BF16),
            pltpu.VMEM((rows, columns), F32),
            pltpu.VMEM((rest, step, columns), BF16),
            pltpu.SemaphoreType.DMA((rest - 1 + len(last_parts(step)),)),
        ],
        compiler_params=pltpu.CompilerParams(vmem_limit_bytes=36 * MIB),
        cost_estimate=pl.CostEstimate(
            flops=2 * rows * depth * columns,
            bytes_accessed=2 * rest * step * columns,
            transcendentals=0,
        ),
        name="project",
    )(own, others, held, weight)


def partner_of(me, turn, count):
    if count & (count - 1) == 0:
        return me ^ turn
    return (me + turn) % count


def turn_of(me, partner, count):
    if count & (count - 1) == 0:
        return me ^ partner
    return (partner - me) % count


def exchange_plan(count):
    if count == 4:
        return [(2, 3, 1, 0), (3, 2, 0, 1), (1, 0, 3, 2)]
    turns = range(count - 1, 0, -1)
    return [tuple(partner_of(i, turn, count) for i in range(count)) for turn in turns]


def pair_kernel(kept_ref, *refs, plan, tensors):
    arrived, (own_ref, *outs) = refs[: -1 - len(plan)], refs[-1 - len(plan) :]
    me = lax.axis_index("tensor")
    block_rows = own_ref.shape[0]
    total = kept_ref[...]
    for piece in arrived:
        total = total + piece[...].astype(F32)
    blocks = [total[turn * block_rows : (turn + 1) * block_rows] for turn in range(tensors)]
    own_ref[...] = blocks[0]
    for receivers, out_ref in zip(plan, outs):
        turns = [turn_of(i, j, tensors) for i, j in enumerate(receivers)]
        block = blocks[turns[0]]
        for i, turn in enumerate(turns):
            if turn != turns[0]:
                block = jnp.where(me == i, blocks[turn], block)
        out_ref[...] = block.astype(out_ref.dtype)


def pair(kept, arrived, plan, tensors):
    rows, columns = kept.shape
    block = (rows // tensors, columns)
    return pl.pallas_call(
        functools.partial(pair_kernel, plan=plan, tensors=tensors),
        out_shape=[jax.ShapeDtypeStruct(block, F32)] + [jax.ShapeDtypeStruct(block, BF16)] * len(plan),
        in_specs=[whole()] * (1 + len(arrived)),
        out_specs=[whole()] * (1 + len(plan)),
        compiler_params=pltpu.CompilerParams(vmem_limit_bytes=8 * MIB),
        name="pair",
    )(kept, *arrived)


def places_of(row, slots, owners, local):
    rows = row.shape[1]
    upper = lax.broadcasted_iota(jnp.int32, (rows, rows), 0)
    lower = lax.broadcasted_iota(jnp.int32, (rows, rows), 1)
    column = jnp.sum(jnp.where(upper == lower, row, 0), axis=1, keepdims=True)
    before = jnp.logical_and(column == row, upper < lower)
    rank_of = jnp.sum(before.astype(jnp.int32), axis=0, keepdims=True)
    slot = lax.broadcasted_iota(jnp.int32, (slots * owners, rows), 0)
    owner = (lax.axis_index("dp") + slot // slots) % owners
    adapter = owner * local + slot // MOST % local
    return jnp.logical_and(row == adapter, rank_of == slot % MOST).astype(F32)


def prepare_kernel(index_ref, shrink_ref, places_ref, out_ref, sem, *, slots, owners):
    copy = pltpu.make_async_copy(shrink_ref, out_ref, sem)
    copy.start()
    places_ref[...] = places_of(index_ref[...], slots, owners, slots // MOST)
    copy.wait()


def prepare(index, shrink, slots, owners):
    return pl.pallas_call(
        functools.partial(prepare_kernel, slots=slots, owners=owners),
        out_shape=(
            jax.ShapeDtypeStruct((slots * owners, index.shape[1]), F32),
            pltpu.VMEM(shrink.shape, shrink.dtype),
        ),
        in_specs=[whole(), pl.BlockSpec(memory_space=pl.ANY)],
        out_specs=(whole(), whole()),
        scratch_shapes=[pltpu.SemaphoreType.DMA],
        compiler_params=pltpu.CompilerParams(vmem_limit_bytes=1 * MIB),
        name="prepare",
    )(index, pltpu.with_memory_space_constraint(shrink, pltpu.HBM))


def mix_kernel(residual_ref, places_ref, own_ref, *refs):
    arrived, (mixed_ref, kept_ref, sent_ref) = refs[:-3], refs[-3:]
    slots = kept_ref.shape[0]
    places = places_ref[...]
    total = own_ref[...] + residual_ref[...].astype(F32)
    for piece in arrived:
        total = total + piece[...].astype(F32)
    mixed = total.astype(BF16)
    mixed_ref[...] = mixed
    widened = mixed.astype(F32)
    routed = sum(
        places[:, row : row + 1] * widened[row : row + 1, :] for row in range(widened.shape[0])
    )
    kept_ref[...] = routed[:slots]
    for turn in range(sent_ref.shape[0]):
        sent_ref[turn] = routed[(turn + 1) * slots : (turn + 2) * slots].astype(BF16)


def mix(residual, places, own, arrived, slots, owners):
    rows, columns = residual.shape
    return pl.pallas_call(
        mix_kernel,
        out_shape=(
            pltpu.VMEM((rows, columns), BF16),
            jax.ShapeDtypeStruct((slots, columns), F32),
            jax.ShapeDtypeStruct((owners - 1, slots, columns), BF16),
        ),
        in_specs=[whole()] * (3 + len(arrived)),
        out_specs=(whole(),) * 3,
        compiler_params=pltpu.CompilerParams(vmem_limit_bytes=8 * MIB),
        name="mix",
    )(residual, places, own, *arrived)


def partial_values(rows, gain_ref, shrink_ref, place, columns, local):
    first = pl.multiple_of(place * columns, columns)
    squares = jnp.sum(rows * rows, axis=1, keepdims=True)
    scaled = rows * gain_ref[:, pl.ds(first, columns)].astype(F32)
    high = scaled.astype(BF16)
    low = (scaled - high.astype(F32)).astype(BF16)
    values = []
    for adapter in range(local):
        mine = slice(adapter * MOST, (adapter + 1) * MOST)
        both = jnp.concatenate([high[mine], low[mine]], axis=0)
        product = lax.dot_general(
            both,
            shrink_ref[adapter, :, pl.ds(first, columns)],
            (((1,), (1,)), ((), ())),
            preferred_element_type=F32,
        )
        values.append(product[:MOST] + product[MOST:])
    return jnp.concatenate(values, axis=0), squares


def own_half_kernel(rows_ref, gain_ref, shrink_ref, values_ref, squares_ref):
    columns = rows_ref.shape[1]
    values, squares = partial_values(
        rows_ref[...], gain_ref, shrink_ref, lax.axis_index("dp"), columns, shrink_ref.shape[0]
    )
    values_ref[...] = values
    squares_ref[...] = jnp.broadcast_to(squares, squares_ref.shape)


def own_half(rows, gain, shrink):
    slots = rows.shape[0]
    rank = shrink.shape[1]
    return pl.pallas_call(
        own_half_kernel,
        out_shape=(
            jax.ShapeDtypeStruct((slots, rank), F32),
            jax.ShapeDtypeStruct((slots, rank), F32),
        ),
        in_specs=[whole()] * 3,
        out_specs=(whole(),) * 2,
        compiler_params=pltpu.CompilerParams(vmem_limit_bytes=8 * MIB),
        cost_estimate=pl.CostEstimate(
            flops=2 * slots * rows.shape[1] * rank, bytes_accessed=2 * MIB, transcendentals=0
        ),
        name="own_half",
    )(rows, gain, shrink)


def finish_kernel(values_ref, squares_ref, gain_ref, shrink_ref, *refs):
    arrived, out_ref = refs[:-1], refs[-1]
    dp = 1 + len(arrived)
    me = lax.axis_index("dp")
    local = shrink_ref.shape[0]
    columns = arrived[0].shape[1]
    values, squares = values_ref[...], squares_ref[:, :1]
    for shift, piece in enumerate(arrived, start=1):
        more, more_squares = partial_values(
            piece[...].astype(F32),
            gain_ref,
            shrink_ref,
            lax.rem(me + dp - shift, dp),
            columns,
            local,
        )
        values, squares = values + more, squares + more_squares
    result = 2.0 * values * lax.rsqrt(squares / (columns * dp) + EPS)
    for adapter in range(local):
        out_ref[adapter, 0] = result[adapter * MOST : (adapter + 1) * MOST]


def finish(values, squares, gain, shrink, arrived):
    local, rank, _ = shrink.shape
    return pl.pallas_call(
        finish_kernel,
        out_shape=jax.ShapeDtypeStruct((local, 1, MOST, rank), F32),
        in_specs=[whole()] * (4 + len(arrived)),
        out_specs=whole(),
        compiler_params=pltpu.CompilerParams(vmem_limit_bytes=8 * MIB),
        name="finish",
    )(values, squares, gain, shrink, *arrived)


def shifted(array, axis, shift):
    count = lax.axis_size(axis)
    return lax.ppermute(array, axis, [(i, (i + shift) % count) for i in range(count)])


def across(array, receivers):
    sections = lax.axis_size("section")
    pairs = [
        (i * sections + s, j * sections + (s + 1) % sections)
        for i, j in enumerate(receivers)
        for s in range(sections)
    ]
    return lax.ppermute(array, ("tensor", "section"), pairs)


def body(hidden, down_matrix, residual, next_norm_scale, shrink_matrix, adapter_index):
    dp, tensors, sections = (lax.axis_size(axis) for axis in ("dp", "tensor", "section"))
    depth, _ = down_matrix.shape
    local = shrink_matrix.shape[0]

    others = jnp.stack([shifted(hidden, "dp", shift) for shift in range(1, dp)])

    step = step_of(depth)
    blocks = depth // step
    held_count = max(1, min(blocks // 2, HELD_BYTES // (2 * step * down_matrix.shape[1])))
    held = fetch(down_matrix, held_count, step)

    shrink = jnp.swapaxes(shrink_matrix, 1, 2)
    gain = next_norm_scale[None, :]

    in_vmem = [pltpu.with_memory_space_constraint(x, pltpu.VMEM) for x in (hidden, others, held)]
    kept, sent = project(*in_vmem, down_matrix, tensors, sections)
    index, kept = lax.optimization_barrier((adapter_index.reshape(1, -1), kept))
    places, shrink = prepare(index, shrink, local * MOST, dp)
    arrived = [shifted(sent[s - 1], "section", s) for s in range(1, sections)]
    plan = exchange_plan(tensors)
    own, *sums = pair(kept, arrived, plan, tensors)
    arrived = [across(x, receivers) for x, receivers in zip(sums, plan)]
    mixed, routed, leaving = mix(residual, places, own, arrived, local * MOST, dp)
    arrived = [shifted(leaving[s - 1], "dp", s) for s in range(1, dp)]
    values, squares = own_half(routed, gain, shrink)
    shrunk = finish(values, squares, gain, shrink, arrived)
    return (mixed, shrunk)


def solution(mesh):
    placed = (
        P(("groups", "dp"), ("tensor", "section")),
        P(("tensor", "section"), "dp"),
        P(("groups", "tensor", "section"), "dp"),
        P(),
        P("dp", None, None),
        P(("groups", "tensor", "section"), None),
    )
    return jax.shard_map(
        body,
        mesh=mesh,
        in_specs=placed,
        out_specs=(
            P(("groups", "tensor", "section"), "dp"),
            P("dp", ("groups", "tensor", "section"), None, None),
        ),
        check_vma=False,
    )
```

```python
import functools

import jax
import jax.numpy as jnp
from jax import lax
from jax.experimental import pallas as pl
from jax.experimental.pallas import tpu as pltpu
from jax.sharding import PartitionSpec as P

MOST = 2
EPS = 1e-05
DEPTH_STEP = 512
HELD_BYTES = 21 * 2**20
WIDTH = 1024
MIB = 2**20
F32 = jnp.float32
BF16 = jnp.bfloat16


def whole():
    return pl.BlockSpec(memory_space=pltpu.VMEM)


def step_of(depth):
    return max(s for s in range(16, DEPTH_STEP + 1, 16) if depth % s == 0)


def fetch_kernel(weight_ref, held_ref, sems):
    count, step, _ = held_ref.shape
    copies = [
        pltpu.make_async_copy(
            weight_ref.at[pl.ds(i * step, step), :], held_ref.at[i], sems.at[i]
        )
        for i in range(count)
    ]
    for copy in copies:
        copy.start()
    for copy in copies:
        copy.wait()


def fetch(weight, count, step):
    columns = weight.shape[1]
    return pl.pallas_call(
        fetch_kernel,
        out_shape=pltpu.VMEM((count, step, columns), weight.dtype),
        in_specs=[pl.BlockSpec(memory_space=pl.ANY)],
        out_specs=whole(),
        scratch_shapes=[pltpu.SemaphoreType.DMA((count,))],
        compiler_params=pltpu.CompilerParams(vmem_limit_bytes=1 * MIB),
        cost_estimate=pl.CostEstimate(
            flops=0, bytes_accessed=2 * count * step * columns, transcendentals=0
        ),
        name="fetch",
    )(weight)


def last_parts(step):
    if step % 64:
        return [(0, step)]
    return [(0, step // 2), (step // 2, step // 4), (step // 4 * 3, step // 4)]


def project_kernel(
    own_ref,
    others_ref,
    held_ref,
    weight_ref,
    total_ref,
    sent_ref,
    rows_ref,
    rest_ref,
    sems,
    *,
    tensors,
    sections,
):
    held, step, columns = held_ref.shape
    rest = rest_ref.shape[0]
    own_rows = own_ref.shape[0]
    dp = 1 + others_ref.shape[0]
    me = lax.axis_index("dp")
    width = min(columns, WIDTH)

    def copy_of(i, sem, first=0, size=step):
        return pltpu.make_async_copy(
            weight_ref.at[pl.ds((held + i) * step + first, size), :],
            rest_ref.at[i, pl.ds(first, size), :],
            sems.at[sem],
        )

    parts = last_parts(step)
    last = [copy_of(rest - 1, rest - 1 + k, *part) for k, part in enumerate(parts)]
    for i in range(rest - 1):
        copy_of(i, i).start()
    for copy in last:
        copy.start()

    for i in range(held + rest):
        block = slice(i * step, (i + 1) * step)
        for shift in range(dp):
            first = pl.multiple_of((me + dp - shift) % dp * own_rows, own_rows)
            source = own_ref[:, block] if shift == 0 else others_ref[shift - 1, :, block]
            rows_ref[i, pl.ds(first, own_rows), :] = source

    def add(i, part=slice(None)):
        for n in range(0, columns, width):
            lanes = slice(n, n + width)
            total_ref[:, lanes] += jnp.dot(
                rows_ref[held + i, :, part], rest_ref[i, part, lanes], preferred_element_type=F32
            )

    def rest_step(i, _):
        copy_of(i, i).wait()
        add(i)
        return 0

    for n in range(0, columns, width):
        lanes = slice(n, n + width)
        total_ref[:, lanes] = sum(
            jnp.dot(rows_ref[i], held_ref[i, :, lanes], preferred_element_type=F32)
            for i in range(held)
        )
    lax.fori_loop(0, rest - 1, rest_step, 0)
    for copy, (first, size) in zip(last, parts):
        copy.wait()
        add(rest - 1, slice(first, first + size))

    for turn in range(1, sections):
        for n in range(0, columns, width):
            lanes = slice(n, n + width)
            rows = rows_of(turn, total_ref, lanes, tensors, sections)
            sent_ref[turn - 1, :, lanes] = rows.astype(BF16)


def rows_of(turn, total_ref, lanes, tensors, sections):
    tensor, section = lax.axis_index("tensor"), lax.axis_index("section")
    block_rows = total_ref.shape[0] // (tensors * sections)
    group = sections * block_rows
    blocks = []
    for k in range(tensors):
        first = pl.multiple_of(partner_of(tensor, k, tensors) * group, group)
        rows = total_ref[pl.ds(first, group), lanes]
        rows = pltpu.roll(rows, (sections - section) % sections * block_rows, 0)
        part = (turn + (k > 0)) % sections
        blocks.append(rows[part * block_rows : (part + 1) * block_rows])
    return jnp.concatenate(blocks, axis=0)


def keep_kernel(total_ref, kept_ref, *, tensors, sections):
    columns = total_ref.shape[1]
    width = min(columns, WIDTH)
    for n in range(0, columns, width):
        lanes = slice(n, n + width)
        kept_ref[:, lanes] = rows_of(0, total_ref, lanes, tensors, sections)


def keep(total, tensors, sections):
    rows, columns = total.shape
    return pl.pallas_call(
        functools.partial(keep_kernel, tensors=tensors, sections=sections),
        out_shape=jax.ShapeDtypeStruct((rows // sections, columns), F32),
        in_specs=[whole()],
        out_specs=whole(),
        compiler_params=pltpu.CompilerParams(vmem_limit_bytes=4 * MIB),
        name="keep",
    )(total)


def project(own, others, held, weight, tensors, sections):
    own_rows, depth = own.shape
    rows = own_rows * (1 + others.shape[0])
    columns = weight.shape[1]
    count, step, _ = held.shape
    rest = depth // step - count
    return pl.pallas_call(
        functools.partial(project_kernel, tensors=tensors, sections=sections),
        out_shape=(
            pltpu.VMEM((rows, columns), F32),
            pltpu.VMEM((sections - 1, rows // sections, columns), BF16),
        ),
        in_specs=[whole(), whole(), whole(), pl.BlockSpec(memory_space=pl.ANY)],
        out_specs=(whole(), whole()),
        scratch_shapes=[
            pltpu.VMEM((depth // step, rows, step), BF16),
            pltpu.VMEM((rest, step, columns), BF16),
            pltpu.SemaphoreType.DMA((rest - 1 + len(last_parts(step)),)),
        ],
        compiler_params=pltpu.CompilerParams(vmem_limit_bytes=36 * MIB),
        cost_estimate=pl.CostEstimate(
            flops=2 * rows * depth * columns,
            bytes_accessed=2 * rest * step * columns,
            transcendentals=0,
        ),
        name="project",
    )(own, others, held, weight)


def partner_of(me, turn, count):
    if count & (count - 1) == 0:
        return me ^ turn
    return (me + turn) % count


def turn_of(me, partner, count):
    if count & (count - 1) == 0:
        return me ^ partner
    return (partner - me) % count


def exchange_plan(count):
    if count == 4:
        return [(2, 3, 1, 0), (3, 2, 0, 1), (1, 0, 3, 2)]
    turns = range(count - 1, 0, -1)
    return [tuple(partner_of(i, turn, count) for i in range(count)) for turn in turns]


def pair_kernel(kept_ref, *refs, plan, tensors):
    arrived, (own_ref, *outs) = refs[: -1 - len(plan)], refs[-1 - len(plan) :]
    me = lax.axis_index("tensor")
    block_rows = own_ref.shape[0]
    total = kept_ref[...]
    for piece in arrived:
        total = total + piece[...].astype(F32)
    blocks = [total[turn * block_rows : (turn + 1) * block_rows] for turn in range(tensors)]
    own_ref[...] = blocks[0]
    for receivers, out_ref in zip(plan, outs):
        turns = [turn_of(i, j, tensors) for i, j in enumerate(receivers)]
        block = blocks[turns[0]]
        for i, turn in enumerate(turns):
            if turn != turns[0]:
                block = jnp.where(me == i, blocks[turn], block)
        out_ref[...] = block.astype(out_ref.dtype)


def pair(kept, arrived, plan, tensors):
    rows, columns = kept.shape
    block = (rows // tensors, columns)
    return pl.pallas_call(
        functools.partial(pair_kernel, plan=plan, tensors=tensors),
        out_shape=[jax.ShapeDtypeStruct(block, F32)] + [jax.ShapeDtypeStruct(block, BF16)] * len(plan),
        in_specs=[whole()] * (1 + len(arrived)),
        out_specs=[whole()] * (1 + len(plan)),
        compiler_params=pltpu.CompilerParams(vmem_limit_bytes=8 * MIB),
        name="pair",
    )(kept, *arrived)


def places_of(row, slots, owners, local):
    rows = row.shape[1]
    upper = lax.broadcasted_iota(jnp.int32, (rows, rows), 0)
    lower = lax.broadcasted_iota(jnp.int32, (rows, rows), 1)
    column = jnp.sum(jnp.where(upper == lower, row, 0), axis=1, keepdims=True)
    before = jnp.logical_and(column == row, upper < lower)
    rank_of = jnp.sum(before.astype(jnp.int32), axis=0, keepdims=True)
    slot = lax.broadcasted_iota(jnp.int32, (slots * owners, rows), 0)
    owner = (lax.axis_index("dp") + slot // slots) % owners
    adapter = owner * local + slot // MOST % local
    return jnp.logical_and(row == adapter, rank_of == slot % MOST).astype(F32)


def prepare_kernel(index_ref, shrink_ref, places_ref, out_ref, sem, *, slots, owners):
    copy = pltpu.make_async_copy(shrink_ref, out_ref, sem)
    copy.start()
    places_ref[...] = places_of(index_ref[...], slots, owners, slots // MOST)
    copy.wait()


def prepare(index, shrink, slots, owners):
    return pl.pallas_call(
        functools.partial(prepare_kernel, slots=slots, owners=owners),
        out_shape=(
            jax.ShapeDtypeStruct((slots * owners, index.shape[1]), F32),
            pltpu.VMEM(shrink.shape, shrink.dtype),
        ),
        in_specs=[whole(), pl.BlockSpec(memory_space=pl.ANY)],
        out_specs=(whole(), whole()),
        scratch_shapes=[pltpu.SemaphoreType.DMA],
        compiler_params=pltpu.CompilerParams(vmem_limit_bytes=1 * MIB),
        name="prepare",
    )(index, pltpu.with_memory_space_constraint(shrink, pltpu.HBM))


def mix_kernel(residual_ref, places_ref, own_ref, *refs):
    arrived, (mixed_ref, kept_ref, sent_ref) = refs[:-3], refs[-3:]
    slots = kept_ref.shape[0]
    places = places_ref[...]
    total = own_ref[...] + residual_ref[...].astype(F32)
    for piece in arrived:
        total = total + piece[...].astype(F32)
    mixed = total.astype(BF16)
    mixed_ref[...] = mixed
    widened = mixed.astype(F32)
    routed = sum(
        places[:, row : row + 1] * widened[row : row + 1, :] for row in range(widened.shape[0])
    )
    kept_ref[...] = routed[:slots]
    for turn in range(sent_ref.shape[0]):
        sent_ref[turn] = routed[(turn + 1) * slots : (turn + 2) * slots].astype(BF16)


def mix(residual, places, own, arrived, slots, owners):
    rows, columns = residual.shape
    return pl.pallas_call(
        mix_kernel,
        out_shape=(
            pltpu.VMEM((rows, columns), BF16),
            jax.ShapeDtypeStruct((slots, columns), F32),
            jax.ShapeDtypeStruct((owners - 1, slots, columns), BF16),
        ),
        in_specs=[whole()] * (3 + len(arrived)),
        out_specs=(whole(),) * 3,
        compiler_params=pltpu.CompilerParams(vmem_limit_bytes=8 * MIB),
        name="mix",
    )(residual, places, own, *arrived)


def partial_values(rows, gain_ref, shrink_ref, place, columns, local):
    first = pl.multiple_of(place * columns, columns)
    squares = jnp.sum(rows * rows, axis=1, keepdims=True)
    scaled = rows * gain_ref[:, pl.ds(first, columns)].astype(F32)
    high = scaled.astype(BF16)
    low = (scaled - high.astype(F32)).astype(BF16)
    values = []
    for adapter in range(local):
        mine = slice(adapter * MOST, (adapter + 1) * MOST)
        both = jnp.concatenate([high[mine], low[mine]], axis=0)
        product = lax.dot_general(
            both,
            shrink_ref[adapter, :, pl.ds(first, columns)],
            (((1,), (1,)), ((), ())),
            preferred_element_type=F32,
        )
        values.append(product[:MOST] + product[MOST:])
    return jnp.concatenate(values, axis=0), squares


def own_half_kernel(rows_ref, gain_ref, shrink_ref, values_ref, squares_ref):
    columns = rows_ref.shape[1]
    values, squares = partial_values(
        rows_ref[...], gain_ref, shrink_ref, lax.axis_index("dp"), columns, shrink_ref.shape[0]
    )
    values_ref[...] = values
    squares_ref[...] = jnp.broadcast_to(squares, squares_ref.shape)


def own_half(rows, gain, shrink):
    slots = rows.shape[0]
    rank = shrink.shape[1]
    return pl.pallas_call(
        own_half_kernel,
        out_shape=(
            jax.ShapeDtypeStruct((slots, rank), F32),
            jax.ShapeDtypeStruct((slots, rank), F32),
        ),
        in_specs=[whole()] * 3,
        out_specs=(whole(),) * 2,
        compiler_params=pltpu.CompilerParams(vmem_limit_bytes=8 * MIB),
        cost_estimate=pl.CostEstimate(
            flops=2 * slots * rows.shape[1] * rank, bytes_accessed=2 * MIB, transcendentals=0
        ),
        name="own_half",
    )(rows, gain, shrink)


def finish_kernel(values_ref, squares_ref, gain_ref, shrink_ref, *refs):
    arrived, out_ref = refs[:-1], refs[-1]
    dp = 1 + len(arrived)
    me = lax.axis_index("dp")
    local = shrink_ref.shape[0]
    columns = arrived[0].shape[1]
    values, squares = values_ref[...], squares_ref[:, :1]
    for shift, piece in enumerate(arrived, start=1):
        more, more_squares = partial_values(
            piece[...].astype(F32),
            gain_ref,
            shrink_ref,
            lax.rem(me + dp - shift, dp),
            columns,
            local,
        )
        values, squares = values + more, squares + more_squares
    result = 2.0 * values * lax.rsqrt(squares / (columns * dp) + EPS)
    for adapter in range(local):
        out_ref[adapter, 0] = result[adapter * MOST : (adapter + 1) * MOST]


def finish(values, squares, gain, shrink, arrived):
    local, rank, _ = shrink.shape
    return pl.pallas_call(
        finish_kernel,
        out_shape=jax.ShapeDtypeStruct((local, 1, MOST, rank), F32),
        in_specs=[whole()] * (4 + len(arrived)),
        out_specs=whole(),
        compiler_params=pltpu.CompilerParams(vmem_limit_bytes=8 * MIB),
        name="finish",
    )(values, squares, gain, shrink, *arrived)


def shifted(array, axis, shift):
    count = lax.axis_size(axis)
    return lax.ppermute(array, axis, [(i, (i + shift) % count) for i in range(count)])


def across(array, receivers):
    sections = lax.axis_size("section")
    pairs = [
        (i * sections + s, j * sections + (s + 1) % sections)
        for i, j in enumerate(receivers)
        for s in range(sections)
    ]
    return lax.ppermute(array, ("tensor", "section"), pairs)


def body(hidden, down_matrix, residual, next_norm_scale, shrink_matrix, adapter_index):
    dp, tensors, sections = (lax.axis_size(axis) for axis in ("dp", "tensor", "section"))
    depth, _ = down_matrix.shape
    local = shrink_matrix.shape[0]

    others = jnp.stack([shifted(hidden, "dp", shift) for shift in range(1, dp)])

    step = step_of(depth)
    blocks = depth // step
    held_count = max(1, min(blocks // 2, HELD_BYTES // (2 * step * down_matrix.shape[1])))
    held = fetch(down_matrix, held_count, step)

    shrink = jnp.swapaxes(shrink_matrix, 1, 2)
    gain = next_norm_scale[None, :]

    in_vmem = [pltpu.with_memory_space_constraint(x, pltpu.VMEM) for x in (hidden, others, held)]
    total, sent = project(*in_vmem, down_matrix, tensors, sections)
    index, total = lax.optimization_barrier((adapter_index.reshape(1, -1), total))
    kept = keep(total, tensors, sections)
    places, shrink = prepare(index, shrink, local * MOST, dp)
    arrived = [shifted(sent[s - 1], "section", s) for s in range(1, sections)]
    plan = exchange_plan(tensors)
    own, *sums = pair(kept, arrived, plan, tensors)
    arrived = [across(x, receivers) for x, receivers in zip(sums, plan)]
    mixed, routed, leaving = mix(residual, places, own, arrived, local * MOST, dp)
    arrived = [shifted(leaving[s - 1], "dp", s) for s in range(1, dp)]
    values, squares = own_half(routed, gain, shrink)
    shrunk = finish(values, squares, gain, shrink, arrived)
    return (mixed, shrunk)


def solution(mesh):
    placed = (
        P(("groups", "dp"), ("tensor", "section")),
        P(("tensor", "section"), "dp"),
        P(("groups", "tensor", "section"), "dp"),
        P(),
        P("dp", None, None),
        P(("groups", "tensor", "section"), None),
    )
    return jax.shard_map(
        body,
        mesh=mesh,
        in_specs=placed,
        out_specs=(
            P(("groups", "tensor", "section"), "dp"),
            P("dp", ("groups", "tensor", "section"), None, None),
        ),
        check_vma=False,
    )
```

```python
import functools

import jax
import jax.numpy as jnp
from jax import lax
from jax.experimental import pallas as pl
from jax.experimental.pallas import tpu as pltpu
from jax.sharding import PartitionSpec as P

MOST = 2
EPS = 1e-05
DEPTH_STEP = 512
HELD_BYTES = 21 * 2**20
WIDTH = 1024
MIB = 2**20
F32 = jnp.float32
BF16 = jnp.bfloat16


def whole():
    return pl.BlockSpec(memory_space=pltpu.VMEM)


def step_of(depth):
    return max(s for s in range(16, DEPTH_STEP + 1, 16) if depth % s == 0)


def fetch_kernel(weight_ref, held_ref, sems):
    count, step, _ = held_ref.shape
    copies = [
        pltpu.make_async_copy(
            weight_ref.at[pl.ds(i * step, step), :], held_ref.at[i], sems.at[i]
        )
        for i in range(count)
    ]
    for copy in copies:
        copy.start()
    for copy in copies:
        copy.wait()


def fetch(weight, count, step):
    columns = weight.shape[1]
    return pl.pallas_call(
        fetch_kernel,
        out_shape=pltpu.VMEM((count, step, columns), weight.dtype),
        in_specs=[pl.BlockSpec(memory_space=pl.ANY)],
        out_specs=whole(),
        scratch_shapes=[pltpu.SemaphoreType.DMA((count,))],
        compiler_params=pltpu.CompilerParams(vmem_limit_bytes=1 * MIB),
        cost_estimate=pl.CostEstimate(
            flops=0, bytes_accessed=2 * count * step * columns, transcendentals=0
        ),
        name="fetch",
    )(weight)


def project_kernel(
    own_ref,
    others_ref,
    held_ref,
    weight_ref,
    total_ref,
    sent_ref,
    rows_ref,
    halves_ref,
    rest_ref,
    sems,
    *,
    tensors,
    sections,
):
    held, step, columns = held_ref.shape
    rest = rest_ref.shape[0]
    own_rows = own_ref.shape[0]
    dp = 1 + others_ref.shape[0]
    me = lax.axis_index("dp")
    width = min(columns, WIDTH)

    def copy_of(i, sem, first=0, size=step):
        return pltpu.make_async_copy(
            weight_ref.at[pl.ds((held + i) * step + first, size), :],
            rest_ref.at[i, pl.ds(first, size), :],
            sems.at[sem],
        )

    half = step // 2
    for i in range(rest - 1):
        copy_of(i, i).start()
    for part in range(2):
        copy_of(rest - 1, rest - 1 + part, part * half, half).start()

    def fill(target, block):
        for shift in range(dp):
            first = pl.multiple_of((me + dp - shift) % dp * own_rows, own_rows)
            source = own_ref[:, block] if shift == 0 else others_ref[shift - 1, :, block]
            target[pl.ds(first, own_rows), :] = source

    for i in range(held + rest - 1):
        fill(rows_ref.at[i], slice(i * step, (i + 1) * step))
    for part in range(2):
        first = (held + rest - 1) * step + part * half
        fill(halves_ref.at[part], slice(first, first + half))

    def held_step(n, _):
        lanes = pl.ds(pl.multiple_of(n * width, width), width)
        total_ref[:, lanes] = sum(
            jnp.dot(rows_ref[i], held_ref[i, :, lanes], preferred_element_type=F32)
            for i in range(held)
        )
        return 0

    def add(rows, block_ref):
        for n in range(0, columns, width):
            lanes = slice(n, n + width)
            total_ref[:, lanes] += jnp.dot(rows, block_ref[:, lanes], preferred_element_type=F32)

    def rest_step(i, _):
        copy_of(i, i).wait()
        add(rows_ref[held + i], rest_ref.at[i])
        return 0

    def half_step(part, _):
        first = pl.multiple_of(part * half, half)
        copy_of(rest - 1, rest - 1 + part, first, half).wait()
        add(halves_ref[part], rest_ref.at[rest - 1, pl.ds(first, half), :])
        return 0

    def sent_step(n, _):
        lanes = pl.ds(pl.multiple_of(n * width, width), width)
        for turn in range(1, sections):
            rows = rows_of(turn, total_ref, lanes, tensors, sections)
            sent_ref[turn - 1, :, lanes] = rows.astype(BF16)
        return 0

    lax.fori_loop(0, columns // width, held_step, 0)
    lax.fori_loop(0, rest - 1, rest_step, 0)
    lax.fori_loop(0, 2, half_step, 0)
    lax.fori_loop(0, columns // width, sent_step, 0)


def rows_of(turn, total_ref, lanes, tensors, sections):
    tensor, section = lax.axis_index("tensor"), lax.axis_index("section")
    block_rows = total_ref.shape[0] // (tensors * sections)
    group = sections * block_rows
    blocks = []
    for k in range(tensors):
        first = pl.multiple_of(partner_of(tensor, k, tensors) * group, group)
        rows = total_ref[pl.ds(first, group), lanes]
        rows = pltpu.roll(rows, (sections - section) % sections * block_rows, 0)
        part = (turn + (k > 0)) % sections
        blocks.append(rows[part * block_rows : (part + 1) * block_rows])
    return jnp.concatenate(blocks, axis=0)


def keep_kernel(total_ref, kept_ref, *, tensors, sections):
    columns = total_ref.shape[1]
    width = min(columns, WIDTH)
    for n in range(0, columns, width):
        lanes = slice(n, n + width)
        kept_ref[:, lanes] = rows_of(0, total_ref, lanes, tensors, sections)


def keep(total, tensors, sections):
    rows, columns = total.shape
    return pl.pallas_call(
        functools.partial(keep_kernel, tensors=tensors, sections=sections),
        out_shape=jax.ShapeDtypeStruct((rows // sections, columns), F32),
        in_specs=[whole()],
        out_specs=whole(),
        compiler_params=pltpu.CompilerParams(vmem_limit_bytes=4 * MIB),
        name="keep",
    )(total)


def project(own, others, held, weight, tensors, sections):
    own_rows, depth = own.shape
    rows = own_rows * (1 + others.shape[0])
    columns = weight.shape[1]
    count, step, _ = held.shape
    rest = depth // step - count
    return pl.pallas_call(
        functools.partial(project_kernel, tensors=tensors, sections=sections),
        out_shape=(
            pltpu.VMEM((rows, columns), F32),
            pltpu.VMEM((sections - 1, rows // sections, columns), BF16),
        ),
        in_specs=[whole(), whole(), whole(), pl.BlockSpec(memory_space=pl.ANY)],
        out_specs=(whole(), whole()),
        scratch_shapes=[
            pltpu.VMEM((depth // step - 1, rows, step), BF16),
            pltpu.VMEM((2, rows, step // 2), BF16),
            pltpu.VMEM((rest, step, columns), BF16),
            pltpu.SemaphoreType.DMA((rest + 1,)),
        ],
        compiler_params=pltpu.CompilerParams(vmem_limit_bytes=36 * MIB),
        cost_estimate=pl.CostEstimate(
            flops=2 * rows * depth * columns,
            bytes_accessed=2 * rest * step * columns,
            transcendentals=0,
        ),
        name="project",
    )(own, others, held, weight)


def partner_of(me, turn, count):
    if count & (count - 1) == 0:
        return me ^ turn
    return (me + turn) % count


def turn_of(me, partner, count):
    if count & (count - 1) == 0:
        return me ^ partner
    return (partner - me) % count


def exchange_plan(count):
    if count == 4:
        return [(2, 3, 1, 0), (3, 2, 0, 1), (1, 0, 3, 2)]
    turns = range(count - 1, 0, -1)
    return [tuple(partner_of(i, turn, count) for i in range(count)) for turn in turns]


def pair_kernel(kept_ref, *refs, plan, tensors):
    arrived, (own_ref, *outs) = refs[: -1 - len(plan)], refs[-1 - len(plan) :]
    me = lax.axis_index("tensor")
    block_rows = own_ref.shape[0]
    total = kept_ref[...]
    for piece in arrived:
        total = total + piece[...].astype(F32)
    blocks = [total[turn * block_rows : (turn + 1) * block_rows] for turn in range(tensors)]
    own_ref[...] = blocks[0]
    for receivers, out_ref in zip(plan, outs):
        turns = [turn_of(i, j, tensors) for i, j in enumerate(receivers)]
        block = blocks[turns[0]]
        for i, turn in enumerate(turns):
            if turn != turns[0]:
                block = jnp.where(me == i, blocks[turn], block)
        out_ref[...] = block.astype(out_ref.dtype)


def pair(kept, arrived, plan, tensors):
    rows, columns = kept.shape
    block = (rows // tensors, columns)
    return pl.pallas_call(
        functools.partial(pair_kernel, plan=plan, tensors=tensors),
        out_shape=[jax.ShapeDtypeStruct(block, F32)] + [jax.ShapeDtypeStruct(block, BF16)] * len(plan),
        in_specs=[whole()] * (1 + len(arrived)),
        out_specs=[whole()] * (1 + len(plan)),
        compiler_params=pltpu.CompilerParams(vmem_limit_bytes=8 * MIB),
        name="pair",
    )(kept, *arrived)


def places_of(row, slots, owners, local):
    rows = row.shape[1]
    upper = lax.broadcasted_iota(jnp.int32, (rows, rows), 0)
    lower = lax.broadcasted_iota(jnp.int32, (rows, rows), 1)
    column = jnp.sum(jnp.where(upper == lower, row, 0), axis=1, keepdims=True)
    before = jnp.logical_and(column == row, upper < lower)
    rank_of = jnp.sum(before.astype(jnp.int32), axis=0, keepdims=True)
    slot = lax.broadcasted_iota(jnp.int32, (slots * owners, rows), 0)
    owner = (lax.axis_index("dp") + slot // slots) % owners
    adapter = owner * local + slot // MOST % local
    return jnp.logical_and(row == adapter, rank_of == slot % MOST).astype(F32)


def prepare_kernel(index_ref, shrink_ref, places_ref, out_ref, sem, *, slots, owners):
    copy = pltpu.make_async_copy(shrink_ref, out_ref, sem)
    copy.start()
    places_ref[...] = places_of(index_ref[...], slots, owners, slots // MOST)
    copy.wait()


def prepare(index, shrink, slots, owners):
    return pl.pallas_call(
        functools.partial(prepare_kernel, slots=slots, owners=owners),
        out_shape=(
            jax.ShapeDtypeStruct((slots * owners, index.shape[1]), F32),
            pltpu.VMEM(shrink.shape, shrink.dtype),
        ),
        in_specs=[whole(), pl.BlockSpec(memory_space=pl.ANY)],
        out_specs=(whole(), whole()),
        scratch_shapes=[pltpu.SemaphoreType.DMA],
        compiler_params=pltpu.CompilerParams(vmem_limit_bytes=1 * MIB),
        name="prepare",
    )(index, pltpu.with_memory_space_constraint(shrink, pltpu.HBM))


def mix_kernel(residual_ref, places_ref, own_ref, *refs):
    arrived, (mixed_ref, kept_ref, sent_ref) = refs[:-3], refs[-3:]
    slots = kept_ref.shape[0]
    places = places_ref[...]
    total = own_ref[...] + residual_ref[...].astype(F32)
    for piece in arrived:
        total = total + piece[...].astype(F32)
    mixed = total.astype(BF16)
    mixed_ref[...] = mixed
    widened = mixed.astype(F32)
    routed = sum(
        places[:, row : row + 1] * widened[row : row + 1, :] for row in range(widened.shape[0])
    )
    kept_ref[...] = routed[:slots]
    for turn in range(sent_ref.shape[0]):
        sent_ref[turn] = routed[(turn + 1) * slots : (turn + 2) * slots].astype(BF16)


def mix(residual, places, own, arrived, slots, owners):
    rows, columns = residual.shape
    return pl.pallas_call(
        mix_kernel,
        out_shape=(
            pltpu.VMEM((rows, columns), BF16),
            jax.ShapeDtypeStruct((slots, columns), F32),
            jax.ShapeDtypeStruct((owners - 1, slots, columns), BF16),
        ),
        in_specs=[whole()] * (3 + len(arrived)),
        out_specs=(whole(),) * 3,
        compiler_params=pltpu.CompilerParams(vmem_limit_bytes=8 * MIB),
        name="mix",
    )(residual, places, own, *arrived)


def partial_values(rows, gain_ref, shrink_ref, place, columns, local):
    first = pl.multiple_of(place * columns, columns)
    squares = jnp.sum(rows * rows, axis=1, keepdims=True)
    scaled = rows * gain_ref[:, pl.ds(first, columns)].astype(F32)
    high = scaled.astype(BF16)
    low = (scaled - high.astype(F32)).astype(BF16)
    values = []
    for adapter in range(local):
        mine = slice(adapter * MOST, (adapter + 1) * MOST)
        both = jnp.concatenate([high[mine], low[mine]], axis=0)
        product = lax.dot_general(
            both,
            shrink_ref[adapter, :, pl.ds(first, columns)],
            (((1,), (1,)), ((), ())),
            preferred_element_type=F32,
        )
        values.append(product[:MOST] + product[MOST:])
    return jnp.concatenate(values, axis=0), squares


def own_half_kernel(rows_ref, gain_ref, shrink_ref, values_ref, squares_ref):
    columns = rows_ref.shape[1]
    values, squares = partial_values(
        rows_ref[...], gain_ref, shrink_ref, lax.axis_index("dp"), columns, shrink_ref.shape[0]
    )
    values_ref[...] = values
    squares_ref[...] = jnp.broadcast_to(squares, squares_ref.shape)


def own_half(rows, gain, shrink):
    slots = rows.shape[0]
    rank = shrink.shape[1]
    return pl.pallas_call(
        own_half_kernel,
        out_shape=(
            jax.ShapeDtypeStruct((slots, rank), F32),
            jax.ShapeDtypeStruct((slots, rank), F32),
        ),
        in_specs=[whole()] * 3,
        out_specs=(whole(),) * 2,
        compiler_params=pltpu.CompilerParams(vmem_limit_bytes=8 * MIB),
        cost_estimate=pl.CostEstimate(
            flops=2 * slots * rows.shape[1] * rank, bytes_accessed=2 * MIB, transcendentals=0
        ),
        name="own_half",
    )(rows, gain, shrink)


def finish_kernel(values_ref, squares_ref, gain_ref, shrink_ref, *refs):
    arrived, out_ref = refs[:-1], refs[-1]
    dp = 1 + len(arrived)
    me = lax.axis_index("dp")
    local = shrink_ref.shape[0]
    columns = arrived[0].shape[1]
    values, squares = values_ref[...], squares_ref[:, :1]
    for shift, piece in enumerate(arrived, start=1):
        more, more_squares = partial_values(
            piece[...].astype(F32),
            gain_ref,
            shrink_ref,
            lax.rem(me + dp - shift, dp),
            columns,
            local,
        )
        values, squares = values + more, squares + more_squares
    result = 2.0 * values * lax.rsqrt(squares / (columns * dp) + EPS)
    for adapter in range(local):
        out_ref[adapter, 0] = result[adapter * MOST : (adapter + 1) * MOST]


def finish(values, squares, gain, shrink, arrived):
    local, rank, _ = shrink.shape
    return pl.pallas_call(
        finish_kernel,
        out_shape=jax.ShapeDtypeStruct((local, 1, MOST, rank), F32),
        in_specs=[whole()] * (4 + len(arrived)),
        out_specs=whole(),
        compiler_params=pltpu.CompilerParams(vmem_limit_bytes=8 * MIB),
        name="finish",
    )(values, squares, gain, shrink, *arrived)


def shifted(array, axis, shift):
    count = lax.axis_size(axis)
    return lax.ppermute(array, axis, [(i, (i + shift) % count) for i in range(count)])


def across(array, receivers):
    sections = lax.axis_size("section")
    pairs = [
        (i * sections + s, j * sections + (s + 1) % sections)
        for i, j in enumerate(receivers)
        for s in range(sections)
    ]
    return lax.ppermute(array, ("tensor", "section"), pairs)


def body(hidden, down_matrix, residual, next_norm_scale, shrink_matrix, adapter_index):
    dp, tensors, sections = (lax.axis_size(axis) for axis in ("dp", "tensor", "section"))
    depth, _ = down_matrix.shape
    local = shrink_matrix.shape[0]

    others = jnp.stack([shifted(hidden, "dp", shift) for shift in range(1, dp)])

    step = step_of(depth)
    blocks = depth // step
    held_count = max(1, min(blocks // 2, HELD_BYTES // (2 * step * down_matrix.shape[1])))
    held = fetch(down_matrix, held_count, step)

    shrink = jnp.swapaxes(shrink_matrix, 1, 2)
    gain = next_norm_scale[None, :]

    in_vmem = [pltpu.with_memory_space_constraint(x, pltpu.VMEM) for x in (hidden, others, held)]
    total, sent = project(*in_vmem, down_matrix, tensors, sections)
    index, total = lax.optimization_barrier((adapter_index.reshape(1, -1), total))
    kept = keep(total, tensors, sections)
    places, shrink = prepare(index, shrink, local * MOST, dp)
    arrived = [shifted(sent[s - 1], "section", s) for s in range(1, sections)]
    plan = exchange_plan(tensors)
    own, *sums = pair(kept, arrived, plan, tensors)
    arrived = [across(x, receivers) for x, receivers in zip(sums, plan)]
    mixed, routed, leaving = mix(residual, places, own, arrived, local * MOST, dp)
    arrived = [shifted(leaving[s - 1], "dp", s) for s in range(1, dp)]
    values, squares = own_half(routed, gain, shrink)
    shrunk = finish(values, squares, gain, shrink, arrived)
    return (mixed, shrunk)


def solution(mesh):
    placed = (
        P(("groups", "dp"), ("tensor", "section")),
        P(("tensor", "section"), "dp"),
        P(("groups", "tensor", "section"), "dp"),
        P(),
        P("dp", None, None),
        P(("groups", "tensor", "section"), None),
    )
    return jax.shard_map(
        body,
        mesh=mesh,
        in_specs=placed,
        out_specs=(
            P(("groups", "tensor", "section"), "dp"),
            P("dp", ("groups", "tensor", "section"), None, None),
        ),
        check_vma=False,
    )
```

```python
import functools

import jax
import jax.numpy as jnp
from jax import lax
from jax.experimental import pallas as pl
from jax.experimental.pallas import tpu as pltpu
from jax.sharding import PartitionSpec as P

MOST = 2
EPS = 1e-05
DEPTH_STEP = 512
HELD_BYTES = 21 * 2**20
WIDTH = 1024
MIB = 2**20
F32 = jnp.float32
BF16 = jnp.bfloat16


def whole():
    return pl.BlockSpec(memory_space=pltpu.VMEM)


def step_of(depth):
    return max(s for s in range(16, DEPTH_STEP + 1, 16) if depth % s == 0)


def fetch_kernel(weight_ref, held_ref, sems):
    count, step, _ = held_ref.shape
    copies = [
        pltpu.make_async_copy(
            weight_ref.at[pl.ds(i * step, step), :], held_ref.at[i], sems.at[i]
        )
        for i in range(count)
    ]
    for copy in copies:
        copy.start()
    for copy in copies:
        copy.wait()


def fetch(weight, count, step):
    columns = weight.shape[1]
    return pl.pallas_call(
        fetch_kernel,
        out_shape=pltpu.VMEM((count, step, columns), weight.dtype),
        in_specs=[pl.BlockSpec(memory_space=pl.ANY)],
        out_specs=whole(),
        scratch_shapes=[pltpu.SemaphoreType.DMA((count,))],
        compiler_params=pltpu.CompilerParams(vmem_limit_bytes=1 * MIB),
        cost_estimate=pl.CostEstimate(
            flops=0, bytes_accessed=2 * count * step * columns, transcendentals=0
        ),
        name="fetch",
    )(weight)


def last_parts(step):
    if step % 64:
        return [(0, step)]
    return [(0, step // 2), (step // 2, step // 4), (step // 4 * 3, step // 4)]


def project_kernel(
    own_ref,
    others_ref,
    held_ref,
    weight_ref,
    total_ref,
    sent_ref,
    rows_ref,
    rest_ref,
    sems,
    *,
    tensors,
    sections,
):
    held, step, columns = held_ref.shape
    rest = rest_ref.shape[0]
    own_rows = own_ref.shape[0]
    dp = 1 + others_ref.shape[0]
    me = lax.axis_index("dp")
    width = min(columns, WIDTH)

    def copy_of(i, sem, first=0, size=step):
        return pltpu.make_async_copy(
            weight_ref.at[pl.ds((held + i) * step + first, size), :],
            rest_ref.at[i, pl.ds(first, size), :],
            sems.at[sem],
        )

    parts = last_parts(step)
    last = [copy_of(rest - 1, rest - 1 + k, *part) for k, part in enumerate(parts)]
    for i in range(rest - 1):
        copy_of(i, i).start()
    for copy in last:
        copy.start()

    for i in range(held + rest):
        block = slice(i * step, (i + 1) * step)
        for shift in range(dp):
            first = pl.multiple_of((me + dp - shift) % dp * own_rows, own_rows)
            source = own_ref[:, block] if shift == 0 else others_ref[shift - 1, :, block]
            rows_ref[i, pl.ds(first, own_rows), :] = source

    def held_step(n, _):
        lanes = pl.ds(pl.multiple_of(n * width, width), width)
        total_ref[:, lanes] = sum(
            jnp.dot(rows_ref[i], held_ref[i, :, lanes], preferred_element_type=F32)
            for i in range(held)
        )
        return 0

    def add(i, part=slice(None)):
        for n in range(0, columns, width):
            lanes = slice(n, n + width)
            total_ref[:, lanes] += jnp.dot(
                rows_ref[held + i, :, part], rest_ref[i, part, lanes], preferred_element_type=F32
            )

    def rest_step(i, _):
        copy_of(i, i).wait()
        add(i)
        return 0

    lax.fori_loop(0, columns // width, held_step, 0)
    lax.fori_loop(0, rest - 1, rest_step, 0)
    for copy, (first, size) in zip(last, parts):
        copy.wait()
        add(rest - 1, slice(first, first + size))

    for turn in range(1, sections):
        for n in range(0, columns, width):
            lanes = slice(n, n + width)
            rows = rows_of(turn, total_ref, lanes, tensors, sections)
            sent_ref[turn - 1, :, lanes] = rows.astype(BF16)


def rows_of(turn, total_ref, lanes, tensors, sections):
    tensor, section = lax.axis_index("tensor"), lax.axis_index("section")
    block_rows = total_ref.shape[0] // (tensors * sections)
    group = sections * block_rows
    blocks = []
    for k in range(tensors):
        first = pl.multiple_of(partner_of(tensor, k, tensors) * group, group)
        rows = total_ref[pl.ds(first, group), lanes]
        rows = pltpu.roll(rows, (sections - section) % sections * block_rows, 0)
        part = (turn + (k > 0)) % sections
        blocks.append(rows[part * block_rows : (part + 1) * block_rows])
    return jnp.concatenate(blocks, axis=0)


def keep_kernel(total_ref, kept_ref, *, tensors, sections):
    columns = total_ref.shape[1]
    width = min(columns, WIDTH)
    for n in range(0, columns, width):
        lanes = slice(n, n + width)
        kept_ref[:, lanes] = rows_of(0, total_ref, lanes, tensors, sections)


def keep(total, tensors, sections):
    rows, columns = total.shape
    return pl.pallas_call(
        functools.partial(keep_kernel, tensors=tensors, sections=sections),
        out_shape=jax.ShapeDtypeStruct((rows // sections, columns), F32),
        in_specs=[whole()],
        out_specs=whole(),
        compiler_params=pltpu.CompilerParams(vmem_limit_bytes=4 * MIB),
        name="keep",
    )(total)


def project(own, others, held, weight, tensors, sections):
    own_rows, depth = own.shape
    rows = own_rows * (1 + others.shape[0])
    columns = weight.shape[1]
    count, step, _ = held.shape
    rest = depth // step - count
    return pl.pallas_call(
        functools.partial(project_kernel, tensors=tensors, sections=sections),
        out_shape=(
            pltpu.VMEM((rows, columns), F32),
            pltpu.VMEM((sections - 1, rows // sections, columns), BF16),
        ),
        in_specs=[whole(), whole(), whole(), pl.BlockSpec(memory_space=pl.ANY)],
        out_specs=(whole(), whole()),
        scratch_shapes=[
            pltpu.VMEM((depth // step, rows, step), BF16),
            pltpu.VMEM((rest, step, columns), BF16),
            pltpu.SemaphoreType.DMA((rest - 1 + len(last_parts(step)),)),
        ],
        compiler_params=pltpu.CompilerParams(vmem_limit_bytes=36 * MIB),
        cost_estimate=pl.CostEstimate(
            flops=2 * rows * depth * columns,
            bytes_accessed=2 * rest * step * columns,
            transcendentals=0,
        ),
        name="project",
    )(own, others, held, weight)


def partner_of(me, turn, count):
    if count & (count - 1) == 0:
        return me ^ turn
    return (me + turn) % count


def turn_of(me, partner, count):
    if count & (count - 1) == 0:
        return me ^ partner
    return (partner - me) % count


def exchange_plan(count):
    if count == 4:
        return [(1, 3, 0, 2), (3, 2, 1, 0), (2, 0, 3, 1)]
    turns = range(count - 1, 0, -1)
    return [tuple(partner_of(i, turn, count) for i in range(count)) for turn in turns]


def pair_kernel(kept_ref, *refs, plan, tensors):
    arrived, (own_ref, *outs) = refs[: -1 - len(plan)], refs[-1 - len(plan) :]
    me = lax.axis_index("tensor")
    block_rows = own_ref.shape[0]
    total = kept_ref[...]
    for piece in arrived:
        total = total + piece[...].astype(F32)
    blocks = [total[turn * block_rows : (turn + 1) * block_rows] for turn in range(tensors)]
    own_ref[...] = blocks[0]
    for receivers, out_ref in zip(plan, outs):
        turns = [turn_of(i, j, tensors) for i, j in enumerate(receivers)]
        block = blocks[turns[0]]
        for i, turn in enumerate(turns):
            if turn != turns[0]:
                block = jnp.where(me == i, blocks[turn], block)
        out_ref[...] = block.astype(out_ref.dtype)


def pair(kept, arrived, plan, tensors):
    rows, columns = kept.shape
    block = (rows // tensors, columns)
    return pl.pallas_call(
        functools.partial(pair_kernel, plan=plan, tensors=tensors),
        out_shape=[jax.ShapeDtypeStruct(block, F32)] + [jax.ShapeDtypeStruct(block, BF16)] * len(plan),
        in_specs=[whole()] * (1 + len(arrived)),
        out_specs=[whole()] * (1 + len(plan)),
        compiler_params=pltpu.CompilerParams(vmem_limit_bytes=8 * MIB),
        name="pair",
    )(kept, *arrived)


def places_of(row, slots, owners, local):
    rows = row.shape[1]
    upper = lax.broadcasted_iota(jnp.int32, (rows, rows), 0)
    lower = lax.broadcasted_iota(jnp.int32, (rows, rows), 1)
    column = jnp.sum(jnp.where(upper == lower, row, 0), axis=1, keepdims=True)
    before = jnp.logical_and(column == row, upper < lower)
    rank_of = jnp.sum(before.astype(jnp.int32), axis=0, keepdims=True)
    slot = lax.broadcasted_iota(jnp.int32, (slots * owners, rows), 0)
    owner = (lax.axis_index("dp") + slot // slots) % owners
    adapter = owner * local + slot // MOST % local
    return jnp.logical_and(row == adapter, rank_of == slot % MOST).astype(F32)


def prepare_kernel(index_ref, shrink_ref, places_ref, out_ref, sem, *, slots, owners):
    copy = pltpu.make_async_copy(shrink_ref, out_ref, sem)
    copy.start()
    places_ref[...] = places_of(index_ref[...], slots, owners, slots // MOST)
    copy.wait()


def prepare(index, shrink, slots, owners):
    return pl.pallas_call(
        functools.partial(prepare_kernel, slots=slots, owners=owners),
        out_shape=(
            jax.ShapeDtypeStruct((slots * owners, index.shape[1]), F32),
            pltpu.VMEM(shrink.shape, shrink.dtype),
        ),
        in_specs=[whole(), pl.BlockSpec(memory_space=pl.ANY)],
        out_specs=(whole(), whole()),
        scratch_shapes=[pltpu.SemaphoreType.DMA],
        compiler_params=pltpu.CompilerParams(vmem_limit_bytes=1 * MIB),
        name="prepare",
    )(index, pltpu.with_memory_space_constraint(shrink, pltpu.HBM))


def mix_kernel(residual_ref, places_ref, own_ref, *refs):
    arrived, (mixed_ref, kept_ref, sent_ref) = refs[:-3], refs[-3:]
    slots = kept_ref.shape[0]
    places = places_ref[...]
    total = own_ref[...] + residual_ref[...].astype(F32)
    for piece in arrived:
        total = total + piece[...].astype(F32)
    mixed = total.astype(BF16)
    mixed_ref[...] = mixed
    widened = mixed.astype(F32)
    routed = sum(
        places[:, row : row + 1] * widened[row : row + 1, :] for row in range(widened.shape[0])
    )
    kept_ref[...] = routed[:slots]
    for turn in range(sent_ref.shape[0]):
        sent_ref[turn] = routed[(turn + 1) * slots : (turn + 2) * slots].astype(BF16)


def mix(residual, places, own, arrived, slots, owners):
    rows, columns = residual.shape
    return pl.pallas_call(
        mix_kernel,
        out_shape=(
            pltpu.VMEM((rows, columns), BF16),
            jax.ShapeDtypeStruct((slots, columns), F32),
            jax.ShapeDtypeStruct((owners - 1, slots, columns), BF16),
        ),
        in_specs=[whole()] * (3 + len(arrived)),
        out_specs=(whole(),) * 3,
        compiler_params=pltpu.CompilerParams(vmem_limit_bytes=8 * MIB),
        name="mix",
    )(residual, places, own, *arrived)


def partial_values(rows, gain_ref, shrink_ref, place, columns, local):
    first = pl.multiple_of(place * columns, columns)
    squares = jnp.sum(rows * rows, axis=1, keepdims=True)
    scaled = rows * gain_ref[:, pl.ds(first, columns)].astype(F32)
    high = scaled.astype(BF16)
    low = (scaled - high.astype(F32)).astype(BF16)
    values = []
    for adapter in range(local):
        mine = slice(adapter * MOST, (adapter + 1) * MOST)
        both = jnp.concatenate([high[mine], low[mine]], axis=0)
        product = lax.dot_general(
            both,
            shrink_ref[adapter, :, pl.ds(first, columns)],
            (((1,), (1,)), ((), ())),
            preferred_element_type=F32,
        )
        values.append(product[:MOST] + product[MOST:])
    return jnp.concatenate(values, axis=0), squares


def own_half_kernel(rows_ref, gain_ref, shrink_ref, values_ref, squares_ref):
    columns = rows_ref.shape[1]
    values, squares = partial_values(
        rows_ref[...], gain_ref, shrink_ref, lax.axis_index("dp"), columns, shrink_ref.shape[0]
    )
    values_ref[...] = values
    squares_ref[...] = jnp.broadcast_to(squares, squares_ref.shape)


def own_half(rows, gain, shrink):
    slots = rows.shape[0]
    rank = shrink.shape[1]
    return pl.pallas_call(
        own_half_kernel,
        out_shape=(
            jax.ShapeDtypeStruct((slots, rank), F32),
            jax.ShapeDtypeStruct((slots, rank), F32),
        ),
        in_specs=[whole()] * 3,
        out_specs=(whole(),) * 2,
        compiler_params=pltpu.CompilerParams(vmem_limit_bytes=8 * MIB),
        cost_estimate=pl.CostEstimate(
            flops=2 * slots * rows.shape[1] * rank, bytes_accessed=2 * MIB, transcendentals=0
        ),
        name="own_half",
    )(rows, gain, shrink)


def finish_kernel(values_ref, squares_ref, gain_ref, shrink_ref, *refs):
    arrived, out_ref = refs[:-1], refs[-1]
    dp = 1 + len(arrived)
    me = lax.axis_index("dp")
    local = shrink_ref.shape[0]
    columns = arrived[0].shape[1]
    values, squares = values_ref[...], squares_ref[:, :1]
    for shift, piece in enumerate(arrived, start=1):
        more, more_squares = partial_values(
            piece[...].astype(F32),
            gain_ref,
            shrink_ref,
            lax.rem(me + dp - shift, dp),
            columns,
            local,
        )
        values, squares = values + more, squares + more_squares
    result = 2.0 * values * lax.rsqrt(squares / (columns * dp) + EPS)
    for adapter in range(local):
        out_ref[adapter, 0] = result[adapter * MOST : (adapter + 1) * MOST]


def finish(values, squares, gain, shrink, arrived):
    local, rank, _ = shrink.shape
    return pl.pallas_call(
        finish_kernel,
        out_shape=jax.ShapeDtypeStruct((local, 1, MOST, rank), F32),
        in_specs=[whole()] * (4 + len(arrived)),
        out_specs=whole(),
        compiler_params=pltpu.CompilerParams(vmem_limit_bytes=8 * MIB),
        name="finish",
    )(values, squares, gain, shrink, *arrived)


def shifted(array, axis, shift):
    count = lax.axis_size(axis)
    return lax.ppermute(array, axis, [(i, (i + shift) % count) for i in range(count)])


def across(array, receivers):
    sections = lax.axis_size("section")
    pairs = [
        (i * sections + s, j * sections + (s + 1) % sections)
        for i, j in enumerate(receivers)
        for s in range(sections)
    ]
    return lax.ppermute(array, ("tensor", "section"), pairs)


def body(hidden, down_matrix, residual, next_norm_scale, shrink_matrix, adapter_index):
    dp, tensors, sections = (lax.axis_size(axis) for axis in ("dp", "tensor", "section"))
    depth, _ = down_matrix.shape
    local = shrink_matrix.shape[0]

    others = jnp.stack([shifted(hidden, "dp", shift) for shift in range(1, dp)])

    step = step_of(depth)
    blocks = depth // step
    held_count = max(1, min(blocks // 2, HELD_BYTES // (2 * step * down_matrix.shape[1])))
    held = fetch(down_matrix, held_count, step)

    shrink = jnp.swapaxes(shrink_matrix, 1, 2)
    gain = next_norm_scale[None, :]

    in_vmem = [pltpu.with_memory_space_constraint(x, pltpu.VMEM) for x in (hidden, others, held)]
    total, sent = project(*in_vmem, down_matrix, tensors, sections)
    index, total = lax.optimization_barrier((adapter_index.reshape(1, -1), total))
    kept = keep(total, tensors, sections)
    places, shrink = prepare(index, shrink, local * MOST, dp)
    arrived = [shifted(sent[s - 1], "section", s) for s in range(1, sections)]
    plan = exchange_plan(tensors)
    own, *sums = pair(kept, arrived, plan, tensors)
    arrived = [across(x, receivers) for x, receivers in zip(sums, plan)]
    mixed, routed, leaving = mix(residual, places, own, arrived, local * MOST, dp)
    arrived = [shifted(leaving[s - 1], "dp", s) for s in range(1, dp)]
    values, squares = own_half(routed, gain, shrink)
    shrunk = finish(values, squares, gain, shrink, arrived)
    return (mixed, shrunk)


def solution(mesh):
    placed = (
        P(("groups", "dp"), ("tensor", "section")),
        P(("tensor", "section"), "dp"),
        P(("groups", "tensor", "section"), "dp"),
        P(),
        P("dp", None, None),
        P(("groups", "tensor", "section"), None),
    )
    return jax.shard_map(
        body,
        mesh=mesh,
        in_specs=placed,
        out_specs=(
            P(("groups", "tensor", "section"), "dp"),
            P("dp", ("groups", "tensor", "section"), None, None),
        ),
        check_vma=False,
    )
```

```python
import functools

import jax
import jax.numpy as jnp
from jax import lax
from jax.experimental import pallas as pl
from jax.experimental.pallas import tpu as pltpu
from jax.sharding import PartitionSpec as P

MOST = 2
EPS = 1e-05
DEPTH_STEP = 512
HELD_BYTES = 21 * 2**20
WIDTH = 1024
MIB = 2**20
F32 = jnp.float32
BF16 = jnp.bfloat16


def whole():
    return pl.BlockSpec(memory_space=pltpu.VMEM)


def step_of(depth):
    return max(s for s in range(16, DEPTH_STEP + 1, 16) if depth % s == 0)


def fetch_kernel(weight_ref, held_ref, sems):
    count, step, _ = held_ref.shape
    copies = [
        pltpu.make_async_copy(
            weight_ref.at[pl.ds(i * step, step), :], held_ref.at[i], sems.at[i]
        )
        for i in range(count)
    ]
    for copy in copies:
        copy.start()
    for copy in copies:
        copy.wait()


def fetch(weight, count, step):
    columns = weight.shape[1]
    return pl.pallas_call(
        fetch_kernel,
        out_shape=pltpu.VMEM((count, step, columns), weight.dtype),
        in_specs=[pl.BlockSpec(memory_space=pl.ANY)],
        out_specs=whole(),
        scratch_shapes=[pltpu.SemaphoreType.DMA((count,))],
        compiler_params=pltpu.CompilerParams(vmem_limit_bytes=1 * MIB),
        cost_estimate=pl.CostEstimate(
            flops=0, bytes_accessed=2 * count * step * columns, transcendentals=0
        ),
        name="fetch",
    )(weight)


def last_parts(step):
    if step % 64:
        return [(0, step)]
    return [(0, step // 2), (step // 2, step // 4), (step // 4 * 3, step // 4)]


def project_kernel(
    own_ref,
    others_ref,
    held_ref,
    weight_ref,
    total_ref,
    sent_ref,
    rows_ref,
    rest_ref,
    sems,
    *,
    tensors,
    sections,
):
    held, step, columns = held_ref.shape
    rest = rest_ref.shape[0]
    own_rows = own_ref.shape[0]
    dp = 1 + others_ref.shape[0]
    me = lax.axis_index("dp")
    width = min(columns, WIDTH)

    def copy_of(i, sem, first=0, size=step):
        return pltpu.make_async_copy(
            weight_ref.at[pl.ds((held + i) * step + first, size), :],
            rest_ref.at[i, pl.ds(first, size), :],
            sems.at[sem],
        )

    parts = last_parts(step)
    last = [copy_of(rest - 1, rest - 1 + k, *part) for k, part in enumerate(parts)]
    for i in range(rest - 1):
        copy_of(i, i).start()
    for copy in last:
        copy.start()

    for i in range(held + rest):
        block = slice(i * step, (i + 1) * step)
        for shift in range(dp):
            first = pl.multiple_of((me + dp - shift) % dp * own_rows, own_rows)
            source = own_ref[:, block] if shift == 0 else others_ref[shift - 1, :, block]
            rows_ref[i, pl.ds(first, own_rows), :] = source

    def held_step(n, _):
        lanes = pl.ds(pl.multiple_of(n * width, width), width)
        total_ref[:, lanes] = sum(
            jnp.dot(rows_ref[i], held_ref[i, :, lanes], preferred_element_type=F32)
            for i in range(held)
        )
        return 0

    def add(i, part=slice(None)):
        for n in range(0, columns, width):
            lanes = slice(n, n + width)
            total_ref[:, lanes] += jnp.dot(
                rows_ref[held + i, :, part], rest_ref[i, part, lanes], preferred_element_type=F32
            )

    def rest_step(i, _):
        copy_of(i, i).wait()
        add(i)
        return 0

    lax.fori_loop(0, columns // width, held_step, 0)
    lax.fori_loop(0, rest - 1, rest_step, 0)
    for copy, (first, size) in zip(last, parts):
        copy.wait()
        add(rest - 1, slice(first, first + size))

    for turn in range(1, sections):
        for n in range(0, columns, width):
            lanes = slice(n, n + width)
            rows = rows_of(turn, total_ref, lanes, tensors, sections)
            sent_ref[turn - 1, :, lanes] = rows.astype(BF16)


def rows_of(turn, total_ref, lanes, tensors, sections):
    tensor, section = lax.axis_index("tensor"), lax.axis_index("section")
    block_rows = total_ref.shape[0] // (tensors * sections)
    group = sections * block_rows
    blocks = []
    for k in range(tensors):
        first = pl.multiple_of(partner_of(tensor, k, tensors) * group, group)
        rows = total_ref[pl.ds(first, group), lanes]
        rows = pltpu.roll(rows, (sections - section) % sections * block_rows, 0)
        part = (turn + (k > 0)) % sections
        blocks.append(rows[part * block_rows : (part + 1) * block_rows])
    return jnp.concatenate(blocks, axis=0)


def keep_kernel(total_ref, kept_ref, *, tensors, sections):
    columns = total_ref.shape[1]
    width = min(columns, WIDTH)
    for n in range(0, columns, width):
        lanes = slice(n, n + width)
        kept_ref[:, lanes] = rows_of(0, total_ref, lanes, tensors, sections)


def keep(total, tensors, sections):
    rows, columns = total.shape
    return pl.pallas_call(
        functools.partial(keep_kernel, tensors=tensors, sections=sections),
        out_shape=jax.ShapeDtypeStruct((rows // sections, columns), F32),
        in_specs=[whole()],
        out_specs=whole(),
        compiler_params=pltpu.CompilerParams(vmem_limit_bytes=4 * MIB),
        name="keep",
    )(total)


def project(own, others, held, weight, tensors, sections):
    own_rows, depth = own.shape
    rows = own_rows * (1 + others.shape[0])
    columns = weight.shape[1]
    count, step, _ = held.shape
    rest = depth // step - count
    return pl.pallas_call(
        functools.partial(project_kernel, tensors=tensors, sections=sections),
        out_shape=(
            pltpu.VMEM((rows, columns), F32),
            pltpu.VMEM((sections - 1, rows // sections, columns), BF16),
        ),
        in_specs=[whole(), whole(), whole(), pl.BlockSpec(memory_space=pl.ANY)],
        out_specs=(whole(), whole()),
        scratch_shapes=[
            pltpu.VMEM((depth // step, rows, step), BF16),
            pltpu.VMEM((rest, step, columns), BF16),
            pltpu.SemaphoreType.DMA((rest - 1 + len(last_parts(step)),)),
        ],
        compiler_params=pltpu.CompilerParams(vmem_limit_bytes=36 * MIB),
        cost_estimate=pl.CostEstimate(
            flops=2 * rows * depth * columns,
            bytes_accessed=2 * rest * step * columns,
            transcendentals=0,
        ),
        name="project",
    )(own, others, held, weight)


def partner_of(me, turn, count):
    if count & (count - 1) == 0:
        return me ^ turn
    return (me + turn) % count


def turn_of(me, partner, count):
    if count & (count - 1) == 0:
        return me ^ partner
    return (partner - me) % count


def exchange_plan(count):
    if count == 4:
        return [(2, 3, 1, 0), (3, 2, 0, 1), (1, 0, 3, 2)]
    turns = range(count - 1, 0, -1)
    return [tuple(partner_of(i, turn, count) for i in range(count)) for turn in turns]


def pair_kernel(kept_ref, *refs, plan, tensors):
    arrived, (own_ref, *outs) = refs[: -1 - len(plan)], refs[-1 - len(plan) :]
    me = lax.axis_index("tensor")
    block_rows = own_ref.shape[0]
    total = kept_ref[...]
    for piece in arrived:
        total = total + piece[...].astype(F32)
    blocks = [total[turn * block_rows : (turn + 1) * block_rows] for turn in range(tensors)]
    own_ref[...] = blocks[0]
    for receivers, out_ref in zip(plan, outs):
        turns = [turn_of(i, j, tensors) for i, j in enumerate(receivers)]
        block = blocks[turns[0]]
        for i, turn in enumerate(turns):
            if turn != turns[0]:
                block = jnp.where(me == i, blocks[turn], block)
        out_ref[...] = block.astype(out_ref.dtype)


def pair(kept, arrived, plan, tensors):
    rows, columns = kept.shape
    block = (rows // tensors, columns)
    return pl.pallas_call(
        functools.partial(pair_kernel, plan=plan, tensors=tensors),
        out_shape=[jax.ShapeDtypeStruct(block, F32)] + [jax.ShapeDtypeStruct(block, BF16)] * len(plan),
        in_specs=[whole()] * (1 + len(arrived)),
        out_specs=[whole()] * (1 + len(plan)),
        compiler_params=pltpu.CompilerParams(vmem_limit_bytes=8 * MIB),
        name="pair",
    )(kept, *arrived)


def places_of(row, slots, owners, local):
    rows = row.shape[1]
    upper = lax.broadcasted_iota(jnp.int32, (rows, rows), 0)
    lower = lax.broadcasted_iota(jnp.int32, (rows, rows), 1)
    column = jnp.sum(jnp.where(upper == lower, row, 0), axis=1, keepdims=True)
    before = jnp.logical_and(column == row, upper < lower)
    rank_of = jnp.sum(before.astype(jnp.int32), axis=0, keepdims=True)
    slot = lax.broadcasted_iota(jnp.int32, (slots * owners, rows), 0)
    owner = (lax.axis_index("dp") + slot // slots) % owners
    adapter = owner * local + slot // MOST % local
    return jnp.logical_and(row == adapter, rank_of == slot % MOST).astype(F32)


def prepare_kernel(index_ref, shrink_ref, places_ref, out_ref, sem, *, slots, owners):
    copy = pltpu.make_async_copy(shrink_ref, out_ref, sem)
    copy.start()
    places_ref[...] = places_of(index_ref[...], slots, owners, slots // MOST)
    copy.wait()


def prepare(index, shrink, slots, owners):
    return pl.pallas_call(
        functools.partial(prepare_kernel, slots=slots, owners=owners),
        out_shape=(
            jax.ShapeDtypeStruct((slots * owners, index.shape[1]), F32),
            pltpu.VMEM(shrink.shape, shrink.dtype),
        ),
        in_specs=[whole(), pl.BlockSpec(memory_space=pl.ANY)],
        out_specs=(whole(), whole()),
        scratch_shapes=[pltpu.SemaphoreType.DMA],
        compiler_params=pltpu.CompilerParams(vmem_limit_bytes=1 * MIB),
        name="prepare",
    )(index, pltpu.with_memory_space_constraint(shrink, pltpu.HBM))


def mix_kernel(residual_ref, places_ref, own_ref, *refs):
    arrived, (mixed_ref, kept_ref, sent_ref) = refs[:-3], refs[-3:]
    slots = kept_ref.shape[0]
    places = places_ref[...]
    total = own_ref[...] + residual_ref[...].astype(F32)
    for piece in arrived:
        total = total + piece[...].astype(F32)
    mixed = total.astype(BF16)
    mixed_ref[...] = mixed
    widened = mixed.astype(F32)
    routed = sum(
        places[:, row : row + 1] * widened[row : row + 1, :] for row in range(widened.shape[0])
    )
    kept_ref[...] = routed[:slots]
    for turn in range(sent_ref.shape[0]):
        sent_ref[turn] = routed[(turn + 1) * slots : (turn + 2) * slots].astype(BF16)


def mix(residual, places, own, arrived, slots, owners):
    rows, columns = residual.shape
    return pl.pallas_call(
        mix_kernel,
        out_shape=(
            pltpu.VMEM((rows, columns), BF16),
            jax.ShapeDtypeStruct((slots, columns), F32),
            jax.ShapeDtypeStruct((owners - 1, slots, columns), BF16),
        ),
        in_specs=[whole()] * (3 + len(arrived)),
        out_specs=(whole(),) * 3,
        compiler_params=pltpu.CompilerParams(vmem_limit_bytes=8 * MIB),
        name="mix",
    )(residual, places, own, *arrived)


def partial_values(rows, gain_ref, shrink_ref, place, columns, local):
    first = pl.multiple_of(place * columns, columns)
    squares = jnp.sum(rows * rows, axis=1, keepdims=True)
    scaled = rows * gain_ref[:, pl.ds(first, columns)].astype(F32)
    high = scaled.astype(BF16)
    low = (scaled - high.astype(F32)).astype(BF16)
    values = []
    for adapter in range(local):
        mine = slice(adapter * MOST, (adapter + 1) * MOST)
        both = jnp.concatenate([high[mine], low[mine]], axis=0)
        product = lax.dot_general(
            both,
            shrink_ref[adapter, :, pl.ds(first, columns)],
            (((1,), (1,)), ((), ())),
            preferred_element_type=F32,
        )
        values.append(product[:MOST] + product[MOST:])
    return jnp.concatenate(values, axis=0), squares


def own_half_kernel(rows_ref, gain_ref, shrink_ref, values_ref, squares_ref):
    columns = rows_ref.shape[1]
    values, squares = partial_values(
        rows_ref[...], gain_ref, shrink_ref, lax.axis_index("dp"), columns, shrink_ref.shape[0]
    )
    values_ref[...] = values
    squares_ref[...] = jnp.broadcast_to(squares, squares_ref.shape)


def own_half(rows, gain, shrink):
    slots = rows.shape[0]
    rank = shrink.shape[1]
    return pl.pallas_call(
        own_half_kernel,
        out_shape=(
            jax.ShapeDtypeStruct((slots, rank), F32),
            jax.ShapeDtypeStruct((slots, rank), F32),
        ),
        in_specs=[whole()] * 3,
        out_specs=(whole(),) * 2,
        compiler_params=pltpu.CompilerParams(vmem_limit_bytes=8 * MIB),
        cost_estimate=pl.CostEstimate(
            flops=2 * slots * rows.shape[1] * rank, bytes_accessed=2 * MIB, transcendentals=0
        ),
        name="own_half",
    )(rows, gain, shrink)


def finish_kernel(values_ref, squares_ref, gain_ref, shrink_ref, *refs):
    arrived, out_ref = refs[:-1], refs[-1]
    dp = 1 + len(arrived)
    me = lax.axis_index("dp")
    local = shrink_ref.shape[0]
    columns = arrived[0].shape[1]
    values, squares = values_ref[...], squares_ref[:, :1]
    for shift, piece in enumerate(arrived, start=1):
        more, more_squares = partial_values(
            piece[...].astype(F32),
            gain_ref,
            shrink_ref,
            lax.rem(me + dp - shift, dp),
            columns,
            local,
        )
        values, squares = values + more, squares + more_squares
    result = 2.0 * values * lax.rsqrt(squares / (columns * dp) + EPS)
    for adapter in range(local):
        out_ref[adapter, 0] = result[adapter * MOST : (adapter + 1) * MOST]


def finish(values, squares, gain, shrink, arrived):
    local, rank, _ = shrink.shape
    return pl.pallas_call(
        finish_kernel,
        out_shape=jax.ShapeDtypeStruct((local, 1, MOST, rank), F32),
        in_specs=[whole()] * (4 + len(arrived)),
        out_specs=whole(),
        compiler_params=pltpu.CompilerParams(vmem_limit_bytes=8 * MIB),
        name="finish",
    )(values, squares, gain, shrink, *arrived)


def shifted(array, axis, shift):
    count = lax.axis_size(axis)
    return lax.ppermute(array, axis, [(i, (i + shift) % count) for i in range(count)])


def across(array, receivers):
    sections = lax.axis_size("section")
    pairs = [
        (i * sections + s, j * sections + (s + 1) % sections)
        for i, j in enumerate(receivers)
        for s in range(sections)
    ]
    return lax.ppermute(array, ("tensor", "section"), pairs)


def body(hidden, down_matrix, residual, next_norm_scale, shrink_matrix, adapter_index):
    dp, tensors, sections = (lax.axis_size(axis) for axis in ("dp", "tensor", "section"))
    depth, _ = down_matrix.shape
    local = shrink_matrix.shape[0]

    others = jnp.stack([shifted(hidden, "dp", shift) for shift in range(1, dp)])

    step = step_of(depth)
    blocks = depth // step
    held_count = max(1, min(blocks // 2, HELD_BYTES // (2 * step * down_matrix.shape[1])))
    held = fetch(down_matrix, held_count, step)

    shrink = jnp.swapaxes(shrink_matrix, 1, 2)
    gain = next_norm_scale[None, :]

    in_vmem = [pltpu.with_memory_space_constraint(x, pltpu.VMEM) for x in (hidden, others, held)]
    total, sent = project(*in_vmem, down_matrix, tensors, sections)
    index, total = lax.optimization_barrier((adapter_index.reshape(1, -1), total))
    kept = keep(total, tensors, sections)
    places, shrink = prepare(index, shrink, local * MOST, dp)
    arrived = [shifted(sent[s - 1], "section", s) for s in range(1, sections)]
    plan = exchange_plan(tensors)
    own, *sums = pair(kept, arrived, plan, tensors)
    arrived = [across(x, receivers) for x, receivers in zip(sums, plan)]
    mixed, routed, leaving = mix(residual, places, own, arrived, local * MOST, dp)
    arrived = [shifted(leaving[s - 1], "dp", s) for s in range(1, dp)]
    values, squares = own_half(routed, gain, shrink)
    shrunk = finish(values, squares, gain, shrink, arrived)
    return (mixed, shrunk)


def solution(mesh):
    placed = (
        P(("groups", "dp"), ("tensor", "section")),
        P(("tensor", "section"), "dp"),
        P(("groups", "tensor", "section"), "dp"),
        P(),
        P("dp", None, None),
        P(("groups", "tensor", "section"), None),
    )
    return jax.shard_map(
        body,
        mesh=mesh,
        in_specs=placed,
        out_specs=(
            P(("groups", "tensor", "section"), "dp"),
            P("dp", ("groups", "tensor", "section"), None, None),
        ),
        check_vma=False,
    )
```

```python
import functools

import jax
import jax.numpy as jnp
from jax import lax
from jax.experimental import pallas as pl
from jax.experimental.pallas import tpu as pltpu
from jax.sharding import PartitionSpec as P

MOST = 2
EPS = 1e-05
DEPTH_STEP = 512
HELD_BYTES = 21 * 2**20
WIDTH = 1024
MIB = 2**20
F32 = jnp.float32
BF16 = jnp.bfloat16


def whole():
    return pl.BlockSpec(memory_space=pltpu.VMEM)


def step_of(depth):
    return max(s for s in range(16, DEPTH_STEP + 1, 16) if depth % s == 0)


def fetch_kernel(weight_ref, held_ref, sem):
    copy = pltpu.make_async_copy(
        weight_ref.at[pl.ds(0, held_ref.shape[0]), :], held_ref, sem
    )
    copy.start()
    copy.wait()


def fetch(weight, rows):
    columns = weight.shape[1]
    return pl.pallas_call(
        fetch_kernel,
        out_shape=pltpu.VMEM((rows, columns), weight.dtype),
        in_specs=[pl.BlockSpec(memory_space=pl.ANY)],
        out_specs=whole(),
        scratch_shapes=[pltpu.SemaphoreType.DMA],
        compiler_params=pltpu.CompilerParams(vmem_limit_bytes=1 * MIB),
        cost_estimate=pl.CostEstimate(
            flops=0, bytes_accessed=2 * rows * columns, transcendentals=0
        ),
        name="fetch",
    )(weight)


def last_parts(step):
    if step % 64:
        return [(0, step)]
    return [(0, step // 2), (step // 2, step // 4), (step // 4 * 3, step // 4)]


def project_kernel(
    own_ref,
    others_ref,
    held_ref,
    weight_ref,
    total_ref,
    sent_ref,
    rows_ref,
    rest_ref,
    sems,
    *,
    tensors,
    sections,
):
    rest, step, columns = rest_ref.shape
    held = held_ref.shape[0] // step
    own_rows = own_ref.shape[0]
    dp = 1 + others_ref.shape[0]
    me = lax.axis_index("dp")
    width = min(columns, WIDTH)

    def copy_of(i, sem, first=0, size=step):
        return pltpu.make_async_copy(
            weight_ref.at[pl.ds((held + i) * step + first, size), :],
            rest_ref.at[i, pl.ds(first, size), :],
            sems.at[sem],
        )

    parts = last_parts(step)
    last = [copy_of(rest - 1, rest - 1 + k, *part) for k, part in enumerate(parts)]
    for i in range(rest - 1):
        copy_of(i, i).start()
    for copy in last:
        copy.start()

    for i in range(held + rest):
        block = slice(i * step, (i + 1) * step)
        for shift in range(dp):
            first = pl.multiple_of((me + dp - shift) % dp * own_rows, own_rows)
            source = own_ref[:, block] if shift == 0 else others_ref[shift - 1, :, block]
            rows_ref[i, pl.ds(first, own_rows), :] = source

    def held_step(n, _):
        lanes = pl.ds(pl.multiple_of(n * width, width), width)
        total_ref[:, lanes] = sum(
            jnp.dot(
                rows_ref[i], held_ref[i * step : (i + 1) * step, lanes], preferred_element_type=F32
            )
            for i in range(held)
        )
        return 0

    def add(i, part=slice(None)):
        for n in range(0, columns, width):
            lanes = slice(n, n + width)
            total_ref[:, lanes] += jnp.dot(
                rows_ref[held + i, :, part], rest_ref[i, part, lanes], preferred_element_type=F32
            )

    def rest_step(i, _):
        copy_of(i, i).wait()
        add(i)
        return 0

    lax.fori_loop(0, columns // width, held_step, 0)
    lax.fori_loop(0, rest - 1, rest_step, 0)
    for copy, (first, size) in zip(last, parts):
        copy.wait()
        add(rest - 1, slice(first, first + size))

    for turn in range(1, sections):
        for n in range(0, columns, width):
            lanes = slice(n, n + width)
            rows = rows_of(turn, total_ref, lanes, tensors, sections)
            sent_ref[turn - 1, :, lanes] = rows.astype(BF16)


def rows_of(turn, total_ref, lanes, tensors, sections):
    tensor, section = lax.axis_index("tensor"), lax.axis_index("section")
    block_rows = total_ref.shape[0] // (tensors * sections)
    group = sections * block_rows
    blocks = []
    for k in range(tensors):
        first = pl.multiple_of(partner_of(tensor, k, tensors) * group, group)
        rows = total_ref[pl.ds(first, group), lanes]
        rows = pltpu.roll(rows, (sections - section) % sections * block_rows, 0)
        part = (turn + (k > 0)) % sections
        blocks.append(rows[part * block_rows : (part + 1) * block_rows])
    return jnp.concatenate(blocks, axis=0)


def keep_kernel(total_ref, kept_ref, *, tensors, sections):
    columns = total_ref.shape[1]
    width = min(columns, WIDTH)
    for n in range(0, columns, width):
        lanes = slice(n, n + width)
        kept_ref[:, lanes] = rows_of(0, total_ref, lanes, tensors, sections)


def keep(total, tensors, sections):
    rows, columns = total.shape
    return pl.pallas_call(
        functools.partial(keep_kernel, tensors=tensors, sections=sections),
        out_shape=jax.ShapeDtypeStruct((rows // sections, columns), F32),
        in_specs=[whole()],
        out_specs=whole(),
        compiler_params=pltpu.CompilerParams(vmem_limit_bytes=4 * MIB),
        name="keep",
    )(total)


def project(own, others, held, weight, tensors, sections):
    own_rows, depth = own.shape
    rows = own_rows * (1 + others.shape[0])
    columns = weight.shape[1]
    step = step_of(depth)
    rest = (depth - held.shape[0]) // step
    return pl.pallas_call(
        functools.partial(project_kernel, tensors=tensors, sections=sections),
        out_shape=(
            pltpu.VMEM((rows, columns), F32),
            pltpu.VMEM((sections - 1, rows // sections, columns), BF16),
        ),
        in_specs=[whole(), whole(), whole(), pl.BlockSpec(memory_space=pl.ANY)],
        out_specs=(whole(), whole()),
        scratch_shapes=[
            pltpu.VMEM((depth // step, rows, step), BF16),
            pltpu.VMEM((rest, step, columns), BF16),
            pltpu.SemaphoreType.DMA((rest - 1 + len(last_parts(step)),)),
        ],
        compiler_params=pltpu.CompilerParams(vmem_limit_bytes=36 * MIB),
        cost_estimate=pl.CostEstimate(
            flops=2 * rows * depth * columns,
            bytes_accessed=2 * rest * step * columns,
            transcendentals=0,
        ),
        name="project",
    )(own, others, held, weight)


def partner_of(me, turn, count):
    if count & (count - 1) == 0:
        return me ^ turn
    return (me + turn) % count


def turn_of(me, partner, count):
    if count & (count - 1) == 0:
        return me ^ partner
    return (partner - me) % count


def exchange_plan(count):
    if count == 4:
        return [(2, 3, 1, 0), (3, 2, 0, 1), (1, 0, 3, 2)]
    turns = range(count - 1, 0, -1)
    return [tuple(partner_of(i, turn, count) for i in range(count)) for turn in turns]


def pair_kernel(kept_ref, *refs, plan, tensors):
    arrived, (own_ref, *outs) = refs[: -1 - len(plan)], refs[-1 - len(plan) :]
    me = lax.axis_index("tensor")
    block_rows = own_ref.shape[0]
    total = kept_ref[...]
    for piece in arrived:
        total = total + piece[...].astype(F32)
    blocks = [total[turn * block_rows : (turn + 1) * block_rows] for turn in range(tensors)]
    own_ref[...] = blocks[0]
    for receivers, out_ref in zip(plan, outs):
        turns = [turn_of(i, j, tensors) for i, j in enumerate(receivers)]
        block = blocks[turns[0]]
        for i, turn in enumerate(turns):
            if turn != turns[0]:
                block = jnp.where(me == i, blocks[turn], block)
        out_ref[...] = block.astype(out_ref.dtype)


def pair(kept, arrived, plan, tensors):
    rows, columns = kept.shape
    block = (rows // tensors, columns)
    return pl.pallas_call(
        functools.partial(pair_kernel, plan=plan, tensors=tensors),
        out_shape=[jax.ShapeDtypeStruct(block, F32)] + [jax.ShapeDtypeStruct(block, BF16)] * len(plan),
        in_specs=[whole()] * (1 + len(arrived)),
        out_specs=[whole()] * (1 + len(plan)),
        compiler_params=pltpu.CompilerParams(vmem_limit_bytes=8 * MIB),
        name="pair",
    )(kept, *arrived)


def places_of(row, slots, owners, local):
    rows = row.shape[1]
    upper = lax.broadcasted_iota(jnp.int32, (rows, rows), 0)
    lower = lax.broadcasted_iota(jnp.int32, (rows, rows), 1)
    column = jnp.sum(jnp.where(upper == lower, row, 0), axis=1, keepdims=True)
    before = jnp.logical_and(column == row, upper < lower)
    rank_of = jnp.sum(before.astype(jnp.int32), axis=0, keepdims=True)
    slot = lax.broadcasted_iota(jnp.int32, (slots * owners, rows), 0)
    owner = (lax.axis_index("dp") + slot // slots) % owners
    adapter = owner * local + slot // MOST % local
    return jnp.logical_and(row == adapter, rank_of == slot % MOST).astype(F32)


def prepare_kernel(index_ref, shrink_ref, places_ref, out_ref, sem, *, slots, owners):
    copy = pltpu.make_async_copy(shrink_ref, out_ref, sem)
    copy.start()
    places_ref[...] = places_of(index_ref[...], slots, owners, slots // MOST)
    copy.wait()


def prepare(index, shrink, slots, owners):
    return pl.pallas_call(
        functools.partial(prepare_kernel, slots=slots, owners=owners),
        out_shape=(
            jax.ShapeDtypeStruct((slots * owners, index.shape[1]), F32),
            pltpu.VMEM(shrink.shape, shrink.dtype),
        ),
        in_specs=[whole(), pl.BlockSpec(memory_space=pl.ANY)],
        out_specs=(whole(), whole()),
        scratch_shapes=[pltpu.SemaphoreType.DMA],
        compiler_params=pltpu.CompilerParams(vmem_limit_bytes=1 * MIB),
        name="prepare",
    )(index, pltpu.with_memory_space_constraint(shrink, pltpu.HBM))


def mix_kernel(residual_ref, places_ref, own_ref, *refs):
    arrived, (mixed_ref, kept_ref, sent_ref) = refs[:-3], refs[-3:]
    slots = kept_ref.shape[0]
    places = places_ref[...]
    total = own_ref[...] + residual_ref[...].astype(F32)
    for piece in arrived:
        total = total + piece[...].astype(F32)
    mixed = total.astype(BF16)
    mixed_ref[...] = mixed
    widened = mixed.astype(F32)
    routed = sum(
        places[:, row : row + 1] * widened[row : row + 1, :] for row in range(widened.shape[0])
    )
    kept_ref[...] = routed[:slots]
    for turn in range(sent_ref.shape[0]):
        sent_ref[turn] = routed[(turn + 1) * slots : (turn + 2) * slots].astype(BF16)


def mix(residual, places, own, arrived, slots, owners):
    rows, columns = residual.shape
    return pl.pallas_call(
        mix_kernel,
        out_shape=(
            pltpu.VMEM((rows, columns), BF16),
            jax.ShapeDtypeStruct((slots, columns), F32),
            jax.ShapeDtypeStruct((owners - 1, slots, columns), BF16),
        ),
        in_specs=[whole()] * (3 + len(arrived)),
        out_specs=(whole(),) * 3,
        compiler_params=pltpu.CompilerParams(vmem_limit_bytes=8 * MIB),
        name="mix",
    )(residual, places, own, *arrived)


def partial_values(rows, gain_ref, shrink_ref, place, columns, local):
    first = pl.multiple_of(place * columns, columns)
    squares = jnp.sum(rows * rows, axis=1, keepdims=True)
    scaled = rows * gain_ref[:, pl.ds(first, columns)].astype(F32)
    high = scaled.astype(BF16)
    low = (scaled - high.astype(F32)).astype(BF16)
    values = []
    for adapter in range(local):
        mine = slice(adapter * MOST, (adapter + 1) * MOST)
        both = jnp.concatenate([high[mine], low[mine]], axis=0)
        product = lax.dot_general(
            both,
            shrink_ref[adapter, :, pl.ds(first, columns)],
            (((1,), (1,)), ((), ())),
            preferred_element_type=F32,
        )
        values.append(product[:MOST] + product[MOST:])
    return jnp.concatenate(values, axis=0), squares


def own_half_kernel(rows_ref, gain_ref, shrink_ref, values_ref, squares_ref):
    columns = rows_ref.shape[1]
    values, squares = partial_values(
        rows_ref[...], gain_ref, shrink_ref, lax.axis_index("dp"), columns, shrink_ref.shape[0]
    )
    values_ref[...] = values
    squares_ref[...] = jnp.broadcast_to(squares, squares_ref.shape)


def own_half(rows, gain, shrink):
    slots = rows.shape[0]
    rank = shrink.shape[1]
    return pl.pallas_call(
        own_half_kernel,
        out_shape=(
            jax.ShapeDtypeStruct((slots, rank), F32),
            jax.ShapeDtypeStruct((slots, rank), F32),
        ),
        in_specs=[whole()] * 3,
        out_specs=(whole(),) * 2,
        compiler_params=pltpu.CompilerParams(vmem_limit_bytes=8 * MIB),
        cost_estimate=pl.CostEstimate(
            flops=2 * slots * rows.shape[1] * rank, bytes_accessed=2 * MIB, transcendentals=0
        ),
        name="own_half",
    )(rows, gain, shrink)


def finish_kernel(values_ref, squares_ref, gain_ref, shrink_ref, *refs):
    arrived, out_ref = refs[:-1], refs[-1]
    dp = 1 + len(arrived)
    me = lax.axis_index("dp")
    local = shrink_ref.shape[0]
    columns = arrived[0].shape[1]
    values, squares = values_ref[...], squares_ref[:, :1]
    for shift, piece in enumerate(arrived, start=1):
        more, more_squares = partial_values(
            piece[...].astype(F32),
            gain_ref,
            shrink_ref,
            lax.rem(me + dp - shift, dp),
            columns,
            local,
        )
        values, squares = values + more, squares + more_squares
    result = 2.0 * values * lax.rsqrt(squares / (columns * dp) + EPS)
    for adapter in range(local):
        out_ref[adapter, 0] = result[adapter * MOST : (adapter + 1) * MOST]


def finish(values, squares, gain, shrink, arrived):
    local, rank, _ = shrink.shape
    return pl.pallas_call(
        finish_kernel,
        out_shape=jax.ShapeDtypeStruct((local, 1, MOST, rank), F32),
        in_specs=[whole()] * (4 + len(arrived)),
        out_specs=whole(),
        compiler_params=pltpu.CompilerParams(vmem_limit_bytes=8 * MIB),
        name="finish",
    )(values, squares, gain, shrink, *arrived)


def shifted(array, axis, shift):
    count = lax.axis_size(axis)
    return lax.ppermute(array, axis, [(i, (i + shift) % count) for i in range(count)])


def across(array, receivers):
    sections = lax.axis_size("section")
    pairs = [
        (i * sections + s, j * sections + (s + 1) % sections)
        for i, j in enumerate(receivers)
        for s in range(sections)
    ]
    return lax.ppermute(array, ("tensor", "section"), pairs)


def body(hidden, down_matrix, residual, next_norm_scale, shrink_matrix, adapter_index):
    dp, tensors, sections = (lax.axis_size(axis) for axis in ("dp", "tensor", "section"))
    depth, _ = down_matrix.shape
    local = shrink_matrix.shape[0]

    others = jnp.stack([shifted(hidden, "dp", shift) for shift in range(1, dp)])

    step = step_of(depth)
    blocks = depth // step
    held_count = max(1, min(blocks // 2, HELD_BYTES // (2 * step * down_matrix.shape[1])))
    held = fetch(down_matrix, held_count * step)

    shrink = jnp.swapaxes(shrink_matrix, 1, 2)
    gain = next_norm_scale[None, :]

    in_vmem = [pltpu.with_memory_space_constraint(x, pltpu.VMEM) for x in (hidden, others, held)]
    total, sent = project(*in_vmem, down_matrix, tensors, sections)
    index, total = lax.optimization_barrier((adapter_index.reshape(1, -1), total))
    kept = keep(total, tensors, sections)
    places, shrink = prepare(index, shrink, local * MOST, dp)
    arrived = [shifted(sent[s - 1], "section", s) for s in range(1, sections)]
    plan = exchange_plan(tensors)
    own, *sums = pair(kept, arrived, plan, tensors)
    arrived = [across(x, receivers) for x, receivers in zip(sums, plan)]
    mixed, routed, leaving = mix(residual, places, own, arrived, local * MOST, dp)
    arrived = [shifted(leaving[s - 1], "dp", s) for s in range(1, dp)]
    values, squares = own_half(routed, gain, shrink)
    shrunk = finish(values, squares, gain, shrink, arrived)
    return (mixed, shrunk)


def solution(mesh):
    placed = (
        P(("groups", "dp"), ("tensor", "section")),
        P(("tensor", "section"), "dp"),
        P(("groups", "tensor", "section"), "dp"),
        P(),
        P("dp", None, None),
        P(("groups", "tensor", "section"), None),
    )
    return jax.shard_map(
        body,
        mesh=mesh,
        in_specs=placed,
        out_specs=(
            P(("groups", "tensor", "section"), "dp"),
            P("dp", ("groups", "tensor", "section"), None, None),
        ),
        check_vma=False,
    )
```

```python
import functools

import jax
import jax.numpy as jnp
from jax import lax
from jax.experimental import pallas as pl
from jax.experimental.pallas import tpu as pltpu
from jax.sharding import PartitionSpec as P

MOST = 2
EPS = 1e-05
DEPTH_STEP = 512
HELD_BYTES = 21 * 2**20
WIDTH = 1024
MIB = 2**20
F32 = jnp.float32
BF16 = jnp.bfloat16


def whole():
    return pl.BlockSpec(memory_space=pltpu.VMEM)


def step_of(depth):
    return max(s for s in range(16, DEPTH_STEP + 1, 16) if depth % s == 0)


def fetch_kernel(weight_ref, held_ref, sem):
    copy = pltpu.make_async_copy(
        weight_ref.at[pl.ds(0, held_ref.shape[0]), :], held_ref, sem
    )
    copy.start()
    copy.wait()


def fetch(weight, rows):
    columns = weight.shape[1]
    return pl.pallas_call(
        fetch_kernel,
        out_shape=pltpu.VMEM((rows, columns), weight.dtype),
        in_specs=[pl.BlockSpec(memory_space=pl.ANY)],
        out_specs=whole(),
        scratch_shapes=[pltpu.SemaphoreType.DMA],
        compiler_params=pltpu.CompilerParams(vmem_limit_bytes=1 * MIB),
        cost_estimate=pl.CostEstimate(
            flops=0, bytes_accessed=2 * rows * columns, transcendentals=0
        ),
        name="fetch",
    )(weight)


def last_parts(step):
    if step % 64:
        return [(0, step)]
    return [(0, step // 2), (step // 2, step // 4), (step // 4 * 3, step // 4)]


def project_kernel(
    own_ref,
    others_ref,
    held_ref,
    weight_ref,
    total_ref,
    sent_ref,
    rows_ref,
    rest_ref,
    sems,
    *,
    tensors,
    sections,
):
    rest, step, columns = rest_ref.shape
    held = held_ref.shape[0] // step
    own_rows = own_ref.shape[0]
    dp = 1 + others_ref.shape[0]
    me = lax.axis_index("dp")
    width = min(columns, WIDTH)

    def copy_of(i, sem, first=0, size=step):
        return pltpu.make_async_copy(
            weight_ref.at[pl.ds((held + i) * step + first, size), :],
            rest_ref.at[i, pl.ds(first, size), :],
            sems.at[sem],
        )

    parts = last_parts(step)
    last = [copy_of(rest - 1, rest - 1 + k, *part) for k, part in enumerate(parts)]
    steps = columns // width
    early = rest - 1 - steps if rest > steps else rest - 1
    for i in range(early):
        copy_of(i, i).start()

    for i in range(held + rest):
        block = slice(i * step, (i + 1) * step)
        for shift in range(dp):
            first = pl.multiple_of((me + dp - shift) % dp * own_rows, own_rows)
            source = own_ref[:, block] if shift == 0 else others_ref[shift - 1, :, block]
            rows_ref[i, pl.ds(first, own_rows), :] = source

    def held_step(n, _):
        if rest > steps:
            copy_of(early + n, early + n).start()
        lanes = pl.ds(pl.multiple_of(n * width, width), width)
        total_ref[:, lanes] = sum(
            jnp.dot(
                rows_ref[i], held_ref[i * step : (i + 1) * step, lanes], preferred_element_type=F32
            )
            for i in range(held)
        )
        return 0

    def add(i, part=slice(None)):
        for n in range(0, columns, width):
            lanes = slice(n, n + width)
            total_ref[:, lanes] += jnp.dot(
                rows_ref[held + i, :, part], rest_ref[i, part, lanes], preferred_element_type=F32
            )

    def rest_step(i, _):
        copy_of(i, i).wait()
        add(i)
        return 0

    lax.fori_loop(0, steps, held_step, 0)
    for copy in last:
        copy.start()
    lax.fori_loop(0, rest - 1, rest_step, 0)
    for copy, (first, size) in zip(last, parts):
        copy.wait()
        add(rest - 1, slice(first, first + size))

    for turn in range(1, sections):
        for n in range(0, columns, width):
            lanes = slice(n, n + width)
            rows = rows_of(turn, total_ref, lanes, tensors, sections)
            sent_ref[turn - 1, :, lanes] = rows.astype(BF16)


def rows_of(turn, total_ref, lanes, tensors, sections):
    tensor, section = lax.axis_index("tensor"), lax.axis_index("section")
    block_rows = total_ref.shape[0] // (tensors * sections)
    group = sections * block_rows
    blocks = []
    for k in range(tensors):
        first = pl.multiple_of(partner_of(tensor, k, tensors) * group, group)
        rows = total_ref[pl.ds(first, group), lanes]
        rows = pltpu.roll(rows, (sections - section) % sections * block_rows, 0)
        part = (turn + (k > 0)) % sections
        blocks.append(rows[part * block_rows : (part + 1) * block_rows])
    return jnp.concatenate(blocks, axis=0)


def keep_kernel(total_ref, kept_ref, *, tensors, sections):
    columns = total_ref.shape[1]
    width = min(columns, WIDTH)
    for n in range(0, columns, width):
        lanes = slice(n, n + width)
        kept_ref[:, lanes] = rows_of(0, total_ref, lanes, tensors, sections)


def keep(total, tensors, sections):
    rows, columns = total.shape
    return pl.pallas_call(
        functools.partial(keep_kernel, tensors=tensors, sections=sections),
        out_shape=jax.ShapeDtypeStruct((rows // sections, columns), F32),
        in_specs=[whole()],
        out_specs=whole(),
        compiler_params=pltpu.CompilerParams(vmem_limit_bytes=4 * MIB),
        name="keep",
    )(total)


def project(own, others, held, weight, tensors, sections):
    own_rows, depth = own.shape
    rows = own_rows * (1 + others.shape[0])
    columns = weight.shape[1]
    step = step_of(depth)
    rest = (depth - held.shape[0]) // step
    return pl.pallas_call(
        functools.partial(project_kernel, tensors=tensors, sections=sections),
        out_shape=(
            pltpu.VMEM((rows, columns), F32),
            pltpu.VMEM((sections - 1, rows // sections, columns), BF16),
        ),
        in_specs=[whole(), whole(), whole(), pl.BlockSpec(memory_space=pl.ANY)],
        out_specs=(whole(), whole()),
        scratch_shapes=[
            pltpu.VMEM((depth // step, rows, step), BF16),
            pltpu.VMEM((rest, step, columns), BF16),
            pltpu.SemaphoreType.DMA((rest - 1 + len(last_parts(step)),)),
        ],
        compiler_params=pltpu.CompilerParams(vmem_limit_bytes=36 * MIB),
        cost_estimate=pl.CostEstimate(
            flops=2 * rows * depth * columns,
            bytes_accessed=2 * rest * step * columns,
            transcendentals=0,
        ),
        name="project",
    )(own, others, held, weight)


def partner_of(me, turn, count):
    if count & (count - 1) == 0:
        return me ^ turn
    return (me + turn) % count


def turn_of(me, partner, count):
    if count & (count - 1) == 0:
        return me ^ partner
    return (partner - me) % count


def exchange_plan(count):
    if count == 4:
        return [(2, 3, 1, 0), (3, 2, 0, 1), (1, 0, 3, 2)]
    turns = range(count - 1, 0, -1)
    return [tuple(partner_of(i, turn, count) for i in range(count)) for turn in turns]


def pair_kernel(kept_ref, *refs, plan, tensors):
    arrived, (own_ref, *outs) = refs[: -1 - len(plan)], refs[-1 - len(plan) :]
    me = lax.axis_index("tensor")
    block_rows = own_ref.shape[0]
    total = kept_ref[...]
    for piece in arrived:
        total = total + piece[...].astype(F32)
    blocks = [total[turn * block_rows : (turn + 1) * block_rows] for turn in range(tensors)]
    own_ref[...] = blocks[0]
    for receivers, out_ref in zip(plan, outs):
        turns = [turn_of(i, j, tensors) for i, j in enumerate(receivers)]
        block = blocks[turns[0]]
        for i, turn in enumerate(turns):
            if turn != turns[0]:
                block = jnp.where(me == i, blocks[turn], block)
        out_ref[...] = block.astype(out_ref.dtype)


def pair(kept, arrived, plan, tensors):
    rows, columns = kept.shape
    block = (rows // tensors, columns)
    return pl.pallas_call(
        functools.partial(pair_kernel, plan=plan, tensors=tensors),
        out_shape=[jax.ShapeDtypeStruct(block, F32)] + [jax.ShapeDtypeStruct(block, BF16)] * len(plan),
        in_specs=[whole()] * (1 + len(arrived)),
        out_specs=[whole()] * (1 + len(plan)),
        compiler_params=pltpu.CompilerParams(vmem_limit_bytes=8 * MIB),
        name="pair",
    )(kept, *arrived)


def places_of(row, slots, owners, local):
    rows = row.shape[1]
    upper = lax.broadcasted_iota(jnp.int32, (rows, rows), 0)
    lower = lax.broadcasted_iota(jnp.int32, (rows, rows), 1)
    column = jnp.sum(jnp.where(upper == lower, row, 0), axis=1, keepdims=True)
    before = jnp.logical_and(column == row, upper < lower)
    rank_of = jnp.sum(before.astype(jnp.int32), axis=0, keepdims=True)
    slot = lax.broadcasted_iota(jnp.int32, (slots * owners, rows), 0)
    owner = (lax.axis_index("dp") + slot // slots) % owners
    adapter = owner * local + slot // MOST % local
    return jnp.logical_and(row == adapter, rank_of == slot % MOST).astype(F32)


def prepare_kernel(index_ref, shrink_ref, places_ref, out_ref, sem, *, slots, owners):
    copy = pltpu.make_async_copy(shrink_ref, out_ref, sem)
    copy.start()
    places_ref[...] = places_of(index_ref[...], slots, owners, slots // MOST)
    copy.wait()


def prepare(index, shrink, slots, owners):
    return pl.pallas_call(
        functools.partial(prepare_kernel, slots=slots, owners=owners),
        out_shape=(
            jax.ShapeDtypeStruct((slots * owners, index.shape[1]), F32),
            pltpu.VMEM(shrink.shape, shrink.dtype),
        ),
        in_specs=[whole(), pl.BlockSpec(memory_space=pl.ANY)],
        out_specs=(whole(), whole()),
        scratch_shapes=[pltpu.SemaphoreType.DMA],
        compiler_params=pltpu.CompilerParams(vmem_limit_bytes=1 * MIB),
        name="prepare",
    )(index, pltpu.with_memory_space_constraint(shrink, pltpu.HBM))


def mix_kernel(residual_ref, places_ref, own_ref, *refs):
    arrived, (mixed_ref, kept_ref, sent_ref) = refs[:-3], refs[-3:]
    slots = kept_ref.shape[0]
    places = places_ref[...]
    total = own_ref[...] + residual_ref[...].astype(F32)
    for piece in arrived:
        total = total + piece[...].astype(F32)
    mixed = total.astype(BF16)
    mixed_ref[...] = mixed
    widened = mixed.astype(F32)
    routed = sum(
        places[:, row : row + 1] * widened[row : row + 1, :] for row in range(widened.shape[0])
    )
    kept_ref[...] = routed[:slots]
    for turn in range(sent_ref.shape[0]):
        sent_ref[turn] = routed[(turn + 1) * slots : (turn + 2) * slots].astype(BF16)


def mix(residual, places, own, arrived, slots, owners):
    rows, columns = residual.shape
    return pl.pallas_call(
        mix_kernel,
        out_shape=(
            pltpu.VMEM((rows, columns), BF16),
            jax.ShapeDtypeStruct((slots, columns), F32),
            jax.ShapeDtypeStruct((owners - 1, slots, columns), BF16),
        ),
        in_specs=[whole()] * (3 + len(arrived)),
        out_specs=(whole(),) * 3,
        compiler_params=pltpu.CompilerParams(vmem_limit_bytes=8 * MIB),
        name="mix",
    )(residual, places, own, *arrived)


def partial_values(rows, gain_ref, shrink_ref, place, columns, local):
    first = pl.multiple_of(place * columns, columns)
    squares = jnp.sum(rows * rows, axis=1, keepdims=True)
    scaled = rows * gain_ref[:, pl.ds(first, columns)].astype(F32)
    high = scaled.astype(BF16)
    low = (scaled - high.astype(F32)).astype(BF16)
    values = []
    for adapter in range(local):
        mine = slice(adapter * MOST, (adapter + 1) * MOST)
        both = jnp.concatenate([high[mine], low[mine]], axis=0)
        product = lax.dot_general(
            both,
            shrink_ref[adapter, :, pl.ds(first, columns)],
            (((1,), (1,)), ((), ())),
            preferred_element_type=F32,
        )
        values.append(product[:MOST] + product[MOST:])
    return jnp.concatenate(values, axis=0), squares


def own_half_kernel(rows_ref, gain_ref, shrink_ref, values_ref, squares_ref):
    columns = rows_ref.shape[1]
    values, squares = partial_values(
        rows_ref[...], gain_ref, shrink_ref, lax.axis_index("dp"), columns, shrink_ref.shape[0]
    )
    values_ref[...] = values
    squares_ref[...] = jnp.broadcast_to(squares, squares_ref.shape)


def own_half(rows, gain, shrink):
    slots = rows.shape[0]
    rank = shrink.shape[1]
    return pl.pallas_call(
        own_half_kernel,
        out_shape=(
            jax.ShapeDtypeStruct((slots, rank), F32),
            jax.ShapeDtypeStruct((slots, rank), F32),
        ),
        in_specs=[whole()] * 3,
        out_specs=(whole(),) * 2,
        compiler_params=pltpu.CompilerParams(vmem_limit_bytes=8 * MIB),
        cost_estimate=pl.CostEstimate(
            flops=2 * slots * rows.shape[1] * rank, bytes_accessed=2 * MIB, transcendentals=0
        ),
        name="own_half",
    )(rows, gain, shrink)


def finish_kernel(values_ref, squares_ref, gain_ref, shrink_ref, *refs):
    arrived, out_ref = refs[:-1], refs[-1]
    dp = 1 + len(arrived)
    me = lax.axis_index("dp")
    local = shrink_ref.shape[0]
    columns = arrived[0].shape[1]
    values, squares = values_ref[...], squares_ref[:, :1]
    for shift, piece in enumerate(arrived, start=1):
        more, more_squares = partial_values(
            piece[...].astype(F32),
            gain_ref,
            shrink_ref,
            lax.rem(me + dp - shift, dp),
            columns,
            local,
        )
        values, squares = values + more, squares + more_squares
    result = 2.0 * values * lax.rsqrt(squares / (columns * dp) + EPS)
    for adapter in range(local):
        out_ref[adapter, 0] = result[adapter * MOST : (adapter + 1) * MOST]


def finish(values, squares, gain, shrink, arrived):
    local, rank, _ = shrink.shape
    return pl.pallas_call(
        finish_kernel,
        out_shape=jax.ShapeDtypeStruct((local, 1, MOST, rank), F32),
        in_specs=[whole()] * (4 + len(arrived)),
        out_specs=whole(),
        compiler_params=pltpu.CompilerParams(vmem_limit_bytes=8 * MIB),
        name="finish",
    )(values, squares, gain, shrink, *arrived)


def shifted(array, axis, shift):
    count = lax.axis_size(axis)
    return lax.ppermute(array, axis, [(i, (i + shift) % count) for i in range(count)])


def across(array, receivers):
    sections = lax.axis_size("section")
    pairs = [
        (i * sections + s, j * sections + (s + 1) % sections)
        for i, j in enumerate(receivers)
        for s in range(sections)
    ]
    return lax.ppermute(array, ("tensor", "section"), pairs)


def body(hidden, down_matrix, residual, next_norm_scale, shrink_matrix, adapter_index):
    dp, tensors, sections = (lax.axis_size(axis) for axis in ("dp", "tensor", "section"))
    depth, _ = down_matrix.shape
    local = shrink_matrix.shape[0]

    others = jnp.stack([shifted(hidden, "dp", shift) for shift in range(1, dp)])

    step = step_of(depth)
    blocks = depth // step
    held_count = max(1, min(blocks // 2, HELD_BYTES // (2 * step * down_matrix.shape[1])))
    held = fetch(down_matrix, held_count * step)

    shrink = jnp.swapaxes(shrink_matrix, 1, 2)
    gain = next_norm_scale[None, :]

    in_vmem = [pltpu.with_memory_space_constraint(x, pltpu.VMEM) for x in (hidden, others, held)]
    total, sent = project(*in_vmem, down_matrix, tensors, sections)
    index, total = lax.optimization_barrier((adapter_index.reshape(1, -1), total))
    kept = keep(total, tensors, sections)
    places, shrink = prepare(index, shrink, local * MOST, dp)
    arrived = [shifted(sent[s - 1], "section", s) for s in range(1, sections)]
    plan = exchange_plan(tensors)
    own, *sums = pair(kept, arrived, plan, tensors)
    arrived = [across(x, receivers) for x, receivers in zip(sums, plan)]
    mixed, routed, leaving = mix(residual, places, own, arrived, local * MOST, dp)
    arrived = [shifted(leaving[s - 1], "dp", s) for s in range(1, dp)]
    values, squares = own_half(routed, gain, shrink)
    shrunk = finish(values, squares, gain, shrink, arrived)
    return (mixed, shrunk)


def solution(mesh):
    placed = (
        P(("groups", "dp"), ("tensor", "section")),
        P(("tensor", "section"), "dp"),
        P(("groups", "tensor", "section"), "dp"),
        P(),
        P("dp", None, None),
        P(("groups", "tensor", "section"), None),
    )
    return jax.shard_map(
        body,
        mesh=mesh,
        in_specs=placed,
        out_specs=(
            P(("groups", "tensor", "section"), "dp"),
            P("dp", ("groups", "tensor", "section"), None, None),
        ),
        check_vma=False,
    )
```

```python
import functools

import jax
import jax.numpy as jnp
from jax import lax
from jax.experimental import pallas as pl
from jax.experimental.pallas import tpu as pltpu
from jax.sharding import PartitionSpec as P

MOST = 2
EPS = 1e-05
DEPTH_STEP = 512
HELD_BYTES = 21 * 2**20
WIDTH = 2048
MIB = 2**20
F32 = jnp.float32
BF16 = jnp.bfloat16


def whole():
    return pl.BlockSpec(memory_space=pltpu.VMEM)


def step_of(depth):
    return max(s for s in range(16, DEPTH_STEP + 1, 16) if depth % s == 0)


def fetch_kernel(weight_ref, held_ref, sem):
    copy = pltpu.make_async_copy(
        weight_ref.at[pl.ds(0, held_ref.shape[0]), :], held_ref, sem
    )
    copy.start()
    copy.wait()


def fetch(weight, rows):
    columns = weight.shape[1]
    return pl.pallas_call(
        fetch_kernel,
        out_shape=pltpu.VMEM((rows, columns), weight.dtype),
        in_specs=[pl.BlockSpec(memory_space=pl.ANY)],
        out_specs=whole(),
        scratch_shapes=[pltpu.SemaphoreType.DMA],
        compiler_params=pltpu.CompilerParams(vmem_limit_bytes=1 * MIB),
        cost_estimate=pl.CostEstimate(
            flops=0, bytes_accessed=2 * rows * columns, transcendentals=0
        ),
        name="fetch",
    )(weight)


def last_parts(step):
    if step % 64:
        return [(0, step)]
    return [(0, step // 2), (step // 2, step // 4), (step // 4 * 3, step // 4)]


def project_kernel(
    own_ref,
    others_ref,
    held_ref,
    weight_ref,
    total_ref,
    sent_ref,
    rows_ref,
    rest_ref,
    sems,
    *,
    tensors,
    sections,
):
    rest, step, columns = rest_ref.shape
    held = held_ref.shape[0] // step
    own_rows = own_ref.shape[0]
    dp = 1 + others_ref.shape[0]
    me = lax.axis_index("dp")
    width = min(columns, WIDTH)

    def copy_of(i, sem, first=0, size=step):
        return pltpu.make_async_copy(
            weight_ref.at[pl.ds((held + i) * step + first, size), :],
            rest_ref.at[i, pl.ds(first, size), :],
            sems.at[sem],
        )

    parts = last_parts(step)
    last = [copy_of(rest - 1, rest - 1 + k, *part) for k, part in enumerate(parts)]
    for i in range(rest - 1):
        copy_of(i, i).start()
    for copy in last:
        copy.start()

    for i in range(held + rest):
        block = slice(i * step, (i + 1) * step)
        for shift in range(dp):
            first = pl.multiple_of((me + dp - shift) % dp * own_rows, own_rows)
            source = own_ref[:, block] if shift == 0 else others_ref[shift - 1, :, block]
            rows_ref[i, pl.ds(first, own_rows), :] = source

    def held_step(n, _):
        lanes = pl.ds(pl.multiple_of(n * width, width), width)
        total_ref[:, lanes] = sum(
            jnp.dot(
                rows_ref[i], held_ref[i * step : (i + 1) * step, lanes], preferred_element_type=F32
            )
            for i in range(held)
        )
        return 0

    def add(i, part=slice(None)):
        for n in range(0, columns, width):
            lanes = slice(n, n + width)
            total_ref[:, lanes] += jnp.dot(
                rows_ref[held + i, :, part], rest_ref[i, part, lanes], preferred_element_type=F32
            )

    def rest_step(i, _):
        copy_of(i, i).wait()
        add(i)
        return 0

    lax.fori_loop(0, columns // width, held_step, 0)
    lax.fori_loop(0, rest - 1, rest_step, 0)
    for copy, (first, size) in zip(last, parts):
        copy.wait()
        add(rest - 1, slice(first, first + size))

    for turn in range(1, sections):
        for n in range(0, columns, width):
            lanes = slice(n, n + width)
            rows = rows_of(turn, total_ref, lanes, tensors, sections)
            sent_ref[turn - 1, :, lanes] = rows.astype(BF16)


def rows_of(turn, total_ref, lanes, tensors, sections):
    tensor, section = lax.axis_index("tensor"), lax.axis_index("section")
    block_rows = total_ref.shape[0] // (tensors * sections)
    group = sections * block_rows
    blocks = []
    for k in range(tensors):
        first = pl.multiple_of(partner_of(tensor, k, tensors) * group, group)
        rows = total_ref[pl.ds(first, group), lanes]
        rows = pltpu.roll(rows, (sections - section) % sections * block_rows, 0)
        part = (turn + (k > 0)) % sections
        blocks.append(rows[part * block_rows : (part + 1) * block_rows])
    return jnp.concatenate(blocks, axis=0)


def keep_kernel(total_ref, kept_ref, *, tensors, sections):
    columns = total_ref.shape[1]
    width = min(columns, WIDTH)
    for n in range(0, columns, width):
        lanes = slice(n, n + width)
        kept_ref[:, lanes] = rows_of(0, total_ref, lanes, tensors, sections)


def keep(total, tensors, sections):
    rows, columns = total.shape
    return pl.pallas_call(
        functools.partial(keep_kernel, tensors=tensors, sections=sections),
        out_shape=jax.ShapeDtypeStruct((rows // sections, columns), F32),
        in_specs=[whole()],
        out_specs=whole(),
        compiler_params=pltpu.CompilerParams(vmem_limit_bytes=4 * MIB),
        name="keep",
    )(total)


def project(own, others, held, weight, tensors, sections):
    own_rows, depth = own.shape
    rows = own_rows * (1 + others.shape[0])
    columns = weight.shape[1]
    step = step_of(depth)
    rest = (depth - held.shape[0]) // step
    return pl.pallas_call(
        functools.partial(project_kernel, tensors=tensors, sections=sections),
        out_shape=(
            pltpu.VMEM((rows, columns), F32),
            pltpu.VMEM((sections - 1, rows // sections, columns), BF16),
        ),
        in_specs=[whole(), whole(), whole(), pl.BlockSpec(memory_space=pl.ANY)],
        out_specs=(whole(), whole()),
        scratch_shapes=[
            pltpu.VMEM((depth // step, rows, step), BF16),
            pltpu.VMEM((rest, step, columns), BF16),
            pltpu.SemaphoreType.DMA((rest - 1 + len(last_parts(step)),)),
        ],
        compiler_params=pltpu.CompilerParams(vmem_limit_bytes=36 * MIB),
        cost_estimate=pl.CostEstimate(
            flops=2 * rows * depth * columns,
            bytes_accessed=2 * rest * step * columns,
            transcendentals=0,
        ),
        name="project",
    )(own, others, held, weight)


def partner_of(me, turn, count):
    if count & (count - 1) == 0:
        return me ^ turn
    return (me + turn) % count


def turn_of(me, partner, count):
    if count & (count - 1) == 0:
        return me ^ partner
    return (partner - me) % count


def exchange_plan(count):
    if count == 4:
        return [(2, 3, 1, 0), (3, 2, 0, 1), (1, 0, 3, 2)]
    turns = range(count - 1, 0, -1)
    return [tuple(partner_of(i, turn, count) for i in range(count)) for turn in turns]


def pair_kernel(kept_ref, *refs, plan, tensors):
    arrived, (own_ref, *outs) = refs[: -1 - len(plan)], refs[-1 - len(plan) :]
    me = lax.axis_index("tensor")
    block_rows = own_ref.shape[0]
    total = kept_ref[...]
    for piece in arrived:
        total = total + piece[...].astype(F32)
    blocks = [total[turn * block_rows : (turn + 1) * block_rows] for turn in range(tensors)]
    own_ref[...] = blocks[0]
    for receivers, out_ref in zip(plan, outs):
        turns = [turn_of(i, j, tensors) for i, j in enumerate(receivers)]
        block = blocks[turns[0]]
        for i, turn in enumerate(turns):
            if turn != turns[0]:
                block = jnp.where(me == i, blocks[turn], block)
        out_ref[...] = block.astype(out_ref.dtype)


def pair(kept, arrived, plan, tensors):
    rows, columns = kept.shape
    block = (rows // tensors, columns)
    return pl.pallas_call(
        functools.partial(pair_kernel, plan=plan, tensors=tensors),
        out_shape=[jax.ShapeDtypeStruct(block, F32)] + [jax.ShapeDtypeStruct(block, BF16)] * len(plan),
        in_specs=[whole()] * (1 + len(arrived)),
        out_specs=[whole()] * (1 + len(plan)),
        compiler_params=pltpu.CompilerParams(vmem_limit_bytes=8 * MIB),
        name="pair",
    )(kept, *arrived)


def places_of(row, slots, owners, local):
    rows = row.shape[1]
    upper = lax.broadcasted_iota(jnp.int32, (rows, rows), 0)
    lower = lax.broadcasted_iota(jnp.int32, (rows, rows), 1)
    column = jnp.sum(jnp.where(upper == lower, row, 0), axis=1, keepdims=True)
    before = jnp.logical_and(column == row, upper < lower)
    rank_of = jnp.sum(before.astype(jnp.int32), axis=0, keepdims=True)
    slot = lax.broadcasted_iota(jnp.int32, (slots * owners, rows), 0)
    owner = (lax.axis_index("dp") + slot // slots) % owners
    adapter = owner * local + slot // MOST % local
    return jnp.logical_and(row == adapter, rank_of == slot % MOST).astype(F32)


def prepare_kernel(index_ref, shrink_ref, places_ref, out_ref, sem, *, slots, owners):
    copy = pltpu.make_async_copy(shrink_ref, out_ref, sem)
    copy.start()
    places_ref[...] = places_of(index_ref[...], slots, owners, slots // MOST)
    copy.wait()


def prepare(index, shrink, slots, owners):
    return pl.pallas_call(
        functools.partial(prepare_kernel, slots=slots, owners=owners),
        out_shape=(
            jax.ShapeDtypeStruct((slots * owners, index.shape[1]), F32),
            pltpu.VMEM(shrink.shape, shrink.dtype),
        ),
        in_specs=[whole(), pl.BlockSpec(memory_space=pl.ANY)],
        out_specs=(whole(), whole()),
        scratch_shapes=[pltpu.SemaphoreType.DMA],
        compiler_params=pltpu.CompilerParams(vmem_limit_bytes=1 * MIB),
        name="prepare",
    )(index, pltpu.with_memory_space_constraint(shrink, pltpu.HBM))


def mix_kernel(residual_ref, places_ref, own_ref, *refs):
    arrived, (mixed_ref, kept_ref, sent_ref) = refs[:-3], refs[-3:]
    slots = kept_ref.shape[0]
    places = places_ref[...]
    total = own_ref[...] + residual_ref[...].astype(F32)
    for piece in arrived:
        total = total + piece[...].astype(F32)
    mixed = total.astype(BF16)
    mixed_ref[...] = mixed
    widened = mixed.astype(F32)
    routed = sum(
        places[:, row : row + 1] * widened[row : row + 1, :] for row in range(widened.shape[0])
    )
    kept_ref[...] = routed[:slots]
    for turn in range(sent_ref.shape[0]):
        sent_ref[turn] = routed[(turn + 1) * slots : (turn + 2) * slots].astype(BF16)


def mix(residual, places, own, arrived, slots, owners):
    rows, columns = residual.shape
    return pl.pallas_call(
        mix_kernel,
        out_shape=(
            pltpu.VMEM((rows, columns), BF16),
            jax.ShapeDtypeStruct((slots, columns), F32),
            jax.ShapeDtypeStruct((owners - 1, slots, columns), BF16),
        ),
        in_specs=[whole()] * (3 + len(arrived)),
        out_specs=(whole(),) * 3,
        compiler_params=pltpu.CompilerParams(vmem_limit_bytes=8 * MIB),
        name="mix",
    )(residual, places, own, *arrived)


def partial_values(rows, gain_ref, shrink_ref, place, columns, local):
    first = pl.multiple_of(place * columns, columns)
    squares = jnp.sum(rows * rows, axis=1, keepdims=True)
    scaled = rows * gain_ref[:, pl.ds(first, columns)].astype(F32)
    high = scaled.astype(BF16)
    low = (scaled - high.astype(F32)).astype(BF16)
    values = []
    for adapter in range(local):
        mine = slice(adapter * MOST, (adapter + 1) * MOST)
        both = jnp.concatenate([high[mine], low[mine]], axis=0)
        product = lax.dot_general(
            both,
            shrink_ref[adapter, :, pl.ds(first, columns)],
            (((1,), (1,)), ((), ())),
            preferred_element_type=F32,
        )
        values.append(product[:MOST] + product[MOST:])
    return jnp.concatenate(values, axis=0), squares


def own_half_kernel(rows_ref, gain_ref, shrink_ref, values_ref, squares_ref):
    columns = rows_ref.shape[1]
    values, squares = partial_values(
        rows_ref[...], gain_ref, shrink_ref, lax.axis_index("dp"), columns, shrink_ref.shape[0]
    )
    values_ref[...] = values
    squares_ref[...] = jnp.broadcast_to(squares, squares_ref.shape)


def own_half(rows, gain, shrink):
    slots = rows.shape[0]
    rank = shrink.shape[1]
    return pl.pallas_call(
        own_half_kernel,
        out_shape=(
            jax.ShapeDtypeStruct((slots, rank), F32),
            jax.ShapeDtypeStruct((slots, rank), F32),
        ),
        in_specs=[whole()] * 3,
        out_specs=(whole(),) * 2,
        compiler_params=pltpu.CompilerParams(vmem_limit_bytes=8 * MIB),
        cost_estimate=pl.CostEstimate(
            flops=2 * slots * rows.shape[1] * rank, bytes_accessed=2 * MIB, transcendentals=0
        ),
        name="own_half",
    )(rows, gain, shrink)


def finish_kernel(values_ref, squares_ref, gain_ref, shrink_ref, *refs):
    arrived, out_ref = refs[:-1], refs[-1]
    dp = 1 + len(arrived)
    me = lax.axis_index("dp")
    local = shrink_ref.shape[0]
    columns = arrived[0].shape[1]
    values, squares = values_ref[...], squares_ref[:, :1]
    for shift, piece in enumerate(arrived, start=1):
        more, more_squares = partial_values(
            piece[...].astype(F32),
            gain_ref,
            shrink_ref,
            lax.rem(me + dp - shift, dp),
            columns,
            local,
        )
        values, squares = values + more, squares + more_squares
    result = 2.0 * values * lax.rsqrt(squares / (columns * dp) + EPS)
    for adapter in range(local):
        out_ref[adapter, 0] = result[adapter * MOST : (adapter + 1) * MOST]


def finish(values, squares, gain, shrink, arrived):
    local, rank, _ = shrink.shape
    return pl.pallas_call(
        finish_kernel,
        out_shape=jax.ShapeDtypeStruct((local, 1, MOST, rank), F32),
        in_specs=[whole()] * (4 + len(arrived)),
        out_specs=whole(),
        compiler_params=pltpu.CompilerParams(vmem_limit_bytes=8 * MIB),
        name="finish",
    )(values, squares, gain, shrink, *arrived)


def shifted(array, axis, shift):
    count = lax.axis_size(axis)
    return lax.ppermute(array, axis, [(i, (i + shift) % count) for i in range(count)])


def across(array, receivers):
    sections = lax.axis_size("section")
    pairs = [
        (i * sections + s, j * sections + (s + 1) % sections)
        for i, j in enumerate(receivers)
        for s in range(sections)
    ]
    return lax.ppermute(array, ("tensor", "section"), pairs)


def body(hidden, down_matrix, residual, next_norm_scale, shrink_matrix, adapter_index):
    dp, tensors, sections = (lax.axis_size(axis) for axis in ("dp", "tensor", "section"))
    depth, _ = down_matrix.shape
    local = shrink_matrix.shape[0]

    others = jnp.stack([shifted(hidden, "dp", shift) for shift in range(1, dp)])

    step = step_of(depth)
    blocks = depth // step
    held_count = max(1, min(blocks // 2, HELD_BYTES // (2 * step * down_matrix.shape[1])))
    held = fetch(down_matrix, held_count * step)

    shrink = jnp.swapaxes(shrink_matrix, 1, 2)
    gain = next_norm_scale[None, :]

    in_vmem = [pltpu.with_memory_space_constraint(x, pltpu.VMEM) for x in (hidden, others, held)]
    total, sent = project(*in_vmem, down_matrix, tensors, sections)
    index, total = lax.optimization_barrier((adapter_index.reshape(1, -1), total))
    kept = keep(total, tensors, sections)
    places, shrink = prepare(index, shrink, local * MOST, dp)
    arrived = [shifted(sent[s - 1], "section", s) for s in range(1, sections)]
    plan = exchange_plan(tensors)
    own, *sums = pair(kept, arrived, plan, tensors)
    arrived = [across(x, receivers) for x, receivers in zip(sums, plan)]
    mixed, routed, leaving = mix(residual, places, own, arrived, local * MOST, dp)
    arrived = [shifted(leaving[s - 1], "dp", s) for s in range(1, dp)]
    values, squares = own_half(routed, gain, shrink)
    shrunk = finish(values, squares, gain, shrink, arrived)
    return (mixed, shrunk)


def solution(mesh):
    placed = (
        P(("groups", "dp"), ("tensor", "section")),
        P(("tensor", "section"), "dp"),
        P(("groups", "tensor", "section"), "dp"),
        P(),
        P("dp", None, None),
        P(("groups", "tensor", "section"), None),
    )
    return jax.shard_map(
        body,
        mesh=mesh,
        in_specs=placed,
        out_specs=(
            P(("groups", "tensor", "section"), "dp"),
            P("dp", ("groups", "tensor", "section"), None, None),
        ),
        check_vma=False,
    )
```

```python
import functools

import jax
import jax.numpy as jnp
from jax import lax
from jax.experimental import pallas as pl
from jax.experimental.pallas import tpu as pltpu
from jax.sharding import PartitionSpec as P

MOST = 2
EPS = 1e-05
DEPTH_STEP = 512
HELD_BYTES = 17 * 2**20
WIDTH = 1024
MIB = 2**20
F32 = jnp.float32
BF16 = jnp.bfloat16


def whole():
    return pl.BlockSpec(memory_space=pltpu.VMEM)


def step_of(depth):
    return max(s for s in range(16, DEPTH_STEP + 1, 16) if depth % s == 0)


def fetch_kernel(weight_ref, held_ref, sem):
    copy = pltpu.make_async_copy(
        weight_ref.at[pl.ds(0, held_ref.shape[0]), :], held_ref, sem
    )
    copy.start()
    copy.wait()


def fetch(weight, rows):
    columns = weight.shape[1]
    return pl.pallas_call(
        fetch_kernel,
        out_shape=pltpu.VMEM((rows, columns), weight.dtype),
        in_specs=[pl.BlockSpec(memory_space=pl.ANY)],
        out_specs=whole(),
        scratch_shapes=[pltpu.SemaphoreType.DMA],
        compiler_params=pltpu.CompilerParams(vmem_limit_bytes=1 * MIB),
        cost_estimate=pl.CostEstimate(
            flops=0, bytes_accessed=2 * rows * columns, transcendentals=0
        ),
        name="fetch",
    )(weight)


def last_parts(step):
    if step % 64:
        return [(0, step)]
    return [(0, step // 2), (step // 2, step // 4), (step // 4 * 3, step // 4)]


def project_kernel(
    own_ref,
    others_ref,
    held_ref,
    weight_ref,
    total_ref,
    sent_ref,
    rows_ref,
    rest_ref,
    sems,
    *,
    tensors,
    sections,
):
    rest, step, columns = rest_ref.shape
    held = held_ref.shape[0] // step
    own_rows = own_ref.shape[0]
    dp = 1 + others_ref.shape[0]
    me = lax.axis_index("dp")
    width = min(columns, WIDTH)

    def copy_of(i, sem, first=0, size=step):
        return pltpu.make_async_copy(
            weight_ref.at[pl.ds((held + i) * step + first, size), :],
            rest_ref.at[i, pl.ds(first, size), :],
            sems.at[sem],
        )

    parts = last_parts(step)
    last = [copy_of(rest - 1, rest - 1 + k, *part) for k, part in enumerate(parts)]
    for i in range(rest - 1):
        copy_of(i, i).start()
    for copy in last:
        copy.start()

    for i in range(held + rest):
        block = slice(i * step, (i + 1) * step)
        for shift in range(dp):
            first = pl.multiple_of((me + dp - shift) % dp * own_rows, own_rows)
            source = own_ref[:, block] if shift == 0 else others_ref[shift - 1, :, block]
            rows_ref[i, pl.ds(first, own_rows), :] = source

    def held_step(n, _):
        lanes = pl.ds(pl.multiple_of(n * width, width), width)
        total_ref[:, lanes] = sum(
            jnp.dot(
                rows_ref[i], held_ref[i * step : (i + 1) * step, lanes], preferred_element_type=F32
            )
            for i in range(held)
        )
        return 0

    def add(i, part=slice(None)):
        for n in range(0, columns, width):
            lanes = slice(n, n + width)
            total_ref[:, lanes] += jnp.dot(
                rows_ref[held + i, :, part], rest_ref[i, part, lanes], preferred_element_type=F32
            )

    def rest_step(i, _):
        copy_of(i, i).wait()
        add(i)
        return 0

    lax.fori_loop(0, columns // width, held_step, 0)
    lax.fori_loop(0, rest - 1, rest_step, 0)
    for copy, (first, size) in zip(last, parts):
        copy.wait()
        add(rest - 1, slice(first, first + size))

    for turn in range(1, sections):
        for n in range(0, columns, width):
            lanes = slice(n, n + width)
            rows = rows_of(turn, total_ref, lanes, tensors, sections)
            sent_ref[turn - 1, :, lanes] = rows.astype(BF16)


def rows_of(turn, total_ref, lanes, tensors, sections):
    tensor, section = lax.axis_index("tensor"), lax.axis_index("section")
    block_rows = total_ref.shape[0] // (tensors * sections)
    group = sections * block_rows
    blocks = []
    for k in range(tensors):
        first = pl.multiple_of(partner_of(tensor, k, tensors) * group, group)
        rows = total_ref[pl.ds(first, group), lanes]
        rows = pltpu.roll(rows, (sections - section) % sections * block_rows, 0)
        part = (turn + (k > 0)) % sections
        blocks.append(rows[part * block_rows : (part + 1) * block_rows])
    return jnp.concatenate(blocks, axis=0)


def keep_kernel(total_ref, kept_ref, *, tensors, sections):
    columns = total_ref.shape[1]
    width = min(columns, WIDTH)
    for n in range(0, columns, width):
        lanes = slice(n, n + width)
        kept_ref[:, lanes] = rows_of(0, total_ref, lanes, tensors, sections)


def keep(total, tensors, sections):
    rows, columns = total.shape
    return pl.pallas_call(
        functools.partial(keep_kernel, tensors=tensors, sections=sections),
        out_shape=jax.ShapeDtypeStruct((rows // sections, columns), F32),
        in_specs=[whole()],
        out_specs=whole(),
        compiler_params=pltpu.CompilerParams(vmem_limit_bytes=4 * MIB),
        name="keep",
    )(total)


def project(own, others, held, weight, tensors, sections):
    own_rows, depth = own.shape
    rows = own_rows * (1 + others.shape[0])
    columns = weight.shape[1]
    step = step_of(depth)
    rest = (depth - held.shape[0]) // step
    return pl.pallas_call(
        functools.partial(project_kernel, tensors=tensors, sections=sections),
        out_shape=(
            pltpu.VMEM((rows, columns), F32),
            pltpu.VMEM((sections - 1, rows // sections, columns), BF16),
        ),
        in_specs=[whole(), whole(), whole(), pl.BlockSpec(memory_space=pl.ANY)],
        out_specs=(whole(), whole()),
        scratch_shapes=[
            pltpu.VMEM((depth // step, rows, step), BF16),
            pltpu.VMEM((rest, step, columns), BF16),
            pltpu.SemaphoreType.DMA((rest - 1 + len(last_parts(step)),)),
        ],
        compiler_params=pltpu.CompilerParams(vmem_limit_bytes=40 * MIB),
        cost_estimate=pl.CostEstimate(
            flops=2 * rows * depth * columns,
            bytes_accessed=2 * rest * step * columns,
            transcendentals=0,
        ),
        name="project",
    )(own, others, held, weight)


def partner_of(me, turn, count):
    if count & (count - 1) == 0:
        return me ^ turn
    return (me + turn) % count


def turn_of(me, partner, count):
    if count & (count - 1) == 0:
        return me ^ partner
    return (partner - me) % count


def exchange_plan(count):
    if count == 4:
        return [(2, 3, 1, 0), (3, 2, 0, 1), (1, 0, 3, 2)]
    turns = range(count - 1, 0, -1)
    return [tuple(partner_of(i, turn, count) for i in range(count)) for turn in turns]


def pair_kernel(kept_ref, *refs, plan, tensors):
    arrived, (own_ref, *outs) = refs[: -1 - len(plan)], refs[-1 - len(plan) :]
    me = lax.axis_index("tensor")
    block_rows = own_ref.shape[0]
    total = kept_ref[...]
    for piece in arrived:
        total = total + piece[...].astype(F32)
    blocks = [total[turn * block_rows : (turn + 1) * block_rows] for turn in range(tensors)]
    own_ref[...] = blocks[0]
    for receivers, out_ref in zip(plan, outs):
        turns = [turn_of(i, j, tensors) for i, j in enumerate(receivers)]
        block = blocks[turns[0]]
        for i, turn in enumerate(turns):
            if turn != turns[0]:
                block = jnp.where(me == i, blocks[turn], block)
        out_ref[...] = block.astype(out_ref.dtype)


def pair(kept, arrived, plan, tensors):
    rows, columns = kept.shape
    block = (rows // tensors, columns)
    return pl.pallas_call(
        functools.partial(pair_kernel, plan=plan, tensors=tensors),
        out_shape=[jax.ShapeDtypeStruct(block, F32)] + [jax.ShapeDtypeStruct(block, BF16)] * len(plan),
        in_specs=[whole()] * (1 + len(arrived)),
        out_specs=[whole()] * (1 + len(plan)),
        compiler_params=pltpu.CompilerParams(vmem_limit_bytes=8 * MIB),
        name="pair",
    )(kept, *arrived)


def places_of(row, slots, owners, local):
    rows = row.shape[1]
    upper = lax.broadcasted_iota(jnp.int32, (rows, rows), 0)
    lower = lax.broadcasted_iota(jnp.int32, (rows, rows), 1)
    column = jnp.sum(jnp.where(upper == lower, row, 0), axis=1, keepdims=True)
    before = jnp.logical_and(column == row, upper < lower)
    rank_of = jnp.sum(before.astype(jnp.int32), axis=0, keepdims=True)
    slot = lax.broadcasted_iota(jnp.int32, (slots * owners, rows), 0)
    owner = (lax.axis_index("dp") + slot // slots) % owners
    adapter = owner * local + slot // MOST % local
    return jnp.logical_and(row == adapter, rank_of == slot % MOST).astype(F32)


def prepare_kernel(index_ref, shrink_ref, places_ref, out_ref, sem, *, slots, owners):
    copy = pltpu.make_async_copy(shrink_ref, out_ref, sem)
    copy.start()
    places_ref[...] = places_of(index_ref[...], slots, owners, slots // MOST)
    copy.wait()


def prepare(index, shrink, slots, owners):
    return pl.pallas_call(
        functools.partial(prepare_kernel, slots=slots, owners=owners),
        out_shape=(
            jax.ShapeDtypeStruct((slots * owners, index.shape[1]), F32),
            pltpu.VMEM(shrink.shape, shrink.dtype),
        ),
        in_specs=[whole(), pl.BlockSpec(memory_space=pl.ANY)],
        out_specs=(whole(), whole()),
        scratch_shapes=[pltpu.SemaphoreType.DMA],
        compiler_params=pltpu.CompilerParams(vmem_limit_bytes=1 * MIB),
        name="prepare",
    )(index, pltpu.with_memory_space_constraint(shrink, pltpu.HBM))


def mix_kernel(residual_ref, places_ref, own_ref, *refs):
    arrived, (mixed_ref, kept_ref, sent_ref) = refs[:-3], refs[-3:]
    slots = kept_ref.shape[0]
    places = places_ref[...]
    total = own_ref[...] + residual_ref[...].astype(F32)
    for piece in arrived:
        total = total + piece[...].astype(F32)
    mixed = total.astype(BF16)
    mixed_ref[...] = mixed
    widened = mixed.astype(F32)
    routed = sum(
        places[:, row : row + 1] * widened[row : row + 1, :] for row in range(widened.shape[0])
    )
    kept_ref[...] = routed[:slots]
    for turn in range(sent_ref.shape[0]):
        sent_ref[turn] = routed[(turn + 1) * slots : (turn + 2) * slots].astype(BF16)


def mix(residual, places, own, arrived, slots, owners):
    rows, columns = residual.shape
    return pl.pallas_call(
        mix_kernel,
        out_shape=(
            pltpu.VMEM((rows, columns), BF16),
            jax.ShapeDtypeStruct((slots, columns), F32),
            jax.ShapeDtypeStruct((owners - 1, slots, columns), BF16),
        ),
        in_specs=[whole()] * (3 + len(arrived)),
        out_specs=(whole(),) * 3,
        compiler_params=pltpu.CompilerParams(vmem_limit_bytes=8 * MIB),
        name="mix",
    )(residual, places, own, *arrived)


def partial_values(rows, gain_ref, shrink_ref, place, columns, local):
    first = pl.multiple_of(place * columns, columns)
    squares = jnp.sum(rows * rows, axis=1, keepdims=True)
    scaled = rows * gain_ref[:, pl.ds(first, columns)].astype(F32)
    high = scaled.astype(BF16)
    low = (scaled - high.astype(F32)).astype(BF16)
    values = []
    for adapter in range(local):
        mine = slice(adapter * MOST, (adapter + 1) * MOST)
        both = jnp.concatenate([high[mine], low[mine]], axis=0)
        product = lax.dot_general(
            both,
            shrink_ref[adapter, :, pl.ds(first, columns)],
            (((1,), (1,)), ((), ())),
            preferred_element_type=F32,
        )
        values.append(product[:MOST] + product[MOST:])
    return jnp.concatenate(values, axis=0), squares


def own_half_kernel(rows_ref, gain_ref, shrink_ref, values_ref, squares_ref):
    columns = rows_ref.shape[1]
    values, squares = partial_values(
        rows_ref[...], gain_ref, shrink_ref, lax.axis_index("dp"), columns, shrink_ref.shape[0]
    )
    values_ref[...] = values
    squares_ref[...] = jnp.broadcast_to(squares, squares_ref.shape)


def own_half(rows, gain, shrink):
    slots = rows.shape[0]
    rank = shrink.shape[1]
    return pl.pallas_call(
        own_half_kernel,
        out_shape=(
            jax.ShapeDtypeStruct((slots, rank), F32),
            jax.ShapeDtypeStruct((slots, rank), F32),
        ),
        in_specs=[whole()] * 3,
        out_specs=(whole(),) * 2,
        compiler_params=pltpu.CompilerParams(vmem_limit_bytes=8 * MIB),
        cost_estimate=pl.CostEstimate(
            flops=2 * slots * rows.shape[1] * rank, bytes_accessed=2 * MIB, transcendentals=0
        ),
        name="own_half",
    )(rows, gain, shrink)


def finish_kernel(values_ref, squares_ref, gain_ref, shrink_ref, *refs):
    arrived, out_ref = refs[:-1], refs[-1]
    dp = 1 + len(arrived)
    me = lax.axis_index("dp")
    local = shrink_ref.shape[0]
    columns = arrived[0].shape[1]
    values, squares = values_ref[...], squares_ref[:, :1]
    for shift, piece in enumerate(arrived, start=1):
        more, more_squares = partial_values(
            piece[...].astype(F32),
            gain_ref,
            shrink_ref,
            lax.rem(me + dp - shift, dp),
            columns,
            local,
        )
        values, squares = values + more, squares + more_squares
    result = 2.0 * values * lax.rsqrt(squares / (columns * dp) + EPS)
    for adapter in range(local):
        out_ref[adapter, 0] = result[adapter * MOST : (adapter + 1) * MOST]


def finish(values, squares, gain, shrink, arrived):
    local, rank, _ = shrink.shape
    return pl.pallas_call(
        finish_kernel,
        out_shape=jax.ShapeDtypeStruct((local, 1, MOST, rank), F32),
        in_specs=[whole()] * (4 + len(arrived)),
        out_specs=whole(),
        compiler_params=pltpu.CompilerParams(vmem_limit_bytes=8 * MIB),
        name="finish",
    )(values, squares, gain, shrink, *arrived)


def shifted(array, axis, shift):
    count = lax.axis_size(axis)
    return lax.ppermute(array, axis, [(i, (i + shift) % count) for i in range(count)])


def across(array, receivers):
    sections = lax.axis_size("section")
    pairs = [
        (i * sections + s, j * sections + (s + 1) % sections)
        for i, j in enumerate(receivers)
        for s in range(sections)
    ]
    return lax.ppermute(array, ("tensor", "section"), pairs)


def body(hidden, down_matrix, residual, next_norm_scale, shrink_matrix, adapter_index):
    dp, tensors, sections = (lax.axis_size(axis) for axis in ("dp", "tensor", "section"))
    depth, _ = down_matrix.shape
    local = shrink_matrix.shape[0]

    others = jnp.stack([shifted(hidden, "dp", shift) for shift in range(1, dp)])

    step = step_of(depth)
    blocks = depth // step
    held_count = max(1, min(blocks // 2, HELD_BYTES // (2 * step * down_matrix.shape[1])))
    held = fetch(down_matrix, held_count * step)

    shrink = jnp.swapaxes(shrink_matrix, 1, 2)
    gain = next_norm_scale[None, :]

    in_vmem = [pltpu.with_memory_space_constraint(x, pltpu.VMEM) for x in (hidden, others, held)]
    total, sent = project(*in_vmem, down_matrix, tensors, sections)
    index, total = lax.optimization_barrier((adapter_index.reshape(1, -1), total))
    kept = keep(total, tensors, sections)
    places, shrink = prepare(index, shrink, local * MOST, dp)
    arrived = [shifted(sent[s - 1], "section", s) for s in range(1, sections)]
    plan = exchange_plan(tensors)
    own, *sums = pair(kept, arrived, plan, tensors)
    arrived = [across(x, receivers) for x, receivers in zip(sums, plan)]
    mixed, routed, leaving = mix(residual, places, own, arrived, local * MOST, dp)
    arrived = [shifted(leaving[s - 1], "dp", s) for s in range(1, dp)]
    values, squares = own_half(routed, gain, shrink)
    shrunk = finish(values, squares, gain, shrink, arrived)
    return (mixed, shrunk)


def solution(mesh):
    placed = (
        P(("groups", "dp"), ("tensor", "section")),
        P(("tensor", "section"), "dp"),
        P(("groups", "tensor", "section"), "dp"),
        P(),
        P("dp", None, None),
        P(("groups", "tensor", "section"), None),
    )
    return jax.shard_map(
        body,
        mesh=mesh,
        in_specs=placed,
        out_specs=(
            P(("groups", "tensor", "section"), "dp"),
            P("dp", ("groups", "tensor", "section"), None, None),
        ),
        check_vma=False,
    )
```

```python
import functools

import jax
import jax.numpy as jnp
from jax import lax
from jax.experimental import pallas as pl
from jax.experimental.pallas import tpu as pltpu
from jax.sharding import PartitionSpec as P

MOST = 2
EPS = 1e-05
DEPTH_STEP = 512
HELD_BYTES = 21 * 2**20
WIDTH = 1024
MIB = 2**20
F32 = jnp.float32
BF16 = jnp.bfloat16


def whole():
    return pl.BlockSpec(memory_space=pltpu.VMEM)


def step_of(depth):
    return max(s for s in range(16, DEPTH_STEP + 1, 16) if depth % s == 0)


def fetch_kernel(weight_ref, held_ref, sem):
    copy = pltpu.make_async_copy(
        weight_ref.at[pl.ds(0, held_ref.shape[0]), :], held_ref, sem
    )
    copy.start()
    copy.wait()


def fetch(weight, rows):
    columns = weight.shape[1]
    return pl.pallas_call(
        fetch_kernel,
        out_shape=pltpu.VMEM((rows, columns), weight.dtype),
        in_specs=[pl.BlockSpec(memory_space=pl.ANY)],
        out_specs=whole(),
        scratch_shapes=[pltpu.SemaphoreType.DMA],
        compiler_params=pltpu.CompilerParams(vmem_limit_bytes=1 * MIB),
        cost_estimate=pl.CostEstimate(
            flops=0, bytes_accessed=2 * rows * columns, transcendentals=0
        ),
        name="fetch",
    )(weight)


def last_parts(step):
    if step % 64:
        return [(0, step)]
    return [(0, step // 2), (step // 2, step // 4), (step // 4 * 3, step // 4)]


def project_kernel(
    own_ref,
    others_ref,
    held_ref,
    weight_ref,
    total_ref,
    sent_ref,
    held_rows_ref,
    rows_ref,
    rest_ref,
    sems,
    *,
    tensors,
    sections,
):
    rest, step, columns = rest_ref.shape
    held = held_ref.shape[0] // step
    own_rows = own_ref.shape[0]
    dp = 1 + others_ref.shape[0]
    me = lax.axis_index("dp")
    width = min(columns, WIDTH)

    def copy_of(i, sem, first=0, size=step):
        return pltpu.make_async_copy(
            weight_ref.at[pl.ds((held + i) * step + first, size), :],
            rest_ref.at[i, pl.ds(first, size), :],
            sems.at[sem],
        )

    parts = last_parts(step)
    last = [copy_of(rest - 1, rest - 1 + k, *part) for k, part in enumerate(parts)]
    for i in range(rest - 1):
        copy_of(i, i).start()
    for copy in last:
        copy.start()

    def fill(target, block):
        for shift in range(dp):
            first = pl.multiple_of((me + dp - shift) % dp * own_rows, own_rows)
            source = own_ref[:, block] if shift == 0 else others_ref[shift - 1, :, block]
            target[pl.ds(first, own_rows), :] = source

    fill(held_rows_ref, slice(0, held * step))
    for i in range(rest):
        fill(rows_ref.at[i], slice((held + i) * step, (held + i + 1) * step))

    def held_step(n, _):
        lanes = pl.ds(pl.multiple_of(n * width, width), width)
        total_ref[:, lanes] = jnp.dot(
            held_rows_ref[...], held_ref[:, lanes], preferred_element_type=F32
        )
        return 0

    def add(i, part=slice(None)):
        for n in range(0, columns, width):
            lanes = slice(n, n + width)
            total_ref[:, lanes] += jnp.dot(
                rows_ref[i, :, part], rest_ref[i, part, lanes], preferred_element_type=F32
            )

    def rest_step(i, _):
        copy_of(i, i).wait()
        add(i)
        return 0

    lax.fori_loop(0, columns // width, held_step, 0)
    lax.fori_loop(0, rest - 1, rest_step, 0)
    for copy, (first, size) in zip(last, parts):
        copy.wait()
        add(rest - 1, slice(first, first + size))

    for turn in range(1, sections):
        for n in range(0, columns, width):
            lanes = slice(n, n + width)
            rows = rows_of(turn, total_ref, lanes, tensors, sections)
            sent_ref[turn - 1, :, lanes] = rows.astype(BF16)


def rows_of(turn, total_ref, lanes, tensors, sections):
    tensor, section = lax.axis_index("tensor"), lax.axis_index("section")
    block_rows = total_ref.shape[0] // (tensors * sections)
    group = sections * block_rows
    blocks = []
    for k in range(tensors):
        first = pl.multiple_of(partner_of(tensor, k, tensors) * group, group)
        rows = total_ref[pl.ds(first, group), lanes]
        rows = pltpu.roll(rows, (sections - section) % sections * block_rows, 0)
        part = (turn + (k > 0)) % sections
        blocks.append(rows[part * block_rows : (part + 1) * block_rows])
    return jnp.concatenate(blocks, axis=0)


def keep_kernel(total_ref, kept_ref, *, tensors, sections):
    columns = total_ref.shape[1]
    width = min(columns, WIDTH)
    for n in range(0, columns, width):
        lanes = slice(n, n + width)
        kept_ref[:, lanes] = rows_of(0, total_ref, lanes, tensors, sections)


def keep(total, tensors, sections):
    rows, columns = total.shape
    return pl.pallas_call(
        functools.partial(keep_kernel, tensors=tensors, sections=sections),
        out_shape=jax.ShapeDtypeStruct((rows // sections, columns), F32),
        in_specs=[whole()],
        out_specs=whole(),
        compiler_params=pltpu.CompilerParams(vmem_limit_bytes=4 * MIB),
        name="keep",
    )(total)


def project(own, others, held, weight, tensors, sections):
    own_rows, depth = own.shape
    rows = own_rows * (1 + others.shape[0])
    columns = weight.shape[1]
    step = step_of(depth)
    rest = (depth - held.shape[0]) // step
    return pl.pallas_call(
        functools.partial(project_kernel, tensors=tensors, sections=sections),
        out_shape=(
            pltpu.VMEM((rows, columns), F32),
            pltpu.VMEM((sections - 1, rows // sections, columns), BF16),
        ),
        in_specs=[whole(), whole(), whole(), pl.BlockSpec(memory_space=pl.ANY)],
        out_specs=(whole(), whole()),
        scratch_shapes=[
            pltpu.VMEM((rows, held.shape[0]), BF16),
            pltpu.VMEM((rest, rows, step), BF16),
            pltpu.VMEM((rest, step, columns), BF16),
            pltpu.SemaphoreType.DMA((rest - 1 + len(last_parts(step)),)),
        ],
        compiler_params=pltpu.CompilerParams(vmem_limit_bytes=36 * MIB),
        cost_estimate=pl.CostEstimate(
            flops=2 * rows * depth * columns,
            bytes_accessed=2 * rest * step * columns,
            transcendentals=0,
        ),
        name="project",
    )(own, others, held, weight)


def partner_of(me, turn, count):
    if count & (count - 1) == 0:
        return me ^ turn
    return (me + turn) % count


def turn_of(me, partner, count):
    if count & (count - 1) == 0:
        return me ^ partner
    return (partner - me) % count


def exchange_plan(count):
    if count == 4:
        return [(2, 3, 1, 0), (3, 2, 0, 1), (1, 0, 3, 2)]
    turns = range(count - 1, 0, -1)
    return [tuple(partner_of(i, turn, count) for i in range(count)) for turn in turns]


def pair_kernel(kept_ref, *refs, plan, tensors):
    arrived, (own_ref, *outs) = refs[: -1 - len(plan)], refs[-1 - len(plan) :]
    me = lax.axis_index("tensor")
    block_rows = own_ref.shape[0]
    total = kept_ref[...]
    for piece in arrived:
        total = total + piece[...].astype(F32)
    blocks = [total[turn * block_rows : (turn + 1) * block_rows] for turn in range(tensors)]
    own_ref[...] = blocks[0]
    for receivers, out_ref in zip(plan, outs):
        turns = [turn_of(i, j, tensors) for i, j in enumerate(receivers)]
        block = blocks[turns[0]]
        for i, turn in enumerate(turns):
            if turn != turns[0]:
                block = jnp.where(me == i, blocks[turn], block)
        out_ref[...] = block.astype(out_ref.dtype)


def pair(kept, arrived, plan, tensors):
    rows, columns = kept.shape
    block = (rows // tensors, columns)
    return pl.pallas_call(
        functools.partial(pair_kernel, plan=plan, tensors=tensors),
        out_shape=[jax.ShapeDtypeStruct(block, F32)] + [jax.ShapeDtypeStruct(block, BF16)] * len(plan),
        in_specs=[whole()] * (1 + len(arrived)),
        out_specs=[whole()] * (1 + len(plan)),
        compiler_params=pltpu.CompilerParams(vmem_limit_bytes=8 * MIB),
        name="pair",
    )(kept, *arrived)


def places_of(row, slots, owners, local):
    rows = row.shape[1]
    upper = lax.broadcasted_iota(jnp.int32, (rows, rows), 0)
    lower = lax.broadcasted_iota(jnp.int32, (rows, rows), 1)
    column = jnp.sum(jnp.where(upper == lower, row, 0), axis=1, keepdims=True)
    before = jnp.logical_and(column == row, upper < lower)
    rank_of = jnp.sum(before.astype(jnp.int32), axis=0, keepdims=True)
    slot = lax.broadcasted_iota(jnp.int32, (slots * owners, rows), 0)
    owner = (lax.axis_index("dp") + slot // slots) % owners
    adapter = owner * local + slot // MOST % local
    return jnp.logical_and(row == adapter, rank_of == slot % MOST).astype(F32)


def prepare_kernel(index_ref, shrink_ref, places_ref, out_ref, sem, *, slots, owners):
    copy = pltpu.make_async_copy(shrink_ref, out_ref, sem)
    copy.start()
    places_ref[...] = places_of(index_ref[...], slots, owners, slots // MOST)
    copy.wait()


def prepare(index, shrink, slots, owners):
    return pl.pallas_call(
        functools.partial(prepare_kernel, slots=slots, owners=owners),
        out_shape=(
            jax.ShapeDtypeStruct((slots * owners, index.shape[1]), F32),
            pltpu.VMEM(shrink.shape, shrink.dtype),
        ),
        in_specs=[whole(), pl.BlockSpec(memory_space=pl.ANY)],
        out_specs=(whole(), whole()),
        scratch_shapes=[pltpu.SemaphoreType.DMA],
        compiler_params=pltpu.CompilerParams(vmem_limit_bytes=1 * MIB),
        name="prepare",
    )(index, pltpu.with_memory_space_constraint(shrink, pltpu.HBM))


def mix_kernel(residual_ref, places_ref, own_ref, *refs):
    arrived, (mixed_ref, kept_ref, sent_ref) = refs[:-3], refs[-3:]
    slots = kept_ref.shape[0]
    places = places_ref[...]
    total = own_ref[...] + residual_ref[...].astype(F32)
    for piece in arrived:
        total = total + piece[...].astype(F32)
    mixed = total.astype(BF16)
    mixed_ref[...] = mixed
    widened = mixed.astype(F32)
    routed = sum(
        places[:, row : row + 1] * widened[row : row + 1, :] for row in range(widened.shape[0])
    )
    kept_ref[...] = routed[:slots]
    for turn in range(sent_ref.shape[0]):
        sent_ref[turn] = routed[(turn + 1) * slots : (turn + 2) * slots].astype(BF16)


def mix(residual, places, own, arrived, slots, owners):
    rows, columns = residual.shape
    return pl.pallas_call(
        mix_kernel,
        out_shape=(
            pltpu.VMEM((rows, columns), BF16),
            jax.ShapeDtypeStruct((slots, columns), F32),
            jax.ShapeDtypeStruct((owners - 1, slots, columns), BF16),
        ),
        in_specs=[whole()] * (3 + len(arrived)),
        out_specs=(whole(),) * 3,
        compiler_params=pltpu.CompilerParams(vmem_limit_bytes=8 * MIB),
        name="mix",
    )(residual, places, own, *arrived)


def partial_values(rows, gain_ref, shrink_ref, place, columns, local):
    first = pl.multiple_of(place * columns, columns)
    squares = jnp.sum(rows * rows, axis=1, keepdims=True)
    scaled = rows * gain_ref[:, pl.ds(first, columns)].astype(F32)
    high = scaled.astype(BF16)
    low = (scaled - high.astype(F32)).astype(BF16)
    values = []
    for adapter in range(local):
        mine = slice(adapter * MOST, (adapter + 1) * MOST)
        both = jnp.concatenate([high[mine], low[mine]], axis=0)
        product = lax.dot_general(
            both,
            shrink_ref[adapter, :, pl.ds(first, columns)],
            (((1,), (1,)), ((), ())),
            preferred_element_type=F32,
        )
        values.append(product[:MOST] + product[MOST:])
    return jnp.concatenate(values, axis=0), squares


def own_half_kernel(rows_ref, gain_ref, shrink_ref, values_ref, squares_ref):
    columns = rows_ref.shape[1]
    values, squares = partial_values(
        rows_ref[...], gain_ref, shrink_ref, lax.axis_index("dp"), columns, shrink_ref.shape[0]
    )
    values_ref[...] = values
    squares_ref[...] = jnp.broadcast_to(squares, squares_ref.shape)


def own_half(rows, gain, shrink):
    slots = rows.shape[0]
    rank = shrink.shape[1]
    return pl.pallas_call(
        own_half_kernel,
        out_shape=(
            jax.ShapeDtypeStruct((slots, rank), F32),
            jax.ShapeDtypeStruct((slots, rank), F32),
        ),
        in_specs=[whole()] * 3,
        out_specs=(whole(),) * 2,
        compiler_params=pltpu.CompilerParams(vmem_limit_bytes=8 * MIB),
        cost_estimate=pl.CostEstimate(
            flops=2 * slots * rows.shape[1] * rank, bytes_accessed=2 * MIB, transcendentals=0
        ),
        name="own_half",
    )(rows, gain, shrink)


def finish_kernel(values_ref, squares_ref, gain_ref, shrink_ref, *refs):
    arrived, out_ref = refs[:-1], refs[-1]
    dp = 1 + len(arrived)
    me = lax.axis_index("dp")
    local = shrink_ref.shape[0]
    columns = arrived[0].shape[1]
    values, squares = values_ref[...], squares_ref[:, :1]
    for shift, piece in enumerate(arrived, start=1):
        more, more_squares = partial_values(
            piece[...].astype(F32),
            gain_ref,
            shrink_ref,
            lax.rem(me + dp - shift, dp),
            columns,
            local,
        )
        values, squares = values + more, squares + more_squares
    result = 2.0 * values * lax.rsqrt(squares / (columns * dp) + EPS)
    for adapter in range(local):
        out_ref[adapter, 0] = result[adapter * MOST : (adapter + 1) * MOST]


def finish(values, squares, gain, shrink, arrived):
    local, rank, _ = shrink.shape
    return pl.pallas_call(
        finish_kernel,
        out_shape=jax.ShapeDtypeStruct((local, 1, MOST, rank), F32),
        in_specs=[whole()] * (4 + len(arrived)),
        out_specs=whole(),
        compiler_params=pltpu.CompilerParams(vmem_limit_bytes=8 * MIB),
        name="finish",
    )(values, squares, gain, shrink, *arrived)


def shifted(array, axis, shift):
    count = lax.axis_size(axis)
    return lax.ppermute(array, axis, [(i, (i + shift) % count) for i in range(count)])


def across(array, receivers):
    sections = lax.axis_size("section")
    pairs = [
        (i * sections + s, j * sections + (s + 1) % sections)
        for i, j in enumerate(receivers)
        for s in range(sections)
    ]
    return lax.ppermute(array, ("tensor", "section"), pairs)


def body(hidden, down_matrix, residual, next_norm_scale, shrink_matrix, adapter_index):
    dp, tensors, sections = (lax.axis_size(axis) for axis in ("dp", "tensor", "section"))
    depth, _ = down_matrix.shape
    local = shrink_matrix.shape[0]

    others = jnp.stack([shifted(hidden, "dp", shift) for shift in range(1, dp)])

    step = step_of(depth)
    blocks = depth // step
    held_count = max(1, min(blocks // 2, HELD_BYTES // (2 * step * down_matrix.shape[1])))
    held = fetch(down_matrix, held_count * step)

    shrink = jnp.swapaxes(shrink_matrix, 1, 2)
    gain = next_norm_scale[None, :]

    in_vmem = [pltpu.with_memory_space_constraint(x, pltpu.VMEM) for x in (hidden, others, held)]
    total, sent = project(*in_vmem, down_matrix, tensors, sections)
    index, total = lax.optimization_barrier((adapter_index.reshape(1, -1), total))
    kept = keep(total, tensors, sections)
    places, shrink = prepare(index, shrink, local * MOST, dp)
    arrived = [shifted(sent[s - 1], "section", s) for s in range(1, sections)]
    plan = exchange_plan(tensors)
    own, *sums = pair(kept, arrived, plan, tensors)
    arrived = [across(x, receivers) for x, receivers in zip(sums, plan)]
    mixed, routed, leaving = mix(residual, places, own, arrived, local * MOST, dp)
    arrived = [shifted(leaving[s - 1], "dp", s) for s in range(1, dp)]
    values, squares = own_half(routed, gain, shrink)
    shrunk = finish(values, squares, gain, shrink, arrived)
    return (mixed, shrunk)


def solution(mesh):
    placed = (
        P(("groups", "dp"), ("tensor", "section")),
        P(("tensor", "section"), "dp"),
        P(("groups", "tensor", "section"), "dp"),
        P(),
        P("dp", None, None),
        P(("groups", "tensor", "section"), None),
    )
    return jax.shard_map(
        body,
        mesh=mesh,
        in_specs=placed,
        out_specs=(
            P(("groups", "tensor", "section"), "dp"),
            P("dp", ("groups", "tensor", "section"), None, None),
        ),
        check_vma=False,
    )
```

```python
import functools

import jax
import jax.numpy as jnp
from jax import lax
from jax.experimental import pallas as pl
from jax.experimental.pallas import tpu as pltpu
from jax.sharding import PartitionSpec as P

MOST = 2
EPS = 1e-05
DEPTH_STEP = 512
HELD_BYTES = 21 * 2**20
WIDTH = 1024
IN_FLIGHT = 4
MIB = 2**20
F32 = jnp.float32
BF16 = jnp.bfloat16


def whole():
    return pl.BlockSpec(memory_space=pltpu.VMEM)


def step_of(depth):
    return max(s for s in range(16, DEPTH_STEP + 1, 16) if depth % s == 0)


def fetch_kernel(weight_ref, held_ref, sem):
    copy = pltpu.make_async_copy(
        weight_ref.at[pl.ds(0, held_ref.shape[0]), :], held_ref, sem
    )
    copy.start()
    copy.wait()


def fetch(weight, rows):
    columns = weight.shape[1]
    return pl.pallas_call(
        fetch_kernel,
        out_shape=pltpu.VMEM((rows, columns), weight.dtype),
        in_specs=[pl.BlockSpec(memory_space=pl.ANY)],
        out_specs=whole(),
        scratch_shapes=[pltpu.SemaphoreType.DMA],
        compiler_params=pltpu.CompilerParams(vmem_limit_bytes=1 * MIB),
        cost_estimate=pl.CostEstimate(
            flops=0, bytes_accessed=2 * rows * columns, transcendentals=0
        ),
        name="fetch",
    )(weight)


def last_parts(step):
    if step % 64:
        return [(0, step)]
    return [(0, step // 2), (step // 2, step // 4), (step // 4 * 3, step // 4)]


def project_kernel(
    own_ref,
    others_ref,
    held_ref,
    weight_ref,
    total_ref,
    sent_ref,
    rows_ref,
    rest_ref,
    sems,
    *,
    tensors,
    sections,
):
    rest, step, columns = rest_ref.shape
    held = held_ref.shape[0] // step
    own_rows = own_ref.shape[0]
    dp = 1 + others_ref.shape[0]
    me = lax.axis_index("dp")
    width = min(columns, WIDTH)

    def copy_of(i, sem, first=0, size=step):
        return pltpu.make_async_copy(
            weight_ref.at[pl.ds((held + i) * step + first, size), :],
            rest_ref.at[i, pl.ds(first, size), :],
            sems.at[sem],
        )

    parts = last_parts(step)
    last = [copy_of(rest - 1, rest - 1 + k, *part) for k, part in enumerate(parts)]
    for i in range(min(rest - 1, IN_FLIGHT)):
        copy_of(i, i).start()

    for i in range(held + rest):
        block = slice(i * step, (i + 1) * step)
        for shift in range(dp):
            first = pl.multiple_of((me + dp - shift) % dp * own_rows, own_rows)
            source = own_ref[:, block] if shift == 0 else others_ref[shift - 1, :, block]
            rows_ref[i, pl.ds(first, own_rows), :] = source

    def held_step(n, _):
        lanes = pl.ds(pl.multiple_of(n * width, width), width)
        total_ref[:, lanes] = sum(
            jnp.dot(
                rows_ref[i], held_ref[i * step : (i + 1) * step, lanes], preferred_element_type=F32
            )
            for i in range(held)
        )
        return 0

    def add(i, part=slice(None)):
        for n in range(0, columns, width):
            lanes = slice(n, n + width)
            total_ref[:, lanes] += jnp.dot(
                rows_ref[held + i, :, part], rest_ref[i, part, lanes], preferred_element_type=F32
            )

    def rest_step(i, _):
        copy_of(i, i).wait()
        add(i)
        return 0

    lax.fori_loop(0, columns // width, held_step, 0)
    for i in range(IN_FLIGHT, rest - 1):
        copy_of(i, i).start()
    for copy in last:
        copy.start()
    lax.fori_loop(0, rest - 1, rest_step, 0)
    for copy, (first, size) in zip(last, parts):
        copy.wait()
        add(rest - 1, slice(first, first + size))

    for turn in range(1, sections):
        for n in range(0, columns, width):
            lanes = slice(n, n + width)
            rows = rows_of(turn, total_ref, lanes, tensors, sections)
            sent_ref[turn - 1, :, lanes] = rows.astype(BF16)


def rows_of(turn, total_ref, lanes, tensors, sections):
    tensor, section = lax.axis_index("tensor"), lax.axis_index("section")
    block_rows = total_ref.shape[0] // (tensors * sections)
    group = sections * block_rows
    blocks = []
    for k in range(tensors):
        first = pl.multiple_of(partner_of(tensor, k, tensors) * group, group)
        rows = total_ref[pl.ds(first, group), lanes]
        rows = pltpu.roll(rows, (sections - section) % sections * block_rows, 0)
        part = (turn + (k > 0)) % sections
        blocks.append(rows[part * block_rows : (part + 1) * block_rows])
    return jnp.concatenate(blocks, axis=0)


def keep_kernel(total_ref, kept_ref, *, tensors, sections):
    columns = total_ref.shape[1]
    width = min(columns, WIDTH)
    for n in range(0, columns, width):
        lanes = slice(n, n + width)
        kept_ref[:, lanes] = rows_of(0, total_ref, lanes, tensors, sections)


def keep(total, tensors, sections):
    rows, columns = total.shape
    return pl.pallas_call(
        functools.partial(keep_kernel, tensors=tensors, sections=sections),
        out_shape=jax.ShapeDtypeStruct((rows // sections, columns), F32),
        in_specs=[whole()],
        out_specs=whole(),
        compiler_params=pltpu.CompilerParams(vmem_limit_bytes=4 * MIB),
        name="keep",
    )(total)


def project(own, others, held, weight, tensors, sections):
    own_rows, depth = own.shape
    rows = own_rows * (1 + others.shape[0])
    columns = weight.shape[1]
    step = step_of(depth)
    rest = (depth - held.shape[0]) // step
    return pl.pallas_call(
        functools.partial(project_kernel, tensors=tensors, sections=sections),
        out_shape=(
            pltpu.VMEM((rows, columns), F32),
            pltpu.VMEM((sections - 1, rows // sections, columns), BF16),
        ),
        in_specs=[whole(), whole(), whole(), pl.BlockSpec(memory_space=pl.ANY)],
        out_specs=(whole(), whole()),
        scratch_shapes=[
            pltpu.VMEM((depth // step, rows, step), BF16),
            pltpu.VMEM((rest, step, columns), BF16),
            pltpu.SemaphoreType.DMA((rest - 1 + len(last_parts(step)),)),
        ],
        compiler_params=pltpu.CompilerParams(vmem_limit_bytes=36 * MIB),
        cost_estimate=pl.CostEstimate(
            flops=2 * rows * depth * columns,
            bytes_accessed=2 * rest * step * columns,
            transcendentals=0,
        ),
        name="project",
    )(own, others, held, weight)


def partner_of(me, turn, count):
    if count & (count - 1) == 0:
        return me ^ turn
    return (me + turn) % count


def turn_of(me, partner, count):
    if count & (count - 1) == 0:
        return me ^ partner
    return (partner - me) % count


def exchange_plan(count):
    if count == 4:
        return [(2, 3, 1, 0), (3, 2, 0, 1), (1, 0, 3, 2)]
    turns = range(count - 1, 0, -1)
    return [tuple(partner_of(i, turn, count) for i in range(count)) for turn in turns]


def pair_kernel(kept_ref, *refs, plan, tensors):
    arrived, (own_ref, *outs) = refs[: -1 - len(plan)], refs[-1 - len(plan) :]
    me = lax.axis_index("tensor")
    block_rows = own_ref.shape[0]
    total = kept_ref[...]
    for piece in arrived:
        total = total + piece[...].astype(F32)
    blocks = [total[turn * block_rows : (turn + 1) * block_rows] for turn in range(tensors)]
    own_ref[...] = blocks[0]
    for receivers, out_ref in zip(plan, outs):
        turns = [turn_of(i, j, tensors) for i, j in enumerate(receivers)]
        block = blocks[turns[0]]
        for i, turn in enumerate(turns):
            if turn != turns[0]:
                block = jnp.where(me == i, blocks[turn], block)
        out_ref[...] = block.astype(out_ref.dtype)


def pair(kept, arrived, plan, tensors):
    rows, columns = kept.shape
    block = (rows // tensors, columns)
    return pl.pallas_call(
        functools.partial(pair_kernel, plan=plan, tensors=tensors),
        out_shape=[jax.ShapeDtypeStruct(block, F32)] + [jax.ShapeDtypeStruct(block, BF16)] * len(plan),
        in_specs=[whole()] * (1 + len(arrived)),
        out_specs=[whole()] * (1 + len(plan)),
        compiler_params=pltpu.CompilerParams(vmem_limit_bytes=8 * MIB),
        name="pair",
    )(kept, *arrived)


def places_of(row, slots, owners, local):
    rows = row.shape[1]
    upper = lax.broadcasted_iota(jnp.int32, (rows, rows), 0)
    lower = lax.broadcasted_iota(jnp.int32, (rows, rows), 1)
    column = jnp.sum(jnp.where(upper == lower, row, 0), axis=1, keepdims=True)
    before = jnp.logical_and(column == row, upper < lower)
    rank_of = jnp.sum(before.astype(jnp.int32), axis=0, keepdims=True)
    slot = lax.broadcasted_iota(jnp.int32, (slots * owners, rows), 0)
    owner = (lax.axis_index("dp") + slot // slots) % owners
    adapter = owner * local + slot // MOST % local
    return jnp.logical_and(row == adapter, rank_of == slot % MOST).astype(F32)


def prepare_kernel(index_ref, shrink_ref, places_ref, out_ref, sem, *, slots, owners):
    copy = pltpu.make_async_copy(shrink_ref, out_ref, sem)
    copy.start()
    places_ref[...] = places_of(index_ref[...], slots, owners, slots // MOST)
    copy.wait()


def prepare(index, shrink, slots, owners):
    return pl.pallas_call(
        functools.partial(prepare_kernel, slots=slots, owners=owners),
        out_shape=(
            jax.ShapeDtypeStruct((slots * owners, index.shape[1]), F32),
            pltpu.VMEM(shrink.shape, shrink.dtype),
        ),
        in_specs=[whole(), pl.BlockSpec(memory_space=pl.ANY)],
        out_specs=(whole(), whole()),
        scratch_shapes=[pltpu.SemaphoreType.DMA],
        compiler_params=pltpu.CompilerParams(vmem_limit_bytes=1 * MIB),
        name="prepare",
    )(index, pltpu.with_memory_space_constraint(shrink, pltpu.HBM))


def mix_kernel(residual_ref, places_ref, own_ref, *refs):
    arrived, (mixed_ref, kept_ref, sent_ref) = refs[:-3], refs[-3:]
    slots = kept_ref.shape[0]
    places = places_ref[...]
    total = own_ref[...] + residual_ref[...].astype(F32)
    for piece in arrived:
        total = total + piece[...].astype(F32)
    mixed = total.astype(BF16)
    mixed_ref[...] = mixed
    widened = mixed.astype(F32)
    routed = sum(
        places[:, row : row + 1] * widened[row : row + 1, :] for row in range(widened.shape[0])
    )
    kept_ref[...] = routed[:slots]
    for turn in range(sent_ref.shape[0]):
        sent_ref[turn] = routed[(turn + 1) * slots : (turn + 2) * slots].astype(BF16)


def mix(residual, places, own, arrived, slots, owners):
    rows, columns = residual.shape
    return pl.pallas_call(
        mix_kernel,
        out_shape=(
            pltpu.VMEM((rows, columns), BF16),
            jax.ShapeDtypeStruct((slots, columns), F32),
            jax.ShapeDtypeStruct((owners - 1, slots, columns), BF16),
        ),
        in_specs=[whole()] * (3 + len(arrived)),
        out_specs=(whole(),) * 3,
        compiler_params=pltpu.CompilerParams(vmem_limit_bytes=8 * MIB),
        name="mix",
    )(residual, places, own, *arrived)


def partial_values(rows, gain_ref, shrink_ref, place, columns, local):
    first = pl.multiple_of(place * columns, columns)
    squares = jnp.sum(rows * rows, axis=1, keepdims=True)
    scaled = rows * gain_ref[:, pl.ds(first, columns)].astype(F32)
    high = scaled.astype(BF16)
    low = (scaled - high.astype(F32)).astype(BF16)
    values = []
    for adapter in range(local):
        mine = slice(adapter * MOST, (adapter + 1) * MOST)
        both = jnp.concatenate([high[mine], low[mine]], axis=0)
        product = lax.dot_general(
            both,
            shrink_ref[adapter, :, pl.ds(first, columns)],
            (((1,), (1,)), ((), ())),
            preferred_element_type=F32,
        )
        values.append(product[:MOST] + product[MOST:])
    return jnp.concatenate(values, axis=0), squares


def own_half_kernel(rows_ref, gain_ref, shrink_ref, values_ref, squares_ref):
    columns = rows_ref.shape[1]
    values, squares = partial_values(
        rows_ref[...], gain_ref, shrink_ref, lax.axis_index("dp"), columns, shrink_ref.shape[0]
    )
    values_ref[...] = values
    squares_ref[...] = jnp.broadcast_to(squares, squares_ref.shape)


def own_half(rows, gain, shrink):
    slots = rows.shape[0]
    rank = shrink.shape[1]
    return pl.pallas_call(
        own_half_kernel,
        out_shape=(
            jax.ShapeDtypeStruct((slots, rank), F32),
            jax.ShapeDtypeStruct((slots, rank), F32),
        ),
        in_specs=[whole()] * 3,
        out_specs=(whole(),) * 2,
        compiler_params=pltpu.CompilerParams(vmem_limit_bytes=8 * MIB),
        cost_estimate=pl.CostEstimate(
            flops=2 * slots * rows.shape[1] * rank, bytes_accessed=2 * MIB, transcendentals=0
        ),
        name="own_half",
    )(rows, gain, shrink)


def finish_kernel(values_ref, squares_ref, gain_ref, shrink_ref, *refs):
    arrived, out_ref = refs[:-1], refs[-1]
    dp = 1 + len(arrived)
    me = lax.axis_index("dp")
    local = shrink_ref.shape[0]
    columns = arrived[0].shape[1]
    values, squares = values_ref[...], squares_ref[:, :1]
    for shift, piece in enumerate(arrived, start=1):
        more, more_squares = partial_values(
            piece[...].astype(F32),
            gain_ref,
            shrink_ref,
            lax.rem(me + dp - shift, dp),
            columns,
            local,
        )
        values, squares = values + more, squares + more_squares
    result = 2.0 * values * lax.rsqrt(squares / (columns * dp) + EPS)
    for adapter in range(local):
        out_ref[adapter, 0] = result[adapter * MOST : (adapter + 1) * MOST]


def finish(values, squares, gain, shrink, arrived):
    local, rank, _ = shrink.shape
    return pl.pallas_call(
        finish_kernel,
        out_shape=jax.ShapeDtypeStruct((local, 1, MOST, rank), F32),
        in_specs=[whole()] * (4 + len(arrived)),
        out_specs=whole(),
        compiler_params=pltpu.CompilerParams(vmem_limit_bytes=8 * MIB),
        name="finish",
    )(values, squares, gain, shrink, *arrived)


def shifted(array, axis, shift):
    count = lax.axis_size(axis)
    return lax.ppermute(array, axis, [(i, (i + shift) % count) for i in range(count)])


def across(array, receivers):
    sections = lax.axis_size("section")
    pairs = [
        (i * sections + s, j * sections + (s + 1) % sections)
        for i, j in enumerate(receivers)
        for s in range(sections)
    ]
    return lax.ppermute(array, ("tensor", "section"), pairs)


def body(hidden, down_matrix, residual, next_norm_scale, shrink_matrix, adapter_index):
    dp, tensors, sections = (lax.axis_size(axis) for axis in ("dp", "tensor", "section"))
    depth, _ = down_matrix.shape
    local = shrink_matrix.shape[0]

    others = jnp.stack([shifted(hidden, "dp", shift) for shift in range(1, dp)])

    step = step_of(depth)
    blocks = depth // step
    held_count = max(1, min(blocks // 2, HELD_BYTES // (2 * step * down_matrix.shape[1])))
    held = fetch(down_matrix, held_count * step)

    shrink = jnp.swapaxes(shrink_matrix, 1, 2)
    gain = next_norm_scale[None, :]

    in_vmem = [pltpu.with_memory_space_constraint(x, pltpu.VMEM) for x in (hidden, others, held)]
    total, sent = project(*in_vmem, down_matrix, tensors, sections)
    index, total = lax.optimization_barrier((adapter_index.reshape(1, -1), total))
    kept = keep(total, tensors, sections)
    places, shrink = prepare(index, shrink, local * MOST, dp)
    arrived = [shifted(sent[s - 1], "section", s) for s in range(1, sections)]
    plan = exchange_plan(tensors)
    own, *sums = pair(kept, arrived, plan, tensors)
    arrived = [across(x, receivers) for x, receivers in zip(sums, plan)]
    mixed, routed, leaving = mix(residual, places, own, arrived, local * MOST, dp)
    arrived = [shifted(leaving[s - 1], "dp", s) for s in range(1, dp)]
    values, squares = own_half(routed, gain, shrink)
    shrunk = finish(values, squares, gain, shrink, arrived)
    return (mixed, shrunk)


def solution(mesh):
    placed = (
        P(("groups", "dp"), ("tensor", "section")),
        P(("tensor", "section"), "dp"),
        P(("groups", "tensor", "section"), "dp"),
        P(),
        P("dp", None, None),
        P(("groups", "tensor", "section"), None),
    )
    return jax.shard_map(
        body,
        mesh=mesh,
        in_specs=placed,
        out_specs=(
            P(("groups", "tensor", "section"), "dp"),
            P("dp", ("groups", "tensor", "section"), None, None),
        ),
        check_vma=False,
    )
```

```python
import functools

import jax
import jax.numpy as jnp
from jax import lax
from jax.experimental import pallas as pl
from jax.experimental.pallas import tpu as pltpu
from jax.sharding import PartitionSpec as P

MOST = 2
EPS = 1e-05
DEPTH_STEP = 512
HELD_BYTES = 21 * 2**20
WIDTH = 1024
MIB = 2**20
F32 = jnp.float32
BF16 = jnp.bfloat16


def whole():
    return pl.BlockSpec(memory_space=pltpu.VMEM)


def step_of(depth):
    return max(s for s in range(16, DEPTH_STEP + 1, 16) if depth % s == 0)


def fetch_kernel(weight_ref, held_ref, sem):
    copy = pltpu.make_async_copy(
        weight_ref.at[pl.ds(0, held_ref.shape[0]), :], held_ref, sem
    )
    copy.start()
    copy.wait()


def fetch(weight, rows):
    columns = weight.shape[1]
    return pl.pallas_call(
        fetch_kernel,
        out_shape=pltpu.VMEM((rows, columns), weight.dtype),
        in_specs=[pl.BlockSpec(memory_space=pl.ANY)],
        out_specs=whole(),
        scratch_shapes=[pltpu.SemaphoreType.DMA],
        compiler_params=pltpu.CompilerParams(vmem_limit_bytes=1 * MIB),
        cost_estimate=pl.CostEstimate(
            flops=0, bytes_accessed=2 * rows * columns, transcendentals=0
        ),
        name="fetch",
    )(weight)


def last_parts(step):
    if step % 64:
        return [(0, step)]
    return [(0, step // 2), (step // 2, step // 4), (step // 4 * 3, step // 4)]


def project_kernel(
    own_ref,
    others_ref,
    held_ref,
    weight_ref,
    total_ref,
    sent_ref,
    rows_ref,
    rest_ref,
    sems,
    *,
    tensors,
    sections,
):
    rest, step, columns = rest_ref.shape
    held = held_ref.shape[0] // step
    own_rows = own_ref.shape[0]
    dp = 1 + others_ref.shape[0]
    me = lax.axis_index("dp")
    width = min(columns, WIDTH)

    def copy_of(i, sem, first=0, size=step):
        return pltpu.make_async_copy(
            weight_ref.at[pl.ds((held + i) * step + first, size), :],
            rest_ref.at[i, pl.ds(first, size), :],
            sems.at[sem],
        )

    parts = last_parts(step)
    last = [copy_of(rest - 1, rest - 1 + k, *part) for k, part in enumerate(parts)]
    for i in range(rest - 1):
        copy_of(i, i).start()
    for copy in last:
        copy.start()

    for i in range(held + rest):
        block = slice(i * step, (i + 1) * step)
        for shift in range(dp):
            first = pl.multiple_of((me + dp - shift) % dp * own_rows, own_rows)
            source = own_ref[:, block] if shift == 0 else others_ref[shift - 1, :, block]
            rows_ref[i, pl.ds(first, own_rows), :] = source

    def held_step(n, _):
        lanes = pl.ds(pl.multiple_of(n * width, width), width)
        total_ref[:, lanes] = sum(
            jnp.dot(
                rows_ref[i], held_ref[i * step : (i + 1) * step, lanes], preferred_element_type=F32
            )
            for i in range(held)
        )
        return 0

    def add(i, part=slice(None)):
        for n in range(0, columns, width):
            lanes = slice(n, n + width)
            total_ref[:, lanes] += jnp.dot(
                rows_ref[held + i, :, part], rest_ref[i, part, lanes], preferred_element_type=F32
            )

    def rest_step(i, _):
        copy_of(i, i).wait()
        add(i)
        return 0

    lax.fori_loop(0, columns // width, held_step, 0)
    lax.fori_loop(0, rest - 1, rest_step, 0)
    for copy, (first, size) in zip(last, parts):
        copy.wait()
        add(rest - 1, slice(first, first + size))

    for turn in range(1, sections):
        for n in range(0, columns, width):
            lanes = slice(n, n + width)
            rows = rows_of(turn, total_ref, lanes, tensors, sections)
            sent_ref[turn - 1, :, lanes] = rows.astype(BF16)


def rows_of(turn, total_ref, lanes, tensors, sections):
    tensor, section = lax.axis_index("tensor"), lax.axis_index("section")
    block_rows = total_ref.shape[0] // (tensors * sections)
    group = sections * block_rows
    blocks = []
    for k in range(tensors):
        first = pl.multiple_of(partner_of(tensor, k, tensors) * group, group)
        rows = total_ref[pl.ds(first, group), lanes]
        rows = pltpu.roll(rows, (sections - section) % sections * block_rows, 0)
        part = (turn + (k > 0)) % sections
        blocks.append(rows[part * block_rows : (part + 1) * block_rows])
    return jnp.concatenate(blocks, axis=0)


def keep_kernel(total_ref, kept_ref, *, tensors, sections):
    columns = total_ref.shape[1]
    width = min(columns, WIDTH)
    for n in range(0, columns, width):
        lanes = slice(n, n + width)
        kept_ref[:, lanes] = rows_of(0, total_ref, lanes, tensors, sections)


def keep(total, tensors, sections):
    rows, columns = total.shape
    return pl.pallas_call(
        functools.partial(keep_kernel, tensors=tensors, sections=sections),
        out_shape=jax.ShapeDtypeStruct((rows // sections, columns), F32),
        in_specs=[whole()],
        out_specs=whole(),
        compiler_params=pltpu.CompilerParams(vmem_limit_bytes=4 * MIB),
        name="keep",
    )(total)


def project(own, others, held, weight, tensors, sections):
    own_rows, depth = own.shape
    rows = own_rows * (1 + others.shape[0])
    columns = weight.shape[1]
    step = step_of(depth)
    rest = (depth - held.shape[0]) // step
    return pl.pallas_call(
        functools.partial(project_kernel, tensors=tensors, sections=sections),
        out_shape=(
            pltpu.VMEM((rows, columns), F32),
            pltpu.VMEM((sections - 1, rows // sections, columns), BF16),
        ),
        in_specs=[whole(), whole(), whole(), pl.BlockSpec(memory_space=pl.ANY)],
        out_specs=(whole(), whole()),
        scratch_shapes=[
            pltpu.VMEM((depth // step, rows, step), BF16),
            pltpu.VMEM((rest, step, columns), BF16),
            pltpu.SemaphoreType.DMA((rest - 1 + len(last_parts(step)),)),
        ],
        compiler_params=pltpu.CompilerParams(vmem_limit_bytes=36 * MIB),
        cost_estimate=pl.CostEstimate(
            flops=2 * rows * depth * columns,
            bytes_accessed=2 * rest * step * columns,
            transcendentals=0,
        ),
        name="project",
    )(own, others, held, weight)


def partner_of(me, turn, count):
    if count & (count - 1) == 0:
        return me ^ turn
    return (me + turn) % count


def turn_of(me, partner, count):
    if count & (count - 1) == 0:
        return me ^ partner
    return (partner - me) % count


def exchange_plan(count):
    if count == 4:
        return [(2, 3, 1, 0), (3, 2, 0, 1), (1, 0, 3, 2)]
    turns = range(count - 1, 0, -1)
    return [tuple(partner_of(i, turn, count) for i in range(count)) for turn in turns]


def pair_kernel(kept_ref, *refs, plan, tensors):
    arrived, (own_ref, *outs) = refs[: -1 - len(plan)], refs[-1 - len(plan) :]
    me = lax.axis_index("tensor")
    block_rows = own_ref.shape[0]
    total = kept_ref[...]
    for piece in arrived:
        total = total + piece[...].astype(F32)
    blocks = [total[turn * block_rows : (turn + 1) * block_rows] for turn in range(tensors)]
    own_ref[...] = blocks[0]
    for receivers, out_ref in zip(plan, outs):
        turns = [turn_of(i, j, tensors) for i, j in enumerate(receivers)]
        block = blocks[turns[0]]
        for i, turn in enumerate(turns):
            if turn != turns[0]:
                block = jnp.where(me == i, blocks[turn], block)
        out_ref[...] = block.astype(out_ref.dtype)


def pair(kept, arrived, plan, tensors):
    rows, columns = kept.shape
    block = (rows // tensors, columns)
    return pl.pallas_call(
        functools.partial(pair_kernel, plan=plan, tensors=tensors),
        out_shape=[jax.ShapeDtypeStruct(block, F32)] + [jax.ShapeDtypeStruct(block, BF16)] * len(plan),
        in_specs=[whole()] * (1 + len(arrived)),
        out_specs=[whole()] * (1 + len(plan)),
        compiler_params=pltpu.CompilerParams(vmem_limit_bytes=8 * MIB),
        name="pair",
    )(kept, *arrived)


def places_of(row, slots, owners, local):
    rows = row.shape[1]
    upper = lax.broadcasted_iota(jnp.int32, (rows, rows), 0)
    lower = lax.broadcasted_iota(jnp.int32, (rows, rows), 1)
    column = jnp.sum(jnp.where(upper == lower, row, 0), axis=1, keepdims=True)
    before = jnp.logical_and(column == row, upper < lower)
    rank_of = jnp.sum(before.astype(jnp.int32), axis=0, keepdims=True)
    slot = lax.broadcasted_iota(jnp.int32, (slots * owners, rows), 0)
    owner = (lax.axis_index("dp") + slot // slots) % owners
    adapter = owner * local + slot // MOST % local
    return jnp.logical_and(row == adapter, rank_of == slot % MOST).astype(F32)


def prepare_kernel(
    index_ref, gain_ref, shrink_ref, places_ref, folded_ref, raw_ref, sem, *, slots, owners
):
    copy = pltpu.make_async_copy(shrink_ref, raw_ref, sem)
    copy.start()
    places_ref[...] = places_of(index_ref[...], slots, owners, slots // MOST)
    copy.wait()
    local, rank, features = raw_ref.shape
    width = min(features, WIDTH)
    for adapter in range(local):
        for n in range(0, features, width):
            lanes = slice(n, n + width)
            scaled = raw_ref[adapter, :, lanes].astype(F32) * gain_ref[:, lanes].astype(F32)
            high = scaled.astype(BF16)
            folded_ref[adapter, :rank, lanes] = high
            folded_ref[adapter, rank:, lanes] = (scaled - high.astype(F32)).astype(BF16)


def prepare(index, gain, shrink, slots, owners):
    local, rank, features = shrink.shape
    return pl.pallas_call(
        functools.partial(prepare_kernel, slots=slots, owners=owners),
        out_shape=(
            jax.ShapeDtypeStruct((slots * owners, index.shape[1]), F32),
            pltpu.VMEM((local, 2 * rank, features), shrink.dtype),
        ),
        in_specs=[whole(), whole(), pl.BlockSpec(memory_space=pl.ANY)],
        out_specs=(whole(), whole()),
        scratch_shapes=[pltpu.VMEM(shrink.shape, shrink.dtype), pltpu.SemaphoreType.DMA],
        compiler_params=pltpu.CompilerParams(vmem_limit_bytes=4 * MIB),
        name="prepare",
    )(index, gain, pltpu.with_memory_space_constraint(shrink, pltpu.HBM))


def mix_kernel(residual_ref, places_ref, own_ref, *refs):
    arrived, (mixed_ref, kept_ref, sent_ref) = refs[:-3], refs[-3:]
    slots = kept_ref.shape[0]
    places = places_ref[...]
    total = own_ref[...] + residual_ref[...].astype(F32)
    for piece in arrived:
        total = total + piece[...].astype(F32)
    mixed = total.astype(BF16)
    mixed_ref[...] = mixed
    widened = mixed.astype(F32)
    routed = sum(
        places[:, row : row + 1] * widened[row : row + 1, :] for row in range(widened.shape[0])
    )
    kept_ref[...] = routed[:slots]
    for turn in range(sent_ref.shape[0]):
        sent_ref[turn] = routed[(turn + 1) * slots : (turn + 2) * slots].astype(BF16)


def mix(residual, places, own, arrived, slots, owners):
    rows, columns = residual.shape
    return pl.pallas_call(
        mix_kernel,
        out_shape=(
            pltpu.VMEM((rows, columns), BF16),
            jax.ShapeDtypeStruct((slots, columns), F32),
            jax.ShapeDtypeStruct((owners - 1, slots, columns), BF16),
        ),
        in_specs=[whole()] * (3 + len(arrived)),
        out_specs=(whole(),) * 3,
        compiler_params=pltpu.CompilerParams(vmem_limit_bytes=8 * MIB),
        name="mix",
    )(residual, places, own, *arrived)


def partial_values(rows, folded_ref, place):
    columns = rows.shape[1]
    first = pl.multiple_of(place * columns, columns)
    local, rank = folded_ref.shape[0], folded_ref.shape[1] // 2
    values = []
    for adapter in range(local):
        product = lax.dot_general(
            rows[adapter * MOST : (adapter + 1) * MOST],
            folded_ref[adapter, :, pl.ds(first, columns)],
            (((1,), (1,)), ((), ())),
            preferred_element_type=F32,
        )
        values.append(product[:, :rank] + product[:, rank:])
    widened = rows.astype(F32)
    squares = jnp.sum(widened * widened, axis=1, keepdims=True)
    return jnp.concatenate(values, axis=0), squares


def own_half_kernel(rows_ref, folded_ref, values_ref, squares_ref):
    values, squares = partial_values(
        rows_ref[...].astype(BF16), folded_ref, lax.axis_index("dp")
    )
    values_ref[...] = values
    squares_ref[...] = jnp.broadcast_to(squares, squares_ref.shape)


def own_half(rows, folded):
    slots = rows.shape[0]
    rank = folded.shape[1] // 2
    return pl.pallas_call(
        own_half_kernel,
        out_shape=(
            jax.ShapeDtypeStruct((slots, rank), F32),
            jax.ShapeDtypeStruct((slots, rank), F32),
        ),
        in_specs=[whole()] * 2,
        out_specs=(whole(),) * 2,
        compiler_params=pltpu.CompilerParams(vmem_limit_bytes=8 * MIB),
        cost_estimate=pl.CostEstimate(
            flops=4 * slots * rows.shape[1] * rank, bytes_accessed=2 * MIB, transcendentals=0
        ),
        name="own_half",
    )(rows, folded)


def finish_kernel(values_ref, squares_ref, folded_ref, *refs):
    arrived, out_ref = refs[:-1], refs[-1]
    dp = 1 + len(arrived)
    me = lax.axis_index("dp")
    local = folded_ref.shape[0]
    columns = arrived[0].shape[1]
    values, squares = values_ref[...], squares_ref[:, :1]
    for shift, piece in enumerate(arrived, start=1):
        more, more_squares = partial_values(piece[...], folded_ref, lax.rem(me + dp - shift, dp))
        values, squares = values + more, squares + more_squares
    result = 2.0 * values * lax.rsqrt(squares / (columns * dp) + EPS)
    for adapter in range(local):
        out_ref[adapter, 0] = result[adapter * MOST : (adapter + 1) * MOST]


def finish(values, squares, folded, arrived):
    local, rank = folded.shape[0], folded.shape[1] // 2
    return pl.pallas_call(
        finish_kernel,
        out_shape=jax.ShapeDtypeStruct((local, 1, MOST, rank), F32),
        in_specs=[whole()] * (3 + len(arrived)),
        out_specs=whole(),
        compiler_params=pltpu.CompilerParams(vmem_limit_bytes=8 * MIB),
        name="finish",
    )(values, squares, folded, *arrived)


def shifted(array, axis, shift):
    count = lax.axis_size(axis)
    return lax.ppermute(array, axis, [(i, (i + shift) % count) for i in range(count)])


def across(array, receivers):
    sections = lax.axis_size("section")
    pairs = [
        (i * sections + s, j * sections + (s + 1) % sections)
        for i, j in enumerate(receivers)
        for s in range(sections)
    ]
    return lax.ppermute(array, ("tensor", "section"), pairs)


def body(hidden, down_matrix, residual, next_norm_scale, shrink_matrix, adapter_index):
    dp, tensors, sections = (lax.axis_size(axis) for axis in ("dp", "tensor", "section"))
    depth, _ = down_matrix.shape
    local = shrink_matrix.shape[0]

    others = jnp.stack([shifted(hidden, "dp", shift) for shift in range(1, dp)])

    step = step_of(depth)
    blocks = depth // step
    held_count = max(1, min(blocks // 2, HELD_BYTES // (2 * step * down_matrix.shape[1])))
    held = fetch(down_matrix, held_count * step)

    shrink = jnp.swapaxes(shrink_matrix, 1, 2)
    gain = next_norm_scale[None, :]

    in_vmem = [pltpu.with_memory_space_constraint(x, pltpu.VMEM) for x in (hidden, others, held)]
    total, sent = project(*in_vmem, down_matrix, tensors, sections)
    index, total = lax.optimization_barrier((adapter_index.reshape(1, -1), total))
    kept = keep(total, tensors, sections)
    places, folded = prepare(index, gain, shrink, local * MOST, dp)
    arrived = [shifted(sent[s - 1], "section", s) for s in range(1, sections)]
    plan = exchange_plan(tensors)
    own, *sums = pair(kept, arrived, plan, tensors)
    arrived = [across(x, receivers) for x, receivers in zip(sums, plan)]
    mixed, routed, leaving = mix(residual, places, own, arrived, local * MOST, dp)
    arrived = [shifted(leaving[s - 1], "dp", s) for s in range(1, dp)]
    values, squares = own_half(routed, folded)
    shrunk = finish(values, squares, folded, arrived)
    return (mixed, shrunk)


def solution(mesh):
    placed = (
        P(("groups", "dp"), ("tensor", "section")),
        P(("tensor", "section"), "dp"),
        P(("groups", "tensor", "section"), "dp"),
        P(),
        P("dp", None, None),
        P(("groups", "tensor", "section"), None),
    )
    return jax.shard_map(
        body,
        mesh=mesh,
        in_specs=placed,
        out_specs=(
            P(("groups", "tensor", "section"), "dp"),
            P("dp", ("groups", "tensor", "section"), None, None),
        ),
        check_vma=False,
    )
```

```python
import functools

import jax
import jax.numpy as jnp
from jax import lax
from jax.experimental import pallas as pl
from jax.experimental.pallas import tpu as pltpu
from jax.sharding import PartitionSpec as P

MOST = 2
EPS = 1e-05
DEPTH_STEP = 512
HELD_BYTES = 21 * 2**20
WIDTH = 1024
MIB = 2**20
F32 = jnp.float32
BF16 = jnp.bfloat16


def whole():
    return pl.BlockSpec(memory_space=pltpu.VMEM)


def step_of(depth):
    return max(s for s in range(16, DEPTH_STEP + 1, 16) if depth % s == 0)


def fetch_kernel(weight_ref, held_ref, sem):
    copy = pltpu.make_async_copy(
        weight_ref.at[pl.ds(0, held_ref.shape[0]), :], held_ref, sem
    )
    copy.start()
    copy.wait()


def fetch(weight, rows):
    columns = weight.shape[1]
    return pl.pallas_call(
        fetch_kernel,
        out_shape=pltpu.VMEM((rows, columns), weight.dtype),
        in_specs=[pl.BlockSpec(memory_space=pl.ANY)],
        out_specs=whole(),
        scratch_shapes=[pltpu.SemaphoreType.DMA],
        compiler_params=pltpu.CompilerParams(vmem_limit_bytes=1 * MIB),
        cost_estimate=pl.CostEstimate(
            flops=0, bytes_accessed=2 * rows * columns, transcendentals=0
        ),
        name="fetch",
    )(weight)


def last_parts(step):
    if step % 64:
        return [(0, step)]
    return [(0, step // 2), (step // 2, step // 4), (step // 4 * 3, step // 4)]


def project_kernel(
    own_ref,
    others_ref,
    held_ref,
    weight_ref,
    total_ref,
    sent_ref,
    rows_ref,
    rest_ref,
    sems,
    *,
    tensors,
    sections,
):
    rest, step, columns = rest_ref.shape
    held = held_ref.shape[0] // step
    own_rows = own_ref.shape[0]
    dp = 1 + others_ref.shape[0]
    me = lax.axis_index("dp")
    width = min(columns, WIDTH)

    def copy_of(i, sem, first=0, size=step):
        return pltpu.make_async_copy(
            weight_ref.at[pl.ds((held + i) * step + first, size), :],
            rest_ref.at[i, pl.ds(first, size), :],
            sems.at[sem],
        )

    parts = last_parts(step)
    last = [copy_of(rest - 1, rest - 1 + k, *part) for k, part in enumerate(parts)]
    for i in range(rest - 1):
        copy_of(i, i).start()
    for copy in last:
        copy.start()

    for i in range(held + rest):
        block = slice(i * step, (i + 1) * step)
        for shift in range(dp):
            first = pl.multiple_of((me + dp - shift) % dp * own_rows, own_rows)
            source = own_ref[:, block] if shift == 0 else others_ref[shift - 1, :, block]
            rows_ref[i, pl.ds(first, own_rows), :] = source

    def held_step(n, _):
        lanes = pl.ds(pl.multiple_of(n * width, width), width)
        total_ref[:, lanes] = sum(
            jnp.dot(
                rows_ref[i], held_ref[i * step : (i + 1) * step, lanes], preferred_element_type=F32
            )
            for i in range(held)
        )
        return 0

    def add(i, part=slice(None)):
        for n in range(0, columns, width):
            lanes = slice(n, n + width)
            total_ref[:, lanes] += jnp.dot(
                rows_ref[held + i, :, part], rest_ref[i, part, lanes], preferred_element_type=F32
            )

    def rest_step(i, _):
        copy_of(i, i).wait()
        add(i)
        return 0

    lax.fori_loop(0, columns // width, held_step, 0)
    lax.fori_loop(0, rest - 1, rest_step, 0)
    for copy, (first, size) in zip(last, parts):
        copy.wait()
        add(rest - 1, slice(first, first + size))

    for turn in range(1, sections):
        for n in range(0, columns, width):
            lanes = slice(n, n + width)
            rows = rows_of(turn, total_ref, lanes, tensors, sections)
            sent_ref[turn - 1, :, lanes] = rows.astype(BF16)


def rows_of(turn, total_ref, lanes, tensors, sections):
    tensor, section = lax.axis_index("tensor"), lax.axis_index("section")
    block_rows = total_ref.shape[0] // (tensors * sections)
    group = sections * block_rows
    blocks = []
    for k in range(tensors):
        first = pl.multiple_of(partner_of(tensor, k, tensors) * group, group)
        rows = total_ref[pl.ds(first, group), lanes]
        rows = pltpu.roll(rows, (sections - section) % sections * block_rows, 0)
        part = (turn + (k > 0)) % sections
        blocks.append(rows[part * block_rows : (part + 1) * block_rows])
    return jnp.concatenate(blocks, axis=0)


def keep_kernel(total_ref, kept_ref, *, tensors, sections):
    columns = total_ref.shape[1]
    width = min(columns, WIDTH)
    for n in range(0, columns, width):
        lanes = slice(n, n + width)
        kept_ref[:, lanes] = rows_of(0, total_ref, lanes, tensors, sections)


def keep(total, tensors, sections):
    rows, columns = total.shape
    return pl.pallas_call(
        functools.partial(keep_kernel, tensors=tensors, sections=sections),
        out_shape=jax.ShapeDtypeStruct((rows // sections, columns), F32),
        in_specs=[whole()],
        out_specs=whole(),
        compiler_params=pltpu.CompilerParams(vmem_limit_bytes=4 * MIB),
        name="keep",
    )(total)


def project(own, others, held, weight, tensors, sections):
    own_rows, depth = own.shape
    rows = own_rows * (1 + others.shape[0])
    columns = weight.shape[1]
    step = step_of(depth)
    rest = (depth - held.shape[0]) // step
    return pl.pallas_call(
        functools.partial(project_kernel, tensors=tensors, sections=sections),
        out_shape=(
            pltpu.VMEM((rows, columns), F32),
            pltpu.VMEM((sections - 1, rows // sections, columns), BF16),
        ),
        in_specs=[whole(), whole(), whole(), pl.BlockSpec(memory_space=pl.ANY)],
        out_specs=(whole(), whole()),
        scratch_shapes=[
            pltpu.VMEM((depth // step, rows, step), BF16),
            pltpu.VMEM((rest, step, columns), BF16),
            pltpu.SemaphoreType.DMA((rest - 1 + len(last_parts(step)),)),
        ],
        compiler_params=pltpu.CompilerParams(vmem_limit_bytes=36 * MIB),
        cost_estimate=pl.CostEstimate(
            flops=2 * rows * depth * columns,
            bytes_accessed=2 * rest * step * columns,
            transcendentals=0,
        ),
        name="project",
    )(own, others, held, weight)


def partner_of(me, turn, count):
    if count & (count - 1) == 0:
        return me ^ turn
    return (me + turn) % count


def turn_of(me, partner, count):
    if count & (count - 1) == 0:
        return me ^ partner
    return (partner - me) % count


def exchange_plan(count):
    if count == 4:
        return [(2, 3, 1, 0), (3, 2, 0, 1), (1, 0, 3, 2)]
    turns = range(count - 1, 0, -1)
    return [tuple(partner_of(i, turn, count) for i in range(count)) for turn in turns]


def pair_kernel(kept_ref, *refs, plan, tensors):
    arrived, (own_ref, *outs) = refs[: -1 - len(plan)], refs[-1 - len(plan) :]
    me = lax.axis_index("tensor")
    block_rows = own_ref.shape[0]
    total = kept_ref[...]
    for piece in arrived:
        total = total + piece[...].astype(F32)
    blocks = [total[turn * block_rows : (turn + 1) * block_rows] for turn in range(tensors)]
    own_ref[...] = blocks[0]
    for receivers, out_ref in zip(plan, outs):
        turns = [turn_of(i, j, tensors) for i, j in enumerate(receivers)]
        block = blocks[turns[0]]
        for i, turn in enumerate(turns):
            if turn != turns[0]:
                block = jnp.where(me == i, blocks[turn], block)
        out_ref[...] = block.astype(out_ref.dtype)


def pair(kept, arrived, plan, tensors):
    rows, columns = kept.shape
    block = (rows // tensors, columns)
    return pl.pallas_call(
        functools.partial(pair_kernel, plan=plan, tensors=tensors),
        out_shape=[jax.ShapeDtypeStruct(block, F32)] + [jax.ShapeDtypeStruct(block, BF16)] * len(plan),
        in_specs=[whole()] * (1 + len(arrived)),
        out_specs=[whole()] * (1 + len(plan)),
        compiler_params=pltpu.CompilerParams(vmem_limit_bytes=8 * MIB),
        name="pair",
    )(kept, *arrived)


def places_of(row, slots, owners, local):
    rows = row.shape[1]
    upper = lax.broadcasted_iota(jnp.int32, (rows, rows), 0)
    lower = lax.broadcasted_iota(jnp.int32, (rows, rows), 1)
    column = jnp.sum(jnp.where(upper == lower, row, 0), axis=1, keepdims=True)
    before = jnp.logical_and(column == row, upper < lower)
    rank_of = jnp.sum(before.astype(jnp.int32), axis=0, keepdims=True)
    slot = lax.broadcasted_iota(jnp.int32, (slots * owners, rows), 0)
    owner = (lax.axis_index("dp") + slot // slots) % owners
    adapter = owner * local + slot // MOST % local
    return jnp.logical_and(row == adapter, rank_of == slot % MOST).astype(F32)


def prepare_kernel(index_ref, shrink_ref, places_ref, out_ref, sem, *, slots, owners):
    copy = pltpu.make_async_copy(shrink_ref, out_ref, sem)
    copy.start()
    places_ref[...] = places_of(index_ref[...], slots, owners, slots // MOST)
    copy.wait()


def prepare(index, shrink, slots, owners):
    return pl.pallas_call(
        functools.partial(prepare_kernel, slots=slots, owners=owners),
        out_shape=(
            jax.ShapeDtypeStruct((slots * owners, index.shape[1]), F32),
            pltpu.VMEM(shrink.shape, shrink.dtype),
        ),
        in_specs=[whole(), pl.BlockSpec(memory_space=pl.ANY)],
        out_specs=(whole(), whole()),
        scratch_shapes=[pltpu.SemaphoreType.DMA],
        compiler_params=pltpu.CompilerParams(vmem_limit_bytes=1 * MIB),
        name="prepare",
    )(index, pltpu.with_memory_space_constraint(shrink, pltpu.HBM))


def mix_kernel(residual_ref, places_ref, own_ref, *refs):
    arrived, (mixed_ref, kept_ref, sent_ref) = refs[:-3], refs[-3:]
    slots = kept_ref.shape[0]
    places = places_ref[...]
    total = own_ref[...] + residual_ref[...].astype(F32)
    for piece in arrived:
        total = total + piece[...].astype(F32)
    mixed = total.astype(BF16)
    mixed_ref[...] = mixed
    widened = mixed.astype(F32)
    routed = sum(
        places[:, row : row + 1] * widened[row : row + 1, :] for row in range(widened.shape[0])
    )
    kept_ref[...] = routed[:slots]
    for turn in range(sent_ref.shape[0]):
        sent_ref[turn] = routed[(turn + 1) * slots : (turn + 2) * slots].astype(BF16)


def mix(residual, places, own, arrived, slots, owners):
    rows, columns = residual.shape
    return pl.pallas_call(
        mix_kernel,
        out_shape=(
            pltpu.VMEM((rows, columns), BF16),
            jax.ShapeDtypeStruct((slots, columns), F32),
            jax.ShapeDtypeStruct((owners - 1, slots, columns), BF16),
        ),
        in_specs=[whole()] * (3 + len(arrived)),
        out_specs=(whole(),) * 3,
        compiler_params=pltpu.CompilerParams(vmem_limit_bytes=8 * MIB),
        name="mix",
    )(residual, places, own, *arrived)


def partial_values(rows, gain_ref, shrink_ref, place, columns, local):
    first = pl.multiple_of(place * columns, columns)
    squares = jnp.sum(rows * rows, axis=1, keepdims=True)
    scaled = rows * gain_ref[:, pl.ds(first, columns)].astype(F32)
    high = scaled.astype(BF16)
    low = (scaled - high.astype(F32)).astype(BF16)
    values = []
    for adapter in range(local):
        mine = slice(adapter * MOST, (adapter + 1) * MOST)
        both = jnp.concatenate([high[mine], low[mine]], axis=0)
        product = lax.dot_general(
            shrink_ref[adapter, :, pl.ds(first, columns)],
            both,
            (((1,), (1,)), ((), ())),
            preferred_element_type=F32,
        ).T
        values.append(product[:MOST] + product[MOST:])
    return jnp.concatenate(values, axis=0), squares


def own_half_kernel(rows_ref, gain_ref, shrink_ref, values_ref, squares_ref):
    columns = rows_ref.shape[1]
    values, squares = partial_values(
        rows_ref[...], gain_ref, shrink_ref, lax.axis_index("dp"), columns, shrink_ref.shape[0]
    )
    values_ref[...] = values
    squares_ref[...] = jnp.broadcast_to(squares, squares_ref.shape)


def own_half(rows, gain, shrink):
    slots = rows.shape[0]
    rank = shrink.shape[1]
    return pl.pallas_call(
        own_half_kernel,
        out_shape=(
            jax.ShapeDtypeStruct((slots, rank), F32),
            jax.ShapeDtypeStruct((slots, rank), F32),
        ),
        in_specs=[whole()] * 3,
        out_specs=(whole(),) * 2,
        compiler_params=pltpu.CompilerParams(vmem_limit_bytes=8 * MIB),
        cost_estimate=pl.CostEstimate(
            flops=2 * slots * rows.shape[1] * rank, bytes_accessed=2 * MIB, transcendentals=0
        ),
        name="own_half",
    )(rows, gain, shrink)


def finish_kernel(values_ref, squares_ref, gain_ref, shrink_ref, *refs):
    arrived, out_ref = refs[:-1], refs[-1]
    dp = 1 + len(arrived)
    me = lax.axis_index("dp")
    local = shrink_ref.shape[0]
    columns = arrived[0].shape[1]
    values, squares = values_ref[...], squares_ref[:, :1]
    for shift, piece in enumerate(arrived, start=1):
        more, more_squares = partial_values(
            piece[...].astype(F32),
            gain_ref,
            shrink_ref,
            lax.rem(me + dp - shift, dp),
            columns,
            local,
        )
        values, squares = values + more, squares + more_squares
    result = 2.0 * values * lax.rsqrt(squares / (columns * dp) + EPS)
    for adapter in range(local):
        out_ref[adapter, 0] = result[adapter * MOST : (adapter + 1) * MOST]


def finish(values, squares, gain, shrink, arrived):
    local, rank, _ = shrink.shape
    return pl.pallas_call(
        finish_kernel,
        out_shape=jax.ShapeDtypeStruct((local, 1, MOST, rank), F32),
        in_specs=[whole()] * (4 + len(arrived)),
        out_specs=whole(),
        compiler_params=pltpu.CompilerParams(vmem_limit_bytes=8 * MIB),
        name="finish",
    )(values, squares, gain, shrink, *arrived)


def shifted(array, axis, shift):
    count = lax.axis_size(axis)
    return lax.ppermute(array, axis, [(i, (i + shift) % count) for i in range(count)])


def across(array, receivers):
    sections = lax.axis_size("section")
    pairs = [
        (i * sections + s, j * sections + (s + 1) % sections)
        for i, j in enumerate(receivers)
        for s in range(sections)
    ]
    return lax.ppermute(array, ("tensor", "section"), pairs)


def body(hidden, down_matrix, residual, next_norm_scale, shrink_matrix, adapter_index):
    dp, tensors, sections = (lax.axis_size(axis) for axis in ("dp", "tensor", "section"))
    depth, _ = down_matrix.shape
    local = shrink_matrix.shape[0]

    others = jnp.stack([shifted(hidden, "dp", shift) for shift in range(1, dp)])

    step = step_of(depth)
    blocks = depth // step
    held_count = max(1, min(blocks // 2, HELD_BYTES // (2 * step * down_matrix.shape[1])))
    held = fetch(down_matrix, held_count * step)

    shrink = jnp.swapaxes(shrink_matrix, 1, 2)
    gain = next_norm_scale[None, :]

    in_vmem = [pltpu.with_memory_space_constraint(x, pltpu.VMEM) for x in (hidden, others, held)]
    total, sent = project(*in_vmem, down_matrix, tensors, sections)
    index, total = lax.optimization_barrier((adapter_index.reshape(1, -1), total))
    kept = keep(total, tensors, sections)
    places, shrink = prepare(index, shrink, local * MOST, dp)
    arrived = [shifted(sent[s - 1], "section", s) for s in range(1, sections)]
    plan = exchange_plan(tensors)
    own, *sums = pair(kept, arrived, plan, tensors)
    arrived = [across(x, receivers) for x, receivers in zip(sums, plan)]
    mixed, routed, leaving = mix(residual, places, own, arrived, local * MOST, dp)
    arrived = [shifted(leaving[s - 1], "dp", s) for s in range(1, dp)]
    values, squares = own_half(routed, gain, shrink)
    shrunk = finish(values, squares, gain, shrink, arrived)
    return (mixed, shrunk)


def solution(mesh):
    placed = (
        P(("groups", "dp"), ("tensor", "section")),
        P(("tensor", "section"), "dp"),
        P(("groups", "tensor", "section"), "dp"),
        P(),
        P("dp", None, None),
        P(("groups", "tensor", "section"), None),
    )
    return jax.shard_map(
        body,
        mesh=mesh,
        in_specs=placed,
        out_specs=(
            P(("groups", "tensor", "section"), "dp"),
            P("dp", ("groups", "tensor", "section"), None, None),
        ),
        check_vma=False,
    )
```

```python
import functools

import jax
import jax.numpy as jnp
from jax import lax
from jax.experimental import pallas as pl
from jax.experimental.pallas import tpu as pltpu
from jax.sharding import PartitionSpec as P

MOST = 2
EPS = 1e-05
DEPTH_STEP = 512
HELD_BYTES = 21 * 2**20
WIDTH = 1024
MIB = 2**20
F32 = jnp.float32
BF16 = jnp.bfloat16


def whole():
    return pl.BlockSpec(memory_space=pltpu.VMEM)


def step_of(depth):
    return max(s for s in range(16, DEPTH_STEP + 1, 16) if depth % s == 0)


def fetch_kernel(weight_ref, held_ref, sem):
    copy = pltpu.make_async_copy(
        weight_ref.at[pl.ds(0, held_ref.shape[0]), :], held_ref, sem
    )
    copy.start()
    copy.wait()


def fetch(weight, rows):
    columns = weight.shape[1]
    return pl.pallas_call(
        fetch_kernel,
        out_shape=pltpu.VMEM((rows, columns), weight.dtype),
        in_specs=[pl.BlockSpec(memory_space=pl.ANY)],
        out_specs=whole(),
        scratch_shapes=[pltpu.SemaphoreType.DMA],
        compiler_params=pltpu.CompilerParams(vmem_limit_bytes=1 * MIB),
        cost_estimate=pl.CostEstimate(
            flops=0, bytes_accessed=2 * rows * columns, transcendentals=0
        ),
        name="fetch",
    )(weight)


def last_parts(step):
    if step % 64:
        return [(0, step)]
    return [(0, step // 2), (step // 2, step // 4), (step // 4 * 3, step // 4)]


def project_kernel(
    own_ref,
    others_ref,
    held_ref,
    weight_ref,
    total_ref,
    sent_ref,
    rows_ref,
    rest_ref,
    sems,
    *,
    tensors,
    sections,
):
    rest, step, columns = rest_ref.shape
    held = held_ref.shape[0] // step
    own_rows = own_ref.shape[0]
    dp = 1 + others_ref.shape[0]
    me = lax.axis_index("dp")
    width = min(columns, WIDTH)

    def copy_of(i, sem, first=0, size=step):
        return pltpu.make_async_copy(
            weight_ref.at[pl.ds((held + i) * step + first, size), :],
            rest_ref.at[i, pl.ds(first, size), :],
            sems.at[sem],
        )

    parts = last_parts(step)
    last = [copy_of(rest - 1, rest - 1 + k, *part) for k, part in enumerate(parts)]
    for i in range(rest - 1):
        copy_of(i, i).start()
    for copy in last:
        copy.start()

    for i in range(held + rest):
        block = slice(i * step, (i + 1) * step)
        for shift in range(dp):
            first = pl.multiple_of((me + dp - shift) % dp * own_rows, own_rows)
            source = own_ref[:, block] if shift == 0 else others_ref[shift - 1, :, block]
            rows_ref[i, pl.ds(first, own_rows), :] = source

    def held_step(n, _):
        lanes = pl.ds(pl.multiple_of(n * width, width), width)
        total_ref[:, lanes] = sum(
            jnp.dot(
                rows_ref[i], held_ref[i * step : (i + 1) * step, lanes], preferred_element_type=F32
            )
            for i in range(held)
        )
        return 0

    def add(i, part=slice(None)):
        for n in range(0, columns, width):
            lanes = slice(n, n + width)
            total_ref[:, lanes] += jnp.dot(
                rows_ref[held + i, :, part], rest_ref[i, part, lanes], preferred_element_type=F32
            )

    def rest_step(i, _):
        copy_of(i, i).wait()
        add(i)
        return 0

    lax.fori_loop(0, columns // width, held_step, 0)
    lax.fori_loop(0, rest - 1, rest_step, 0)
    for copy, (first, size) in zip(last, parts):
        copy.wait()
        add(rest - 1, slice(first, first + size))

    for turn in range(1, sections):
        for n in range(0, columns, width):
            lanes = slice(n, n + width)
            rows = rows_of(turn, total_ref, lanes, tensors, sections)
            sent_ref[turn - 1, :, lanes] = rows.astype(BF16)


def rows_of(turn, total_ref, lanes, tensors, sections):
    tensor, section = lax.axis_index("tensor"), lax.axis_index("section")
    block_rows = total_ref.shape[0] // (tensors * sections)
    group = sections * block_rows
    blocks = []
    for k in range(tensors):
        first = pl.multiple_of(partner_of(tensor, k, tensors) * group, group)
        rows = total_ref[pl.ds(first, group), lanes]
        rows = pltpu.roll(rows, (sections - section) % sections * block_rows, 0)
        part = (turn + (k > 0)) % sections
        blocks.append(rows[part * block_rows : (part + 1) * block_rows])
    return jnp.concatenate(blocks, axis=0)


def keep_kernel(total_ref, kept_ref, *, tensors, sections):
    columns = total_ref.shape[1]
    width = min(columns, WIDTH)
    for n in range(0, columns, width):
        lanes = slice(n, n + width)
        kept_ref[:, lanes] = rows_of(0, total_ref, lanes, tensors, sections)


def keep(total, tensors, sections):
    rows, columns = total.shape
    return pl.pallas_call(
        functools.partial(keep_kernel, tensors=tensors, sections=sections),
        out_shape=jax.ShapeDtypeStruct((rows // sections, columns), F32),
        in_specs=[whole()],
        out_specs=whole(),
        compiler_params=pltpu.CompilerParams(vmem_limit_bytes=4 * MIB),
        name="keep",
    )(total)


def project(own, others, held, weight, tensors, sections):
    own_rows, depth = own.shape
    rows = own_rows * (1 + others.shape[0])
    columns = weight.shape[1]
    step = step_of(depth)
    rest = (depth - held.shape[0]) // step
    return pl.pallas_call(
        functools.partial(project_kernel, tensors=tensors, sections=sections),
        out_shape=(
            pltpu.VMEM((rows, columns), F32),
            pltpu.VMEM((sections - 1, rows // sections, columns), BF16),
        ),
        in_specs=[whole(), whole(), whole(), pl.BlockSpec(memory_space=pl.ANY)],
        out_specs=(whole(), whole()),
        scratch_shapes=[
            pltpu.VMEM((depth // step, rows, step), BF16),
            pltpu.VMEM((rest, step, columns), BF16),
            pltpu.SemaphoreType.DMA((rest - 1 + len(last_parts(step)),)),
        ],
        compiler_params=pltpu.CompilerParams(vmem_limit_bytes=36 * MIB),
        cost_estimate=pl.CostEstimate(
            flops=2 * rows * depth * columns,
            bytes_accessed=2 * rest * step * columns,
            transcendentals=0,
        ),
        name="project",
    )(own, others, held, weight)


def partner_of(me, turn, count):
    if count & (count - 1) == 0:
        return me ^ turn
    return (me + turn) % count


def turn_of(me, partner, count):
    if count & (count - 1) == 0:
        return me ^ partner
    return (partner - me) % count


def exchange_plan(count):
    if count == 4:
        return [(2, 3, 1, 0), (3, 2, 0, 1), (1, 0, 3, 2)]
    turns = range(count - 1, 0, -1)
    return [tuple(partner_of(i, turn, count) for i in range(count)) for turn in turns]


def pair_kernel(kept_ref, *refs, plan, tensors):
    arrived, (own_ref, *outs) = refs[: -1 - len(plan)], refs[-1 - len(plan) :]
    me = lax.axis_index("tensor")
    block_rows = own_ref.shape[0]
    total = kept_ref[...]
    for piece in arrived:
        total = total + piece[...].astype(F32)
    blocks = [total[turn * block_rows : (turn + 1) * block_rows] for turn in range(tensors)]
    own_ref[...] = blocks[0]
    for receivers, out_ref in zip(plan, outs):
        turns = [turn_of(i, j, tensors) for i, j in enumerate(receivers)]
        block = blocks[turns[0]]
        for i, turn in enumerate(turns):
            if turn != turns[0]:
                block = jnp.where(me == i, blocks[turn], block)
        out_ref[...] = block.astype(out_ref.dtype)


def pair(kept, arrived, plan, tensors):
    rows, columns = kept.shape
    block = (rows // tensors, columns)
    return pl.pallas_call(
        functools.partial(pair_kernel, plan=plan, tensors=tensors),
        out_shape=[jax.ShapeDtypeStruct(block, F32)] + [jax.ShapeDtypeStruct(block, BF16)] * len(plan),
        in_specs=[whole()] * (1 + len(arrived)),
        out_specs=[whole()] * (1 + len(plan)),
        compiler_params=pltpu.CompilerParams(vmem_limit_bytes=8 * MIB),
        name="pair",
    )(kept, *arrived)


def places_of(row, slots, owners, local):
    rows = row.shape[1]
    upper = lax.broadcasted_iota(jnp.int32, (rows, rows), 0)
    lower = lax.broadcasted_iota(jnp.int32, (rows, rows), 1)
    column = jnp.sum(jnp.where(upper == lower, row, 0), axis=1, keepdims=True)
    before = jnp.logical_and(column == row, upper < lower)
    rank_of = jnp.sum(before.astype(jnp.int32), axis=0, keepdims=True)
    slot = lax.broadcasted_iota(jnp.int32, (slots * owners, rows), 0)
    owner = (lax.axis_index("dp") + slot // slots) % owners
    adapter = owner * local + slot // MOST % local
    return jnp.logical_and(row == adapter, rank_of == slot % MOST).astype(F32)


def prepare_kernel(index_ref, shrink_ref, places_ref, out_ref, raw_ref, sem, *, slots, owners):
    copy = pltpu.make_async_copy(shrink_ref, raw_ref, sem)
    copy.start()
    places_ref[...] = places_of(index_ref[...], slots, owners, slots // MOST)
    copy.wait()
    local, _, features = raw_ref.shape
    width = min(features, WIDTH)
    for adapter in range(local):
        for n in range(0, features, width):
            block = raw_ref[adapter, :, n : n + width].astype(F32)
            out_ref[adapter, n : n + width, :] = block.T.astype(BF16)


def prepare(index, shrink, slots, owners):
    return pl.pallas_call(
        functools.partial(prepare_kernel, slots=slots, owners=owners),
        out_shape=(
            jax.ShapeDtypeStruct((slots * owners, index.shape[1]), F32),
            pltpu.VMEM((shrink.shape[0], shrink.shape[2], shrink.shape[1]), shrink.dtype),
        ),
        in_specs=[whole(), pl.BlockSpec(memory_space=pl.ANY)],
        out_specs=(whole(), whole()),
        scratch_shapes=[pltpu.VMEM(shrink.shape, shrink.dtype), pltpu.SemaphoreType.DMA],
        compiler_params=pltpu.CompilerParams(vmem_limit_bytes=6 * MIB),
        name="prepare",
    )(index, pltpu.with_memory_space_constraint(shrink, pltpu.HBM))


def mix_kernel(residual_ref, places_ref, own_ref, *refs):
    arrived, (mixed_ref, kept_ref, sent_ref) = refs[:-3], refs[-3:]
    slots = kept_ref.shape[0]
    places = places_ref[...]
    total = own_ref[...] + residual_ref[...].astype(F32)
    for piece in arrived:
        total = total + piece[...].astype(F32)
    mixed = total.astype(BF16)
    mixed_ref[...] = mixed
    widened = mixed.astype(F32)
    routed = sum(
        places[:, row : row + 1] * widened[row : row + 1, :] for row in range(widened.shape[0])
    )
    kept_ref[...] = routed[:slots]
    for turn in range(sent_ref.shape[0]):
        sent_ref[turn] = routed[(turn + 1) * slots : (turn + 2) * slots].astype(BF16)


def mix(residual, places, own, arrived, slots, owners):
    rows, columns = residual.shape
    return pl.pallas_call(
        mix_kernel,
        out_shape=(
            pltpu.VMEM((rows, columns), BF16),
            jax.ShapeDtypeStruct((slots, columns), F32),
            jax.ShapeDtypeStruct((owners - 1, slots, columns), BF16),
        ),
        in_specs=[whole()] * (3 + len(arrived)),
        out_specs=(whole(),) * 3,
        compiler_params=pltpu.CompilerParams(vmem_limit_bytes=8 * MIB),
        name="mix",
    )(residual, places, own, *arrived)


def partial_values(rows, gain_ref, shrink_ref, place, columns, local):
    first = pl.multiple_of(place * columns, columns)
    squares = jnp.sum(rows * rows, axis=1, keepdims=True)
    scaled = rows * gain_ref[:, pl.ds(first, columns)].astype(F32)
    high = scaled.astype(BF16)
    low = (scaled - high.astype(F32)).astype(BF16)
    values = []
    for adapter in range(local):
        mine = slice(adapter * MOST, (adapter + 1) * MOST)
        both = jnp.concatenate([high[mine], low[mine]], axis=0)
        product = jnp.dot(
            both, shrink_ref[adapter, pl.ds(first, columns), :], preferred_element_type=F32
        )
        values.append(product[:MOST] + product[MOST:])
    return jnp.concatenate(values, axis=0), squares


def own_half_kernel(rows_ref, gain_ref, shrink_ref, values_ref, squares_ref):
    columns = rows_ref.shape[1]
    values, squares = partial_values(
        rows_ref[...], gain_ref, shrink_ref, lax.axis_index("dp"), columns, shrink_ref.shape[0]
    )
    values_ref[...] = values
    squares_ref[...] = jnp.broadcast_to(squares, squares_ref.shape)


def own_half(rows, gain, shrink):
    slots = rows.shape[0]
    rank = shrink.shape[2]
    return pl.pallas_call(
        own_half_kernel,
        out_shape=(
            jax.ShapeDtypeStruct((slots, rank), F32),
            jax.ShapeDtypeStruct((slots, rank), F32),
        ),
        in_specs=[whole()] * 3,
        out_specs=(whole(),) * 2,
        compiler_params=pltpu.CompilerParams(vmem_limit_bytes=8 * MIB),
        cost_estimate=pl.CostEstimate(
            flops=2 * slots * rows.shape[1] * rank, bytes_accessed=2 * MIB, transcendentals=0
        ),
        name="own_half",
    )(rows, gain, shrink)


def finish_kernel(values_ref, squares_ref, gain_ref, shrink_ref, *refs):
    arrived, out_ref = refs[:-1], refs[-1]
    dp = 1 + len(arrived)
    me = lax.axis_index("dp")
    local = shrink_ref.shape[0]
    columns = arrived[0].shape[1]
    values, squares = values_ref[...], squares_ref[:, :1]
    for shift, piece in enumerate(arrived, start=1):
        more, more_squares = partial_values(
            piece[...].astype(F32),
            gain_ref,
            shrink_ref,
            lax.rem(me + dp - shift, dp),
            columns,
            local,
        )
        values, squares = values + more, squares + more_squares
    result = 2.0 * values * lax.rsqrt(squares / (columns * dp) + EPS)
    for adapter in range(local):
        out_ref[adapter, 0] = result[adapter * MOST : (adapter + 1) * MOST]


def finish(values, squares, gain, shrink, arrived):
    local, _, rank = shrink.shape
    return pl.pallas_call(
        finish_kernel,
        out_shape=jax.ShapeDtypeStruct((local, 1, MOST, rank), F32),
        in_specs=[whole()] * (4 + len(arrived)),
        out_specs=whole(),
        compiler_params=pltpu.CompilerParams(vmem_limit_bytes=8 * MIB),
        name="finish",
    )(values, squares, gain, shrink, *arrived)


def shifted(array, axis, shift):
    count = lax.axis_size(axis)
    return lax.ppermute(array, axis, [(i, (i + shift) % count) for i in range(count)])


def across(array, receivers):
    sections = lax.axis_size("section")
    pairs = [
        (i * sections + s, j * sections + (s + 1) % sections)
        for i, j in enumerate(receivers)
        for s in range(sections)
    ]
    return lax.ppermute(array, ("tensor", "section"), pairs)


def body(hidden, down_matrix, residual, next_norm_scale, shrink_matrix, adapter_index):
    dp, tensors, sections = (lax.axis_size(axis) for axis in ("dp", "tensor", "section"))
    depth, _ = down_matrix.shape
    local = shrink_matrix.shape[0]

    others = jnp.stack([shifted(hidden, "dp", shift) for shift in range(1, dp)])

    step = step_of(depth)
    blocks = depth // step
    held_count = max(1, min(blocks // 2, HELD_BYTES // (2 * step * down_matrix.shape[1])))
    held = fetch(down_matrix, held_count * step)

    shrink = jnp.swapaxes(shrink_matrix, 1, 2)
    gain = next_norm_scale[None, :]

    in_vmem = [pltpu.with_memory_space_constraint(x, pltpu.VMEM) for x in (hidden, others, held)]
    total, sent = project(*in_vmem, down_matrix, tensors, sections)
    index, total = lax.optimization_barrier((adapter_index.reshape(1, -1), total))
    kept = keep(total, tensors, sections)
    places, shrink = prepare(index, shrink, local * MOST, dp)
    arrived = [shifted(sent[s - 1], "section", s) for s in range(1, sections)]
    plan = exchange_plan(tensors)
    own, *sums = pair(kept, arrived, plan, tensors)
    arrived = [across(x, receivers) for x, receivers in zip(sums, plan)]
    mixed, routed, leaving = mix(residual, places, own, arrived, local * MOST, dp)
    arrived = [shifted(leaving[s - 1], "dp", s) for s in range(1, dp)]
    values, squares = own_half(routed, gain, shrink)
    shrunk = finish(values, squares, gain, shrink, arrived)
    return (mixed, shrunk)


def solution(mesh):
    placed = (
        P(("groups", "dp"), ("tensor", "section")),
        P(("tensor", "section"), "dp"),
        P(("groups", "tensor", "section"), "dp"),
        P(),
        P("dp", None, None),
        P(("groups", "tensor", "section"), None),
    )
    return jax.shard_map(
        body,
        mesh=mesh,
        in_specs=placed,
        out_specs=(
            P(("groups", "tensor", "section"), "dp"),
            P("dp", ("groups", "tensor", "section"), None, None),
        ),
        check_vma=False,
    )
```

```python
import functools

import jax
import jax.numpy as jnp
from jax import lax
from jax.experimental import pallas as pl
from jax.experimental.pallas import tpu as pltpu
from jax.sharding import PartitionSpec as P

MOST = 2
EPS = 1e-05
DEPTH_STEP = 512
HELD_BYTES = 21 * 2**20
WIDTH = 1024
MIB = 2**20
F32 = jnp.float32
BF16 = jnp.bfloat16


def whole():
    return pl.BlockSpec(memory_space=pltpu.VMEM)


def step_of(depth):
    return max(s for s in range(16, DEPTH_STEP + 1, 16) if depth % s == 0)


def fetch_kernel(weight_ref, held_ref, sem):
    copy = pltpu.make_async_copy(
        weight_ref.at[pl.ds(0, held_ref.shape[0]), :], held_ref, sem
    )
    copy.start()
    copy.wait()


def fetch(weight, rows):
    columns = weight.shape[1]
    return pl.pallas_call(
        fetch_kernel,
        out_shape=pltpu.VMEM((rows, columns), weight.dtype),
        in_specs=[pl.BlockSpec(memory_space=pl.ANY)],
        out_specs=whole(),
        scratch_shapes=[pltpu.SemaphoreType.DMA],
        compiler_params=pltpu.CompilerParams(vmem_limit_bytes=1 * MIB),
        cost_estimate=pl.CostEstimate(
            flops=0, bytes_accessed=2 * rows * columns, transcendentals=0
        ),
        name="fetch",
    )(weight)


def last_parts(step):
    return [(0, step // 2), (step // 2, step // 2)]


def project_kernel(
    own_ref,
    others_ref,
    held_ref,
    weight_ref,
    total_ref,
    sent_ref,
    rows_ref,
    rest_ref,
    sems,
    *,
    tensors,
    sections,
):
    rest, step, columns = rest_ref.shape
    held = held_ref.shape[0] // step
    own_rows = own_ref.shape[0]
    dp = 1 + others_ref.shape[0]
    me = lax.axis_index("dp")
    width = min(columns, WIDTH)

    def copy_of(i, sem, first=0, size=step):
        return pltpu.make_async_copy(
            weight_ref.at[pl.ds((held + i) * step + first, size), :],
            rest_ref.at[i, pl.ds(first, size), :],
            sems.at[sem],
        )

    parts = last_parts(step)
    last = [copy_of(rest - 1, rest - 1 + k, *part) for k, part in enumerate(parts)]
    for i in range(rest - 1):
        copy_of(i, i).start()
    for copy in last:
        copy.start()

    for i in range(held + rest):
        block = slice(i * step, (i + 1) * step)
        for shift in range(dp):
            first = pl.multiple_of((me + dp - shift) % dp * own_rows, own_rows)
            source = own_ref[:, block] if shift == 0 else others_ref[shift - 1, :, block]
            rows_ref[i, pl.ds(first, own_rows), :] = source

    def held_step(n, _):
        lanes = pl.ds(pl.multiple_of(n * width, width), width)
        total_ref[:, lanes] = sum(
            jnp.dot(
                rows_ref[i], held_ref[i * step : (i + 1) * step, lanes], preferred_element_type=F32
            )
            for i in range(held)
        )
        return 0

    def add(i, part=slice(None)):
        for n in range(0, columns, width):
            lanes = slice(n, n + width)
            total_ref[:, lanes] += jnp.dot(
                rows_ref[held + i, :, part], rest_ref[i, part, lanes], preferred_element_type=F32
            )

    def rest_step(i, _):
        copy_of(i, i).wait()
        add(i)
        return 0

    lax.fori_loop(0, columns // width, held_step, 0)
    lax.fori_loop(0, rest - 1, rest_step, 0)
    for copy, (first, size) in zip(last, parts):
        copy.wait()
        add(rest - 1, slice(first, first + size))

    for turn in range(1, sections):
        for n in range(0, columns, width):
            lanes = slice(n, n + width)
            rows = rows_of(turn, total_ref, lanes, tensors, sections)
            sent_ref[turn - 1, :, lanes] = rows.astype(BF16)


def rows_of(turn, total_ref, lanes, tensors, sections):
    tensor, section = lax.axis_index("tensor"), lax.axis_index("section")
    block_rows = total_ref.shape[0] // (tensors * sections)
    group = sections * block_rows
    blocks = []
    for k in range(tensors):
        first = pl.multiple_of(partner_of(tensor, k, tensors) * group, group)
        rows = total_ref[pl.ds(first, group), lanes]
        rows = pltpu.roll(rows, (sections - section) % sections * block_rows, 0)
        part = (turn + (k > 0)) % sections
        blocks.append(rows[part * block_rows : (part + 1) * block_rows])
    return jnp.concatenate(blocks, axis=0)


def keep_kernel(total_ref, kept_ref, *, tensors, sections):
    columns = total_ref.shape[1]
    width = min(columns, WIDTH)
    for n in range(0, columns, width):
        lanes = slice(n, n + width)
        kept_ref[:, lanes] = rows_of(0, total_ref, lanes, tensors, sections)


def keep(total, tensors, sections):
    rows, columns = total.shape
    return pl.pallas_call(
        functools.partial(keep_kernel, tensors=tensors, sections=sections),
        out_shape=jax.ShapeDtypeStruct((rows // sections, columns), F32),
        in_specs=[whole()],
        out_specs=whole(),
        compiler_params=pltpu.CompilerParams(vmem_limit_bytes=4 * MIB),
        name="keep",
    )(total)


def project(own, others, held, weight, tensors, sections):
    own_rows, depth = own.shape
    rows = own_rows * (1 + others.shape[0])
    columns = weight.shape[1]
    step = step_of(depth)
    rest = (depth - held.shape[0]) // step
    return pl.pallas_call(
        functools.partial(project_kernel, tensors=tensors, sections=sections),
        out_shape=(
            pltpu.VMEM((rows, columns), F32),
            pltpu.VMEM((sections - 1, rows // sections, columns), BF16),
        ),
        in_specs=[whole(), whole(), whole(), pl.BlockSpec(memory_space=pl.ANY)],
        out_specs=(whole(), whole()),
        scratch_shapes=[
            pltpu.VMEM((depth // step, rows, step), BF16),
            pltpu.VMEM((rest, step, columns), BF16),
            pltpu.SemaphoreType.DMA((rest - 1 + len(last_parts(step)),)),
        ],
        compiler_params=pltpu.CompilerParams(vmem_limit_bytes=36 * MIB),
        cost_estimate=pl.CostEstimate(
            flops=2 * rows * depth * columns,
            bytes_accessed=2 * rest * step * columns,
            transcendentals=0,
        ),
        name="project",
    )(own, others, held, weight)


def partner_of(me, turn, count):
    if count & (count - 1) == 0:
        return me ^ turn
    return (me + turn) % count


def turn_of(me, partner, count):
    if count & (count - 1) == 0:
        return me ^ partner
    return (partner - me) % count


def exchange_plan(count):
    if count == 4:
        return [(2, 3, 1, 0), (3, 2, 0, 1), (1, 0, 3, 2)]
    turns = range(count - 1, 0, -1)
    return [tuple(partner_of(i, turn, count) for i in range(count)) for turn in turns]


def pair_kernel(kept_ref, *refs, plan, tensors):
    arrived, (own_ref, *outs) = refs[: -1 - len(plan)], refs[-1 - len(plan) :]
    me = lax.axis_index("tensor")
    block_rows = own_ref.shape[0]
    total = kept_ref[...]
    for piece in arrived:
        total = total + piece[...].astype(F32)
    blocks = [total[turn * block_rows : (turn + 1) * block_rows] for turn in range(tensors)]
    own_ref[...] = blocks[0]
    for receivers, out_ref in zip(plan, outs):
        turns = [turn_of(i, j, tensors) for i, j in enumerate(receivers)]
        block = blocks[turns[0]]
        for i, turn in enumerate(turns):
            if turn != turns[0]:
                block = jnp.where(me == i, blocks[turn], block)
        out_ref[...] = block.astype(out_ref.dtype)


def pair(kept, arrived, plan, tensors):
    rows, columns = kept.shape
    block = (rows // tensors, columns)
    return pl.pallas_call(
        functools.partial(pair_kernel, plan=plan, tensors=tensors),
        out_shape=[jax.ShapeDtypeStruct(block, F32)] + [jax.ShapeDtypeStruct(block, BF16)] * len(plan),
        in_specs=[whole()] * (1 + len(arrived)),
        out_specs=[whole()] * (1 + len(plan)),
        compiler_params=pltpu.CompilerParams(vmem_limit_bytes=8 * MIB),
        name="pair",
    )(kept, *arrived)


def places_of(row, slots, owners, local):
    rows = row.shape[1]
    upper = lax.broadcasted_iota(jnp.int32, (rows, rows), 0)
    lower = lax.broadcasted_iota(jnp.int32, (rows, rows), 1)
    column = jnp.sum(jnp.where(upper == lower, row, 0), axis=1, keepdims=True)
    before = jnp.logical_and(column == row, upper < lower)
    rank_of = jnp.sum(before.astype(jnp.int32), axis=0, keepdims=True)
    slot = lax.broadcasted_iota(jnp.int32, (slots * owners, rows), 0)
    owner = (lax.axis_index("dp") + slot // slots) % owners
    adapter = owner * local + slot // MOST % local
    return jnp.logical_and(row == adapter, rank_of == slot % MOST).astype(F32)


def prepare_kernel(index_ref, shrink_ref, places_ref, out_ref, sem, *, slots, owners):
    copy = pltpu.make_async_copy(shrink_ref, out_ref, sem)
    copy.start()
    places_ref[...] = places_of(index_ref[...], slots, owners, slots // MOST)
    copy.wait()


def prepare(index, shrink, slots, owners):
    return pl.pallas_call(
        functools.partial(prepare_kernel, slots=slots, owners=owners),
        out_shape=(
            jax.ShapeDtypeStruct((slots * owners, index.shape[1]), F32),
            pltpu.VMEM(shrink.shape, shrink.dtype),
        ),
        in_specs=[whole(), pl.BlockSpec(memory_space=pl.ANY)],
        out_specs=(whole(), whole()),
        scratch_shapes=[pltpu.SemaphoreType.DMA],
        compiler_params=pltpu.CompilerParams(vmem_limit_bytes=1 * MIB),
        name="prepare",
    )(index, pltpu.with_memory_space_constraint(shrink, pltpu.HBM))


def mix_kernel(residual_ref, places_ref, own_ref, *refs):
    arrived, (mixed_ref, kept_ref, sent_ref) = refs[:-3], refs[-3:]
    slots = kept_ref.shape[0]
    places = places_ref[...]
    total = own_ref[...] + residual_ref[...].astype(F32)
    for piece in arrived:
        total = total + piece[...].astype(F32)
    mixed = total.astype(BF16)
    mixed_ref[...] = mixed
    widened = mixed.astype(F32)
    routed = sum(
        places[:, row : row + 1] * widened[row : row + 1, :] for row in range(widened.shape[0])
    )
    kept_ref[...] = routed[:slots]
    for turn in range(sent_ref.shape[0]):
        sent_ref[turn] = routed[(turn + 1) * slots : (turn + 2) * slots].astype(BF16)


def mix(residual, places, own, arrived, slots, owners):
    rows, columns = residual.shape
    return pl.pallas_call(
        mix_kernel,
        out_shape=(
            pltpu.VMEM((rows, columns), BF16),
            jax.ShapeDtypeStruct((slots, columns), F32),
            jax.ShapeDtypeStruct((owners - 1, slots, columns), BF16),
        ),
        in_specs=[whole()] * (3 + len(arrived)),
        out_specs=(whole(),) * 3,
        compiler_params=pltpu.CompilerParams(vmem_limit_bytes=8 * MIB),
        name="mix",
    )(residual, places, own, *arrived)


def partial_values(rows, gain_ref, shrink_ref, place, columns, local):
    first = pl.multiple_of(place * columns, columns)
    squares = jnp.sum(rows * rows, axis=1, keepdims=True)
    scaled = rows * gain_ref[:, pl.ds(first, columns)].astype(F32)
    high = scaled.astype(BF16)
    low = (scaled - high.astype(F32)).astype(BF16)
    values = []
    for adapter in range(local):
        mine = slice(adapter * MOST, (adapter + 1) * MOST)
        both = jnp.concatenate([high[mine], low[mine]], axis=0)
        product = lax.dot_general(
            both,
            shrink_ref[adapter, :, pl.ds(first, columns)],
            (((1,), (1,)), ((), ())),
            preferred_element_type=F32,
        )
        values.append(product[:MOST] + product[MOST:])
    return jnp.concatenate(values, axis=0), squares


def own_half_kernel(rows_ref, gain_ref, shrink_ref, values_ref, squares_ref):
    columns = rows_ref.shape[1]
    values, squares = partial_values(
        rows_ref[...], gain_ref, shrink_ref, lax.axis_index("dp"), columns, shrink_ref.shape[0]
    )
    values_ref[...] = values
    squares_ref[...] = jnp.broadcast_to(squares, squares_ref.shape)


def own_half(rows, gain, shrink):
    slots = rows.shape[0]
    rank = shrink.shape[1]
    return pl.pallas_call(
        own_half_kernel,
        out_shape=(
            jax.ShapeDtypeStruct((slots, rank), F32),
            jax.ShapeDtypeStruct((slots, rank), F32),
        ),
        in_specs=[whole()] * 3,
        out_specs=(whole(),) * 2,
        compiler_params=pltpu.CompilerParams(vmem_limit_bytes=8 * MIB),
        cost_estimate=pl.CostEstimate(
            flops=2 * slots * rows.shape[1] * rank, bytes_accessed=2 * MIB, transcendentals=0
        ),
        name="own_half",
    )(rows, gain, shrink)


def finish_kernel(values_ref, squares_ref, gain_ref, shrink_ref, *refs):
    arrived, out_ref = refs[:-1], refs[-1]
    dp = 1 + len(arrived)
    me = lax.axis_index("dp")
    local = shrink_ref.shape[0]
    columns = arrived[0].shape[1]
    values, squares = values_ref[...], squares_ref[:, :1]
    for shift, piece in enumerate(arrived, start=1):
        more, more_squares = partial_values(
            piece[...].astype(F32),
            gain_ref,
            shrink_ref,
            lax.rem(me + dp - shift, dp),
            columns,
            local,
        )
        values, squares = values + more, squares + more_squares
    result = 2.0 * values * lax.rsqrt(squares / (columns * dp) + EPS)
    for adapter in range(local):
        out_ref[adapter, 0] = result[adapter * MOST : (adapter + 1) * MOST]


def finish(values, squares, gain, shrink, arrived):
    local, rank, _ = shrink.shape
    return pl.pallas_call(
        finish_kernel,
        out_shape=jax.ShapeDtypeStruct((local, 1, MOST, rank), F32),
        in_specs=[whole()] * (4 + len(arrived)),
        out_specs=whole(),
        compiler_params=pltpu.CompilerParams(vmem_limit_bytes=8 * MIB),
        name="finish",
    )(values, squares, gain, shrink, *arrived)


def shifted(array, axis, shift):
    count = lax.axis_size(axis)
    return lax.ppermute(array, axis, [(i, (i + shift) % count) for i in range(count)])


def across(array, receivers):
    sections = lax.axis_size("section")
    pairs = [
        (i * sections + s, j * sections + (s + 1) % sections)
        for i, j in enumerate(receivers)
        for s in range(sections)
    ]
    return lax.ppermute(array, ("tensor", "section"), pairs)


def body(hidden, down_matrix, residual, next_norm_scale, shrink_matrix, adapter_index):
    dp, tensors, sections = (lax.axis_size(axis) for axis in ("dp", "tensor", "section"))
    depth, _ = down_matrix.shape
    local = shrink_matrix.shape[0]

    others = jnp.stack([shifted(hidden, "dp", shift) for shift in range(1, dp)])

    step = step_of(depth)
    blocks = depth // step
    held_count = max(1, min(blocks // 2, HELD_BYTES // (2 * step * down_matrix.shape[1])))
    held = fetch(down_matrix, held_count * step)

    shrink = jnp.swapaxes(shrink_matrix, 1, 2)
    gain = next_norm_scale[None, :]

    in_vmem = [pltpu.with_memory_space_constraint(x, pltpu.VMEM) for x in (hidden, others, held)]
    total, sent = project(*in_vmem, down_matrix, tensors, sections)
    index, total = lax.optimization_barrier((adapter_index.reshape(1, -1), total))
    kept = keep(total, tensors, sections)
    places, shrink = prepare(index, shrink, local * MOST, dp)
    arrived = [shifted(sent[s - 1], "section", s) for s in range(1, sections)]
    plan = exchange_plan(tensors)
    own, *sums = pair(kept, arrived, plan, tensors)
    arrived = [across(x, receivers) for x, receivers in zip(sums, plan)]
    mixed, routed, leaving = mix(residual, places, own, arrived, local * MOST, dp)
    arrived = [shifted(leaving[s - 1], "dp", s) for s in range(1, dp)]
    values, squares = own_half(routed, gain, shrink)
    shrunk = finish(values, squares, gain, shrink, arrived)
    return (mixed, shrunk)


def solution(mesh):
    placed = (
        P(("groups", "dp"), ("tensor", "section")),
        P(("tensor", "section"), "dp"),
        P(("groups", "tensor", "section"), "dp"),
        P(),
        P("dp", None, None),
        P(("groups", "tensor", "section"), None),
    )
    return jax.shard_map(
        body,
        mesh=mesh,
        in_specs=placed,
        out_specs=(
            P(("groups", "tensor", "section"), "dp"),
            P("dp", ("groups", "tensor", "section"), None, None),
        ),
        check_vma=False,
    )
```
